32 devices in a mesh: wide: 8 (over y, x, core), narrow: 4 (over z).
Axes of the slice: x: 2, y: 2, z: 4, core: 2. Of those that a mesh axis runs over, the one named last changes fastest.
Arguments:
- tokens: bfloat16 [8192, 1152], P(('wide', 'narrow')), may hold values from -6 to 6
- cotangent: bfloat16 [8192, 1152], P(('wide', 'narrow')), may hold values from -6 to 6
- segment_ids: int32 [8192], P('wide'), may hold values from 0 to 31, as said below
- patch_pos: int32 [8192], P('wide'), may hold values from 0 to 255, as said below
- time_index: int32 [32], P('wide'), may hold values from 0 to 999
- time_table: bfloat16 [1000, 1152], replicated, may hold values from -6 to 6
- norm_gain: float32 [2, 2, 1152], replicated, may hold values from 0.5 to 1.5
- norm_shift: float32 [2, 2, 1152], replicated, may hold values from -2 to 2
- attn_weight: bfloat16 [2, 6, 1152, 1152], P(None, None, 'wide', 'narrow'), may hold values from -0.1875 to 0.1875
- out_weight: bfloat16 [2, 1152, 1152], P(None, 'wide', 'narrow'), may hold values from -0.75 to 0.75
- qkv_bias: float32 [2, 2, 1152], P(None, None, 'narrow'), may hold values from -2 to 2
- out_bias: float32 [2, 2, 1152], replicated, may hold values from -2 to 2
- mlp_weight: bfloat16 [2, 2, 1152, 4608], P(None, None, 'wide', 'narrow'), may hold values from -0.1875 to 0.1875
- up_bias: float32 [2, 4608], P(None, 'narrow'), may hold values from -2 to 2
- rel_table: float32 [2, 16, 961], P(None, 'narrow'), may hold values from -5 to 5
Outputs:
- block_output: bfloat16 [8192, 1152], P(('wide', 'narrow'))
- input_grad: bfloat16 [8192, 1152], P(('wide', 'narrow'))
- time_grad: float32 [1000, 1152], replicated
- gain_grad: float32 [2, 2, 1152], replicated
- shift_grad: float32 [2, 2, 1152], replicated
- attn_weight_grad: float32 [2, 6, 1152, 1152], P(None, None, 'wide', 'narrow')
- out_weight_grad: float32 [2, 1152, 1152], P(None, 'wide', 'narrow')
- qkv_bias_grad: float32 [2, 2, 1152], P(None, None, 'narrow')
- out_bias_grad: float32 [2, 2, 1152], replicated
- mlp_weight_grad: float32 [2, 2, 1152, 4608], P(None, None, 'wide', 'narrow')
- up_bias_grad: float32 [2, 4608], P(None, 'narrow')
- rel_table_grad: float32 [2, 16, 961], P(None, 'narrow')
The draws below stay inside these ranges and needn't reach their ends.
Inputs may be any that keep to these rules, and one draw needn't show every extreme that they name: `segment_ids`: image i has exactly 256 rows, all in the aligned block of 1024 rows numbered i // 4, in no particular order. `patch_pos`: within each image every position of the 16 x 16 patch grid occurs once; position p lies in grid row p // 16 and column p % 16.
All inputs are finite; a program needn't handle non-finite values.
Results may differ from the reference program's by a relative error of at most 0.024.
Values may be sent and summed in bfloat16 or wider, within the bound.
A program may use at most 320 MiB of HBM per device.

```python
import jax
import jax.numpy as jnp
from jax import lax

D = 1152
HEADS = 16
HEAD_DIM = 72
FF = 4608
GRID = 16
TSTEPS = 1000
LAYERS = 2
IMG_DEV = 4
PATCHES = 256
NREL = 961
TOK_DEV = 1024
IMAGES = 32
TOKENS = 8192


def patch_order(key):
    groups = TOKENS // TOK_DEV
    keys_all = jax.random.split(key, groups)
    orders = jax.vmap(lambda one_key: jax.random.permutation(one_key, TOK_DEV))(keys_all)
    return orders.astype(jnp.int32)


def draw_segment_ids(key, part):
    orders = patch_order(key)
    groups = TOKENS // TOK_DEV
    image_base = jnp.arange(groups, dtype=jnp.int32)[:, None] * IMG_DEV
    return (orders // PATCHES + image_base).reshape(TOKENS).astype(jnp.int32)


def draw_patch_pos(key, part):
    orders = patch_order(key)
    return (orders % PATCHES).reshape(TOKENS).astype(jnp.int32)


def plant(values, stream_key, low, largest):
    spot = [jax.random.randint(jax.random.fold_in(stream_key, axis), (), 0, length) for axis, length in enumerate(values.shape)]
    widest = values.shape.index(max(values.shape))
    next_to = spot[:widest] + [(spot[widest] + 1) % values.shape[widest]] + spot[widest + 1:]
    return values.at[tuple(spot)].set(low).at[tuple(next_to)].set(largest)


def steps_of(own_key, dims, cuts, least, top_value):
    def one(axis_at, parts):
        draws = jax.random.uniform(jax.random.fold_in(jax.random.fold_in(own_key, 6), axis_at), (parts,), jnp.float32, least / len(cuts), top_value / len(cuts))
        return jnp.repeat(jnp.exp(draws), dims[axis_at] // parts).reshape((-1,) + (1,) * (len(dims) - axis_at - 1))

    factor_of = one(*cuts[0])
    for cut in cuts[1:]:
        factor_of = factor_of * one(*cut)
    return factor_of


def gaussian(own_key, extent, width, reach, cuts=(), kind=jnp.bfloat16):
    values = width * jax.random.normal(own_key, extent, jnp.float32)
    if cuts:
        values = values * steps_of(own_key, extent, cuts, -0.22, 0.18)
    return jnp.clip(values, -reach, reach).astype(kind)


def setup_inputs(seed: int = 0) -> dict:
    arg_keys = jax.random.split(jax.random.key(seed), 16)
    tokens = gaussian(arg_keys[0], (TOKENS, D), 1.0, 6.0, ((0, 32),))
    cotangent = gaussian(arg_keys[1], (TOKENS, D), 1.0, 6.0, ((0, 32),))
    segment_ids = draw_segment_ids(jax.random.fold_in(arg_keys[15], 71), 0)
    patch_pos = draw_patch_pos(jax.random.fold_in(arg_keys[15], 71), 0)
    time_index = plant(jax.random.randint(arg_keys[4], (IMAGES,), 0, TSTEPS), jax.random.fold_in(arg_keys[4], 1), 0, TSTEPS - 1).astype(jnp.int32)
    time_table = gaussian(arg_keys[5], (TSTEPS, D), 1.0, 6.0)
    norm_gain = jnp.clip(1.0 + 0.1 * jax.random.normal(arg_keys[6], (LAYERS, 2, D), jnp.float32), 0.5, 1.5)
    norm_shift = gaussian(arg_keys[7], (LAYERS, 2, D), 0.3, 2.0, (), jnp.float32)
    attn_weight = gaussian(arg_keys[8], (LAYERS, 6, D, D), D ** -0.5, 0.1875, ((2, 8), (3, 4)))
    out_weight = gaussian(arg_keys[9], (LAYERS, D, D), (D // 16) ** -0.5, 0.75, ((1, 8), (2, 4)))
    qkv_bias = gaussian(arg_keys[10], (LAYERS, 2, D), 0.3, 2.0, ((2, 4),), jnp.float32)
    out_bias = gaussian(arg_keys[11], (LAYERS, 2, D), 0.3, 2.0, (), jnp.float32)
    mlp_weight = gaussian(arg_keys[12], (LAYERS, 2, D, FF), D ** -0.5, 0.1875, ((2, 8), (3, 4)))
    up_bias = gaussian(arg_keys[13], (LAYERS, FF), 0.3, 2.0, ((1, 4),), jnp.float32)
    rel_table = gaussian(arg_keys[14], (LAYERS, HEADS, NREL), 1.0, 5.0, ((1, 4),), jnp.float32)
    return dict(tokens=tokens, cotangent=cotangent, segment_ids=segment_ids, patch_pos=patch_pos, time_index=time_index, time_table=time_table, norm_gain=norm_gain, norm_shift=norm_shift, attn_weight=attn_weight, out_weight=out_weight, qkv_bias=qkv_bias, out_bias=out_bias, mlp_weight=mlp_weight, up_bias=up_bias, rel_table=rel_table)


highest = lax.Precision.HIGHEST
eps_norm = 1e-06
masked_score = -1e+30

@jax.custom_vjp
def low(v):
    return lax.optimization_barrier(v.astype(jnp.bfloat16)).astype(jnp.float32)

@jax.custom_vjp
def low_back(v):
    return v

def low_keep(v):
    return (low(v), None)

def low_pass(kept, grad):
    return (grad,)

def back_keep(v):
    return (v, None)

def back_low(kept, grad):
    return (low(grad),)
low.defvjp(low_keep, low_pass)
low_back.defvjp(back_keep, back_low)

def layer_norm(values, norm_gain, norm_shift):
    average = lax.optimization_barrier(jnp.mean(values, axis=-1, keepdims=True))
    centred = values - average
    variance = lax.optimization_barrier(jnp.mean(centred * centred, axis=-1, keepdims=True))
    return centred * lax.rsqrt(variance + eps_norm) * norm_gain + norm_shift

def relative_offsets(query_pos, key_pos):
    row_gap = query_pos[:, None] // GRID - key_pos[None, :] // GRID + (GRID - 1)
    col_gap = query_pos[:, None] % GRID - key_pos[None, :] % GRID + (GRID - 1)
    return (row_gap * (2 * GRID - 1) + col_gap).astype(jnp.int32)

def layer_forward(residual, params, layer_at, time_rows, image_local, segments, positions):
    time_table, norm_gain, norm_shift, attn_weight, out_weight, qkv_bias, out_bias, mlp_weight, up_bias, rel_table = params
    row_count = residual.shape[0]
    normed = low(layer_norm(residual, norm_gain[layer_at, 0], norm_shift[layer_at, 0]))
    spatial = jnp.einsum('rd,jdc->jrc', normed, attn_weight[layer_at, 0:3], precision=highest)
    time_part = low_back(jnp.einsum('id,jdc->jic', time_rows, attn_weight[layer_at, 3:6], precision=highest))
    time_spread = time_part[:, image_local]
    queries = spatial[0] + time_spread[0] + qkv_bias[layer_at, 0]
    key_rows = spatial[1] + time_spread[1]
    value_rows = spatial[2] + time_spread[2] + qkv_bias[layer_at, 1]
    queries = low(low_back(queries)).reshape(row_count, HEADS, HEAD_DIM)
    key_rows = low(low_back(key_rows)).reshape(row_count, HEADS, HEAD_DIM)
    value_rows = low(low_back(value_rows)).reshape(row_count, HEADS, HEAD_DIM)
    offsets = relative_offsets(positions, positions)
    scores = jnp.einsum('qhd,khd->hqk', queries, key_rows, precision=highest) * HEAD_DIM ** (-0.5)
    scores = low_back(scores + rel_table[layer_at][:, offsets])
    same_image = (segments[:, None] == segments[None, :])[None]
    scores = jnp.where(same_image, scores, masked_score)
    attention = low(jax.nn.softmax(scores, axis=-1))
    mixed_heads = jnp.einsum('hqk,khd->qhd', attention, value_rows, precision=highest).reshape(row_count, D)
    mixed_heads = low(low_back(mixed_heads))
    branch = low_back(jnp.dot(mixed_heads, out_weight[layer_at].T, precision=highest) + out_bias[layer_at, 0])
    middle = residual + branch
    normed_mid = low(layer_norm(middle, norm_gain[layer_at, 1], norm_shift[layer_at, 1]))
    hidden = low_back(jnp.dot(normed_mid, mlp_weight[layer_at, 0], precision=highest) + up_bias[layer_at])
    activated = low(jax.nn.gelu(hidden, approximate=True))
    branch_mlp = low_back(jnp.dot(activated, mlp_weight[layer_at, 1].T, precision=highest) + out_bias[layer_at, 1])
    return middle + branch_mlp

def group_forward(params, rows_in, segments, positions, time_steps):
    time_rows = params[0][time_steps]
    image_local = segments % IMG_DEV
    residual = rows_in
    for layer_at in range(LAYERS):
        residual = layer_forward(residual, params, layer_at, time_rows, image_local, segments, positions)
    return residual

def reference(tokens, cotangent, segment_ids, patch_pos, time_index, time_table, norm_gain, norm_shift, attn_weight, out_weight, qkv_bias, out_bias, mlp_weight, up_bias, rel_table):
    groups = TOKENS // TOK_DEV
    params = (time_table.astype(jnp.float32), norm_gain, norm_shift, attn_weight.astype(jnp.float32), out_weight.astype(jnp.float32), qkv_bias, out_bias, mlp_weight.astype(jnp.float32), up_bias, rel_table)
    segments = segment_ids.reshape(groups, TOK_DEV)
    positions = patch_pos.reshape(groups, TOK_DEV)
    time_steps = time_index.reshape(groups, IMG_DEV)
    checked = jax.checkpoint(group_forward)

    def forward(rows_all, params_all):

        def one_group(group_items):
            return checked(params_all, group_items[0], group_items[1], group_items[2], group_items[3])
        return lax.map(one_group, (rows_all, segments, positions, time_steps))
    rows_all = tokens.astype(jnp.float32).reshape(groups, TOK_DEV, D)
    result, backward = jax.vjp(forward, rows_all, params)
    row_grad, param_grad = backward(cotangent.astype(jnp.float32).reshape(groups, TOK_DEV, D))
    return (result.reshape(TOKENS, D).astype(jnp.bfloat16), row_grad.reshape(TOKENS, D).astype(jnp.bfloat16), param_grad[0], param_grad[1], param_grad[2], param_grad[3], param_grad[4], param_grad[5], param_grad[6], param_grad[7], param_grad[8], param_grad[9])
```

```python
import functools

import jax
import jax.numpy as jnp
from jax import lax
from jax.experimental import pallas as pl
from jax.experimental.pallas import tpu as pltpu
from jax.sharding import PartitionSpec as P

HEAD_DIM = 72
GRID = 16
PATCHES = GRID * GRID
SPAN = 2 * GRID - 1


eps_norm = 1e-06
highest = lax.Precision.HIGHEST
f32 = jnp.float32
bf16 = jnp.bfloat16
ROWS_AXES = ("narrow", "wide")
MESH = pl.DeviceIdType.MESH


class Place:
    def __init__(self):
        wide = lax.axis_index("wide")
        self.z = lax.axis_index("narrow")
        self.y, self.x, self.c = wide // 4, (wide // 2) % 2, wide % 2

    def wide(self, flip_y=0, flip_x=0, flip_c=0):
        y = 1 - self.y if flip_y else self.y
        x = 1 - self.x if flip_x else self.x
        c = 1 - self.c if flip_c else self.c
        return y * 4 + x * 2 + c

    def along_z(self, steps):
        return lax.rem(self.z + steps, 4)

    def peers(self):
        across = [(self.wide(1, 0, 0), self.z), (self.wide(0, 1, 0), self.z), (self.wide(0, 0, 1), self.z)]
        return across + [(self.wide(), self.along_z(k)) for k in (1, 2, 3)]

    def greet(self):
        barrier = pltpu.get_barrier_semaphore()
        for peer in self.peers():
            pl.semaphore_signal(barrier, inc=1, device_id=peer, device_id_type=MESH)
        pl.semaphore_wait(barrier, 6)


def unit_cut(unit, rows):
    low = rows // 32 * 16
    return low if unit % 2 == 0 else rows - low


GATHER_SEMS = 3 + 24 + 28


class GatherUnit:
    def __init__(self, place, piece, whole, send, recv, cut):
        self.place, self.piece, self.whole = place, piece, whole
        self.send, self.recv = send, recv
        rows = piece.shape[0]
        self.halves = (pl.ds(0, cut), pl.ds(cut, rows - cut))
        self.whole_rows = pl.ds(0, rows)
        self.copies = {}

    def put(self, slot, peer, src, dst):
        copy = pltpu.make_async_remote_copy(
            src_ref=src, dst_ref=dst, send_sem=self.send.at[slot], recv_sem=self.recv.at[slot],
            device_id=peer, device_id_type=MESH,
        )
        copy.start()
        self.copies[slot] = copy

    def block(self, back, flip_y, flip_x, rows, flip_c=0):
        p = self.place
        return self.whole.at[p.along_z(4 - back), p.wide(flip_y, flip_x, flip_c), rows]

    def forward(self, slot, peer, back, flip_y, flip_x, rows):
        block = self.block(back, flip_y, flip_x, rows)
        self.put(slot, peer, block, block)

    def begin(self):
        p = self.place
        own = self.block(0, 0, 0, self.whole_rows)
        self.local = pltpu.make_async_copy(self.piece, own, self.send.at[GATHER_SEMS])
        self.local.start()
        for k in (1, 2, 3):
            self.put(k - 1, (p.wide(), p.along_z(k)), self.piece, own)
        for slot, peer, rows in ((3, (p.wide(1, 0), p.z), self.halves[0]), (15, (p.wide(0, 1), p.z), self.halves[1])):
            self.put(slot, peer, self.piece.at[rows], own.at[rows])
        self.put(27, (p.wide(0, 0, 1), p.z), self.piece, own)

    def second(self):
        p = self.place
        first, last = self.halves
        for k in (1, 2, 3):
            self.copies[k - 1].wait_recv()
            self.forward(3 + k, (p.wide(1, 0), p.z), k, 0, 0, first)
            self.forward(15 + k, (p.wide(0, 1), p.z), k, 0, 0, last)
            self.forward(27 + k, (p.wide(0, 0, 1), p.z), k, 0, 0, self.whole_rows)

    def third(self):
        p = self.place
        first, last = self.halves
        self.local.wait()
        for k in range(4):
            self.forward(7 + k, (p.wide(0, 1), p.z), k, 0, 0, first)
            self.forward(19 + k, (p.wide(1, 0), p.z), k, 0, 0, last)
        for k in range(4):
            self.copies[3 + k].wait_recv()
            self.forward(11 + k, (p.wide(0, 1), p.z), k, 1, 0, first)
            self.forward(31 + k, (p.wide(0, 0, 1), p.z), k, 1, 0, first)
            self.copies[15 + k].wait_recv()
            self.forward(23 + k, (p.wide(1, 0), p.z), k, 0, 1, last)
            self.forward(35 + k, (p.wide(0, 0, 1), p.z), k, 0, 1, last)

    def fourth(self):
        p = self.place
        first, last = self.halves
        core = (p.wide(0, 0, 1), p.z)
        for k in range(4):
            self.copies[7 + k].wait_recv()
            self.forward(39 + k, core, k, 0, 1, first)
            self.copies[19 + k].wait_recv()
            self.forward(43 + k, core, k, 1, 0, last)
        for k in range(4):
            self.copies[11 + k].wait_recv()
            self.forward(47 + k, core, k, 1, 1, first)
            self.copies[23 + k].wait_recv()
            self.forward(51 + k, core, k, 1, 1, last)

    def finish(self):
        for slot in range(27, 55):
            self.copies[slot].wait_recv()
        for slot in range(55):
            self.copies[slot].wait_send()


def gather_kernel(count, *refs):
    pieces, wholes = refs[:count], refs[count : 2 * count]
    send, recv = refs[2 * count :]
    place = Place()
    place.greet()
    units = [
        GatherUnit(place, pieces[u], wholes[u], send.at[u], recv.at[u], unit_cut(u, pieces[u].shape[0]))
        for u in range(count)
    ]
    for u in range(count + 3):
        if u < count:
            units[u].begin()
        if 0 <= u - 1 < count:
            units[u - 1].second()
            units[u - 1].third()
        if 0 <= u - 2 < count:
            units[u - 2].fourth()
        if 0 <= u - 3 < count:
            units[u - 3].finish()


def gather_units(pieces, collective_id):
    count = len(pieces)
    rows, cols = pieces[0].shape
    wholes = pl.pallas_call(
        functools.partial(gather_kernel, count),
        out_shape=[jax.ShapeDtypeStruct((4, 8, rows, cols), bf16)] * count,
        in_specs=[pl.BlockSpec(memory_space=pl.ANY)] * count,
        out_specs=[pl.BlockSpec(memory_space=pl.ANY)] * count,
        scratch_shapes=[pltpu.SemaphoreType.DMA((count, GATHER_SEMS + 1)), pltpu.SemaphoreType.DMA((count, GATHER_SEMS))],
        compiler_params=pltpu.CompilerParams(collective_id=collective_id, has_side_effects=True),
        name="gather_units",
    )(*pieces)
    return [w.reshape(4, 8 * rows, cols) for w in wholes]


SCATTER_SEMS = 4 * 5 + 3


def add_rows(total, part, rows):
    step = 16

    def one(at, carry):
        here = pl.ds(pl.multiple_of(at * step, step), step)
        both = total[here, :].astype(f32) + part[here, :].astype(f32)
        total[here, :] = both.astype(total.dtype)
        return carry

    lax.fori_loop(0, rows // step, one, 0)


class ScatterUnit:
    ORDER = (2, 1, 3, 0)

    def __init__(self, place, grads, out, total, from_core, far, near, from_z, send, recv, load, cut):
        self.place, self.grads, self.out = place, grads, out
        self.total, self.from_core, self.far, self.near, self.from_z = total, from_core, far, near, from_z
        self.send, self.recv, self.load = send, recv, load
        rows = grads.shape[4]
        self.rows, self.cut = rows, cut
        self.first, self.last = pl.ds(0, cut), pl.ds(cut, rows - cut)
        self.copies, self.loads = {}, {}

    def put(self, slot, peer, src, dst):
        copy = pltpu.make_async_remote_copy(
            src_ref=src, dst_ref=dst, send_sem=self.send.at[slot], recv_sem=self.recv.at[slot],
            device_id=peer, device_id_type=MESH,
        )
        copy.start()
        self.copies[slot] = copy

    def begin(self):
        p = self.place
        for k in self.ORDER:
            z = p.along_z(k)
            self.put(k, (p.wide(0, 0, 1), p.z), self.grads.at[z, :, :, 1 - p.c], self.from_core.at[k])
            self.loads[k] = pltpu.make_async_copy(self.grads.at[z, :, :, p.c], self.total.at[k], self.load.at[k])
            self.loads[k].start()

    def first_stage(self, k):
        p = self.place
        self.loads[k].wait()
        self.copies[k].wait_recv()
        for block in range(4):
            add_rows(self.total.at[k, block // 2, block % 2], self.from_core.at[k, block // 2, block % 2], self.rows)
        self.put(4 + k, (p.wide(0, 1), p.z), self.total.at[k, :, 1 - p.x, self.first], self.far.at[k, :, self.first])
        self.put(8 + k, (p.wide(1, 0), p.z), self.total.at[k, 1 - p.y, :, self.last], self.far.at[k, :, self.last])

    def second_stage(self, k):
        p = self.place
        self.copies[4 + k].wait_recv()
        for block in range(2):
            add_rows(self.total.at[k, block, p.x, self.first], self.far.at[k, block, self.first], self.cut)
        self.put(12 + k, (p.wide(1, 0), p.z), self.total.at[k, 1 - p.y, p.x, self.first], self.near.at[k, self.first])
        self.copies[8 + k].wait_recv()
        for block in range(2):
            add_rows(self.total.at[k, p.y, block, self.last], self.far.at[k, block, self.last], self.rows - self.cut)
        self.put(16 + k, (p.wide(0, 1), p.z), self.total.at[k, p.y, 1 - p.x, self.last], self.near.at[k, self.last])

    def third_stage(self, k):
        p = self.place
        self.copies[12 + k].wait_recv()
        self.copies[16 + k].wait_recv()
        add_rows(self.total.at[k, p.y, p.x], self.near.at[k], self.rows)
        if k:
            self.put(19 + k, (p.wide(), p.along_z(k)), self.total.at[k, p.y, p.x], self.from_z.at[k - 1])

    def finish(self):
        p = self.place
        for k in (1, 2, 3):
            self.copies[19 + k].wait_recv()
        own = self.total.at[0, p.y, p.x]
        step = 16

        def one(at, carry):
            here = pl.ds(pl.multiple_of(at * step, step), step)
            both = own[here, :].astype(f32)
            for k in range(3):
                both = both + self.from_z[k, here, :].astype(f32)
            self.out[here, :] = both
            return carry

        lax.fori_loop(0, self.rows // step, one, 0)
        for slot in self.copies:
            self.copies[slot].wait_send()


def scatter_scratch(count, rows, cols, cut):
    one = [
        pltpu.VMEM((4, 2, 2, rows, cols), bf16),
        pltpu.VMEM((4, 2, 2, rows, cols), bf16),
        pltpu.VMEM((4, 2, rows, cols), bf16),
        pltpu.VMEM((4, rows, cols), bf16),
        pltpu.VMEM((3, rows, cols), bf16),
    ]
    return one * count + [
        pltpu.SemaphoreType.DMA((count, SCATTER_SEMS)),
        pltpu.SemaphoreType.DMA((count, SCATTER_SEMS)),
        pltpu.SemaphoreType.DMA((count, 4)),
    ]


def scatter_kernel(count, *refs):
    grads, outs = refs[:count], refs[count : 2 * count]
    scratch = refs[2 * count : 7 * count]
    send, recv, load = refs[7 * count :]
    place = Place()
    place.greet()
    units = [
        ScatterUnit(place, grads[u], outs[u], *scratch[5 * u : 5 * u + 5], send.at[u], recv.at[u], load.at[u],
                    unit_cut(u, grads[u].shape[4]))
        for u in range(count)
    ]
    steps = [(u, k) for u in range(count) for k in ScatterUnit.ORDER]
    for u in range(count):
        units[u].begin()
    for at in range(len(steps) + 4):
        if at < len(steps):
            u, k = steps[at]
            units[u].first_stage(k)
        if 0 <= at - 1 < len(steps):
            u, k = steps[at - 1]
            units[u].second_stage(k)
        if 0 <= at - 2 < len(steps):
            u, k = steps[at - 2]
            units[u].third_stage(k)
        if 0 <= at - 4 < len(steps) and steps[at - 4][1] == 0:
            units[steps[at - 4][0]].finish()


def scatter_units(grads, collective_id):
    count = len(grads)
    cols = grads[0].shape[-1]
    rows = grads[0].shape[1] // 8
    return pl.pallas_call(
        functools.partial(scatter_kernel, count),
        out_shape=[jax.ShapeDtypeStruct((rows, cols), f32)] * count,
        in_specs=[pl.BlockSpec(memory_space=pl.ANY)] * count,
        out_specs=[pl.BlockSpec(memory_space=pltpu.VMEM)] * count,
        scratch_shapes=scatter_scratch(count, rows, cols, 0),
        compiler_params=pltpu.CompilerParams(
            collective_id=collective_id, has_side_effects=True, vmem_limit_bytes=62 * 2**20
        ),
        name="scatter_units",
    )(*[g.reshape(4, 2, 2, 2, rows, cols) for g in grads])


def by_links(rows):
    return lax.axis_size("wide") == 8 and lax.axis_size("narrow") == 4 and rows % 16 == 0


def gather_all(pieces):
    if by_links(pieces[0].shape[0]):
        return gather_units(pieces, 0)
    return [gather_unit(piece) for piece in pieces]


def scatter_all(grads):
    if by_links(grads[0].shape[1] // lax.axis_size("wide")):
        return scatter_units([item.astype(bf16) for item in grads], 1)
    return [scatter_unit(item).astype(f32) for item in grads]


def layer_norm(values, norm_gain, norm_shift):
    average = jnp.mean(values, axis=-1, keepdims=True)
    centred = values - average
    variance = jnp.mean(centred * centred, axis=-1, keepdims=True)
    scale = lax.rsqrt(variance + eps_norm)
    unit = centred * scale
    return unit * norm_gain + norm_shift, unit, scale


def layer_norm_back(grad, unit, scale, norm_gain):
    weighted = grad * norm_gain
    first = jnp.mean(weighted, axis=-1, keepdims=True)
    second = jnp.mean(weighted * unit, axis=-1, keepdims=True)
    from_norm = scale * (weighted - first - unit * second)
    return from_norm, jnp.sum(grad * unit, axis=0), jnp.sum(grad, axis=0)


def offset_onehot():
    near = jnp.arange(GRID, dtype=jnp.int32)
    span = jnp.arange(SPAN, dtype=jnp.int32)
    return (span[None, None, :] == near[:, None, None] - near[None, :, None] + (GRID - 1)).astype(f32)


def pair_bias(bias_table):
    steps_hot = offset_onehot()
    head_count = bias_table.shape[0]
    table_grid = bias_table.reshape(head_count, SPAN, SPAN)
    row_part = jnp.einsum("ixa,hab->hixb", steps_hot, table_grid, precision=highest)
    pairs = jnp.einsum("jyb,hixb->hijxy", steps_hot, row_part, precision=highest)
    return pairs.reshape(head_count, PATCHES, PATCHES)


def fold_bias_grad(pair_grad):
    steps_hot = offset_onehot()
    head_count = pair_grad.shape[0]
    grid_grad = pair_grad.reshape(head_count, GRID, GRID, GRID, GRID)
    col_part = jnp.einsum("jyb,hijxy->hixb", steps_hot, grid_grad, precision=highest)
    table_grad = jnp.einsum("ixa,hixb->hab", steps_hot, col_part, precision=highest)
    return table_grad.reshape(head_count, SPAN * SPAN)


def gather_unit(piece):
    parts = lax.axis_size("narrow")
    whole = lax.all_gather(piece, ROWS_AXES, axis=0, tiled=True)
    return whole.reshape(parts, whole.shape[0] // parts, whole.shape[1])


def scatter_unit(grads):
    flat = grads.astype(bf16).reshape(-1, grads.shape[-1])
    return lax.psum_scatter(flat, ROWS_AXES, scatter_dimension=0, tiled=True)


def to_heads(values):
    parts, rows, cols = values.shape
    split = values.reshape(parts, rows, cols // HEAD_DIM, HEAD_DIM)
    return split.transpose(0, 2, 1, 3).reshape(-1, rows, HEAD_DIM)


def from_heads(values, parts):
    heads, rows, _ = values.shape
    split = values.reshape(parts, heads // parts, rows, HEAD_DIM).transpose(0, 2, 1, 3)
    return split.reshape(parts, rows, -1)


def attention_forward(residual, proj, time_part, params, pairs):
    norm_gain, norm_shift, qkv_bias, out_bias = params
    parts = proj.shape[0]
    cols = proj.shape[2] // 4
    normed, unit, scale = layer_norm(residual, norm_gain[0], norm_shift[0])
    normed_low = normed.astype(bf16)
    spatial = jnp.einsum("rd,zdc->zrc", normed_low, proj[:, :, : 3 * cols], preferred_element_type=f32)
    offsets = time_part + jnp.stack([qkv_bias[0], jnp.zeros_like(qkv_bias[0]), qkv_bias[1]])
    offsets = offsets.reshape(3, parts, 1, cols)
    queries, key_rows, value_rows = (
        to_heads((spatial[:, :, j * cols : (j + 1) * cols] + offsets[j]).astype(bf16)) for j in range(3)
    )
    scores = jnp.einsum("hqd,hkd->hqk", queries, key_rows, preferred_element_type=f32)
    scores = scores * HEAD_DIM ** (-0.5) + pairs
    attention = jax.nn.softmax(scores, axis=-1)
    attention_low = attention.astype(bf16)
    mixed = jnp.einsum("hqk,hkd->hqd", attention_low, value_rows, preferred_element_type=f32)
    mixed_low = from_heads(mixed.astype(bf16), parts)
    branch = jnp.einsum("zrc,zdc->rd", mixed_low, proj[:, :, 3 * cols :], preferred_element_type=f32)
    middle = residual + (branch + out_bias[0])
    saved = (normed_low, unit, scale, queries, key_rows, value_rows, attention, mixed_low)
    return middle, saved


def mlp_forward(middle, up, down, params, up_bias):
    norm_gain, norm_shift, qkv_bias, out_bias = params
    parts = up.shape[0]
    normed, unit, scale = layer_norm(middle, norm_gain[1], norm_shift[1])
    normed_low = normed.astype(bf16)
    hidden = jnp.einsum("rd,zdc->zrc", normed_low, up, preferred_element_type=f32)
    hidden = hidden + up_bias.reshape(parts, 1, -1)
    activated = jax.nn.gelu(hidden, approximate=True).astype(bf16)
    branch = jnp.einsum("zrc,zdc->rd", activated, down, preferred_element_type=f32)
    return middle + (branch + out_bias[1]), (normed_low, unit, scale, hidden, activated)


def mlp_backward(gradient, up, down, params, saved):
    norm_gain = params[0]
    normed_low, unit, scale, hidden, activated = saved
    grad_low = gradient.astype(bf16)
    out_bias_grad = jnp.sum(grad_low.astype(f32), axis=0)
    down_grad = jnp.einsum("rd,zrc->zdc", grad_low, activated, preferred_element_type=f32)
    act_grad = jnp.einsum("rd,zdc->zrc", grad_low, down, preferred_element_type=f32)
    _, gelu_back = jax.vjp(lambda values: jax.nn.gelu(values, approximate=True), hidden)
    hidden_low = gelu_back(act_grad)[0].astype(bf16)
    up_bias_grad = jnp.sum(hidden_low.astype(f32), axis=1).reshape(-1)
    up_grad = jnp.einsum("rd,zrc->zdc", normed_low, hidden_low, preferred_element_type=f32)
    normed_grad = jnp.einsum("zrc,zdc->rd", hidden_low, up, preferred_element_type=f32)
    from_norm, gain_grad, shift_grad = layer_norm_back(normed_grad, unit, scale, norm_gain[1])
    return gradient + from_norm, up_grad, down_grad, (gain_grad, shift_grad, out_bias_grad, up_bias_grad)


def attention_backward(grad_mid, proj, params, saved):
    norm_gain = params[0]
    normed_low, unit, scale, queries, key_rows, value_rows, attention, mixed_low = saved
    parts = proj.shape[0]
    cols = proj.shape[2] // 4
    score_scale = HEAD_DIM ** (-0.5)
    mid_low = grad_mid.astype(bf16)
    out_bias_grad = jnp.sum(mid_low.astype(f32), axis=0)
    out_grad = jnp.einsum("rd,zrc->zdc", mid_low, mixed_low, preferred_element_type=f32)
    mixed_grad = jnp.einsum("rd,zdc->zrc", mid_low, proj[:, :, 3 * cols :], preferred_element_type=f32)
    mixed_grad = to_heads(mixed_grad.astype(bf16))
    dot_back = jnp.einsum("hqd,hkd->hqk", mixed_grad, value_rows, preferred_element_type=f32)
    score_grad = attention * (dot_back - jnp.sum(attention * dot_back, axis=-1, keepdims=True))
    score_low = score_grad.astype(bf16)
    table_grad = fold_bias_grad(score_low.astype(f32))
    query_grad = jnp.einsum("hqk,hkd->hqd", score_low, key_rows, preferred_element_type=f32) * score_scale
    key_grad = jnp.einsum("hqk,hqd->hkd", score_low, queries, preferred_element_type=f32) * score_scale
    value_grad = jnp.einsum("hqk,hqd->hkd", attention.astype(bf16), mixed_grad, preferred_element_type=f32)
    qkv_low = jnp.concatenate(
        [from_heads(item.astype(bf16), parts) for item in (query_grad, key_grad, value_grad)], axis=-1
    )
    spatial_grad = jnp.einsum("rd,zrc->zdc", normed_low, qkv_low, preferred_element_type=f32)
    proj_grad = jnp.concatenate([spatial_grad, out_grad], axis=-1)
    sums = jnp.sum(qkv_low.astype(f32), axis=1).reshape(parts, 3, cols).transpose(1, 0, 2).reshape(3, -1)
    normed_grad = jnp.einsum("zrc,zdc->rd", qkv_low, proj[:, :, : 3 * cols], preferred_element_type=f32)
    from_norm, gain_grad, shift_grad = layer_norm_back(normed_grad, unit, scale, norm_gain[0])
    return grad_mid + from_norm, proj_grad, sums, table_grad, (gain_grad, shift_grad, out_bias_grad)


def shards(
    tokens,
    cotangent,
    segment_ids,
    patch_pos,
    time_index,
    time_table,
    norm_gain,
    norm_shift,
    attn_weight,
    out_weight,
    qkv_bias,
    out_bias,
    mlp_weight,
    up_bias,
    rel_table,
):
    image_count = time_index.shape[0]
    layer_count = attn_weight.shape[0]
    narrow_at = lax.axis_index("narrow")
    wide_at = lax.axis_index("wide")
    wide_size = lax.axis_size("wide")
    own_rows = tokens.shape[0]
    in_rows, cols = attn_weight.shape[2:]
    image_local = segment_ids % image_count
    grid_slot = image_local * PATCHES + patch_pos
    own_slots = narrow_at * own_rows + jnp.arange(own_rows, dtype=jnp.int32)
    pick_in = (own_slots[:, None] == grid_slot[None, :]).astype(bf16)
    own_grid = lax.dynamic_slice_in_dim(grid_slot, narrow_at * own_rows, own_rows)
    pick_out = (own_grid[:, None] == jnp.arange(grid_slot.shape[0], dtype=jnp.int32)[None, :]).astype(bf16)

    def to_images(rows):
        every = lax.all_gather(rows, "narrow", axis=0, tiled=True)
        return jnp.dot(pick_in, every, preferred_element_type=f32)

    def to_rows(rows):
        every = lax.all_gather(rows, "narrow", axis=0, tiled=True)
        return jnp.dot(pick_out, every, preferred_element_type=f32).astype(bf16)

    steps_all = lax.all_gather(time_index, "wide", axis=0, tiled=True)
    step_hot = (steps_all[:, None] == jnp.arange(time_table.shape[0], dtype=jnp.int32)[None, :]).astype(bf16)
    time_rows = jnp.dot(step_hot, time_table, preferred_element_type=f32).astype(bf16)
    time_slice = lax.dynamic_slice_in_dim(time_rows, wide_at * in_rows, in_rows, axis=1)
    time_weight = attn_weight[:, 3:6]
    time_share = jnp.einsum("id,ljdc->ljic", time_slice, time_weight, preferred_element_type=f32)
    time_share = lax.psum_scatter(time_share, "wide", scatter_dimension=2, tiled=True)
    time_share = lax.all_gather(time_share, "narrow", axis=3, tiled=True)
    time_part = lax.dynamic_index_in_dim(time_share, narrow_at, axis=2, keepdims=False)

    tables = lax.all_gather(rel_table, "narrow", axis=1, tiled=True)
    qkv_bias_all = lax.all_gather(qkv_bias, "narrow", axis=2, tiled=True)
    up_bias_all = lax.all_gather(up_bias, "narrow", axis=1, tiled=True)

    def layer_params(at):
        return (norm_gain[at], norm_shift[at], qkv_bias_all[at], out_bias[at])

    weights = []
    for at in range(layer_count):
        packed = jnp.concatenate([attn_weight[at, 0], attn_weight[at, 1], attn_weight[at, 2], out_weight[at]], axis=1)
        weights += [packed, mlp_weight[at, 0], mlp_weight[at, 1]]
    weights = gather_all(weights)
    weights = [weights[3 * at : 3 * at + 3] for at in range(layer_count)]

    residual = to_images(tokens)
    kept = []
    for at in range(layer_count):
        pairs = pair_bias(tables[at])
        middle, attn_saved = attention_forward(residual, weights[at][0], time_part[at], layer_params(at), pairs)
        residual, mlp_saved = mlp_forward(middle, weights[at][1], weights[at][2], layer_params(at), up_bias_all[at])
        kept.append((attn_saved, mlp_saved))
    block_output = to_rows(residual.astype(bf16))
    gradient = to_images(cotangent)
    attn_grads, out_grads, mlp_grads = [], [], []
    time_sums, small = [], []
    for at in reversed(range(layer_count)):
        attn_saved, mlp_saved = kept[at]
        grad_mid, up_grad, down_grad, mlp_small = mlp_backward(
            gradient, weights[at][1], weights[at][2], layer_params(at), mlp_saved
        )
        gradient, proj_grad, sums, table_grad, attn_small = attention_backward(
            grad_mid, weights[at][0], layer_params(at), attn_saved
        )
        down_part, up_part, packed = scatter_all([down_grad, up_grad, proj_grad])
        mlp_grads.insert(0, jnp.stack([up_part, down_part]))
        attn_grads.insert(0, jnp.stack([packed[:, j * cols : (j + 1) * cols] for j in range(3)]))
        out_grads.insert(0, packed[:, 3 * cols :])
        time_sums.insert(0, sums)
        small.insert(
            0,
            (
                jnp.stack([attn_small[0], mlp_small[0]]),
                jnp.stack([attn_small[1], mlp_small[1]]),
                jnp.stack([attn_small[2], mlp_small[2]]),
                jnp.stack([sums[0], sums[2]]),
                mlp_small[3],
                table_grad,
            ),
        )
    input_grad = to_rows(gradient.astype(bf16))

    def stacked(index_at):
        return jnp.stack([entry[index_at] for entry in small])

    totals = lax.psum(tuple(stacked(index_at) for index_at in range(6)), ("wide", "narrow"))

    def own_part(array, axis):
        size = array.shape[axis] // lax.axis_size("narrow")
        return lax.dynamic_slice_in_dim(array, narrow_at * size, size, axis=axis)

    time_low = jnp.stack(time_sums).astype(bf16)
    time_all = lax.all_gather(time_low, ("wide", "narrow"), axis=0, tiled=False)
    time_own = own_part(time_all, 3)
    time_weight_grad = jnp.einsum("id,iljc->ljdc", time_slice, time_own, preferred_element_type=f32)
    trow_share = jnp.einsum("iljc,ljdc->id", time_own, time_weight, preferred_element_type=f32)
    trow_share = lax.psum(trow_share, "narrow")
    trow = lax.all_gather(trow_share, "wide", axis=1, tiled=True)
    time_grad = jnp.einsum("is,id->sd", step_hot.astype(f32), trow, precision=highest)
    attn_grad = jnp.concatenate([jnp.stack(attn_grads).astype(f32), time_weight_grad], axis=1)
    return (
        block_output,
        input_grad,
        time_grad,
        totals[0],
        totals[1],
        attn_grad,
        jnp.stack(out_grads).astype(f32),
        own_part(totals[3], 2),
        totals[2],
        jnp.stack(mlp_grads).astype(f32),
        own_part(totals[4], 1),
        own_part(totals[5], 1),
    )


def solution(mesh):
    return jax.shard_map(
        shards,
        mesh=mesh,
        in_specs=(
            P(("wide", "narrow"), None),
            P(("wide", "narrow"), None),
            P("wide"),
            P("wide"),
            P("wide"),
            P(),
            P(),
            P(),
            P(None, None, "wide", "narrow"),
            P(None, "wide", "narrow"),
            P(None, None, "narrow"),
            P(),
            P(None, None, "wide", "narrow"),
            P(None, "narrow"),
            P(None, "narrow", None),
        ),
        out_specs=(
            P(("wide", "narrow"), None),
            P(("wide", "narrow"), None),
            P(),
            P(),
            P(),
            P(None, None, "wide", "narrow"),
            P(None, "wide", "narrow"),
            P(None, None, "narrow"),
            P(),
            P(None, None, "wide", "narrow"),
            P(None, "narrow"),
            P(None, "narrow", None),
        ),
        check_vma=False,
    )
```

```python
import functools
import math

import jax
import jax.numpy as jnp
from jax import lax
from jax.experimental import pallas as pl
from jax.experimental.pallas import tpu as pltpu
from jax.sharding import PartitionSpec as P

HEAD_DIM = 72
GRID = 16
PATCHES = GRID * GRID
SPAN = 2 * GRID - 1


eps_norm = 1e-06
highest = lax.Precision.HIGHEST
f32 = jnp.float32
bf16 = jnp.bfloat16
ROWS_AXES = ("narrow", "wide")
MESH = pl.DeviceIdType.MESH


def layer_norm(values, norm_gain, norm_shift):
    average = jnp.mean(values, axis=-1, keepdims=True)
    centred = values - average
    variance = jnp.mean(centred * centred, axis=-1, keepdims=True)
    scale = lax.rsqrt(variance + eps_norm)
    unit = centred * scale
    return unit * norm_gain + norm_shift, unit, scale


def layer_norm_back(grad, unit, scale, norm_gain):
    weighted = grad * norm_gain
    first = jnp.mean(weighted, axis=-1, keepdims=True)
    second = jnp.mean(weighted * unit, axis=-1, keepdims=True)
    from_norm = scale * (weighted - first - unit * second)
    return from_norm, jnp.sum(grad * unit, axis=0), jnp.sum(grad, axis=0)


def offset_onehot():
    near = jnp.arange(GRID, dtype=jnp.int32)
    span = jnp.arange(SPAN, dtype=jnp.int32)
    return (span[None, None, :] == near[:, None, None] - near[None, :, None] + (GRID - 1)).astype(f32)


def pair_bias(bias_table):
    steps_hot = offset_onehot()
    head_count = bias_table.shape[0]
    table_grid = bias_table.reshape(head_count, SPAN, SPAN)
    row_part = jnp.einsum("ixa,hab->hixb", steps_hot, table_grid, precision=highest)
    pairs = jnp.einsum("jyb,hixb->hijxy", steps_hot, row_part, precision=highest)
    return pairs.reshape(head_count, PATCHES, PATCHES)


def fold_bias_grad(pair_grad):
    steps_hot = offset_onehot()
    head_count = pair_grad.shape[0]
    grid_grad = pair_grad.reshape(head_count, GRID, GRID, GRID, GRID)
    col_part = jnp.einsum("jyb,hijxy->hixb", steps_hot, grid_grad, precision=highest)
    table_grad = jnp.einsum("ixa,hixb->hab", steps_hot, col_part, precision=highest)
    return table_grad.reshape(head_count, SPAN * SPAN)


def gather_unit(piece):
    parts = lax.axis_size("narrow")
    whole = lax.all_gather(piece, ROWS_AXES, axis=0, tiled=True)
    return whole.reshape(parts, whole.shape[0] // parts, whole.shape[1])


def scatter_unit(grads):
    flat = grads.astype(bf16).reshape(-1, grads.shape[-1])
    return lax.psum_scatter(flat, ROWS_AXES, scatter_dimension=0, tiled=True)


def to_heads(values):
    parts, rows, cols = values.shape
    split = values.reshape(parts, rows, cols // HEAD_DIM, HEAD_DIM)
    return split.transpose(0, 2, 1, 3).reshape(-1, rows, HEAD_DIM)


def from_heads(values, parts):
    heads, rows, _ = values.shape
    split = values.reshape(parts, heads // parts, rows, HEAD_DIM).transpose(0, 2, 1, 3)
    return split.reshape(parts, rows, -1)


def attention_forward(residual, proj, time_part, params, pairs):
    norm_gain, norm_shift, qkv_bias, out_bias = params
    parts = proj.shape[0]
    cols = proj.shape[2] // 4
    normed, unit, scale = layer_norm(residual, norm_gain[0], norm_shift[0])
    normed_low = normed.astype(bf16)
    spatial = jnp.einsum("rd,zdc->zrc", normed_low, proj[:, :, : 3 * cols], preferred_element_type=f32)
    offsets = time_part + jnp.stack([qkv_bias[0], jnp.zeros_like(qkv_bias[0]), qkv_bias[1]])
    offsets = offsets.reshape(3, parts, 1, cols)
    queries, key_rows, value_rows = (
        to_heads((spatial[:, :, j * cols : (j + 1) * cols] + offsets[j]).astype(bf16)) for j in range(3)
    )
    scores = jnp.einsum("hqd,hkd->hqk", queries, key_rows, preferred_element_type=f32)
    scores = scores * HEAD_DIM ** (-0.5) + pairs
    attention = jax.nn.softmax(scores, axis=-1)
    attention_low = attention.astype(bf16)
    mixed = jnp.einsum("hqk,hkd->hqd", attention_low, value_rows, preferred_element_type=f32)
    mixed_low = from_heads(mixed.astype(bf16), parts)
    branch = jnp.einsum("zrc,zdc->rd", mixed_low, proj[:, :, 3 * cols :], preferred_element_type=f32)
    middle = residual + (branch + out_bias[0])
    saved = (normed_low, unit, scale, queries, key_rows, value_rows, attention, mixed_low)
    return middle, saved


def mlp_forward(middle, up, down, params, up_bias):
    norm_gain, norm_shift, qkv_bias, out_bias = params
    parts = up.shape[0]
    normed, unit, scale = layer_norm(middle, norm_gain[1], norm_shift[1])
    normed_low = normed.astype(bf16)
    hidden = jnp.einsum("rd,zdc->zrc", normed_low, up, preferred_element_type=f32)
    hidden = hidden + up_bias.reshape(parts, 1, -1)
    activated = jax.nn.gelu(hidden, approximate=True).astype(bf16)
    branch = jnp.einsum("zrc,zdc->rd", activated, down, preferred_element_type=f32)
    return middle + (branch + out_bias[1]), (normed_low, unit, scale, hidden, activated)


def mlp_backward(gradient, up, down, params, saved):
    norm_gain = params[0]
    normed_low, unit, scale, hidden, activated = saved
    grad_low = gradient.astype(bf16)
    out_bias_grad = jnp.sum(grad_low.astype(f32), axis=0)
    down_grad = jnp.einsum("rd,zrc->zdc", grad_low, activated, preferred_element_type=f32)
    act_grad = jnp.einsum("rd,zdc->zrc", grad_low, down, preferred_element_type=f32)
    _, gelu_back = jax.vjp(lambda values: jax.nn.gelu(values, approximate=True), hidden)
    hidden_low = gelu_back(act_grad)[0].astype(bf16)
    up_bias_grad = jnp.sum(hidden_low.astype(f32), axis=1).reshape(-1)
    up_grad = jnp.einsum("rd,zrc->zdc", normed_low, hidden_low, preferred_element_type=f32)
    normed_grad = jnp.einsum("zrc,zdc->rd", hidden_low, up, preferred_element_type=f32)
    from_norm, gain_grad, shift_grad = layer_norm_back(normed_grad, unit, scale, norm_gain[1])
    return gradient + from_norm, up_grad, down_grad, (gain_grad, shift_grad, out_bias_grad, up_bias_grad)


def attention_backward(grad_mid, proj, params, saved):
    norm_gain = params[0]
    normed_low, unit, scale, queries, key_rows, value_rows, attention, mixed_low = saved
    parts = proj.shape[0]
    cols = proj.shape[2] // 4
    score_scale = HEAD_DIM ** (-0.5)
    mid_low = grad_mid.astype(bf16)
    out_bias_grad = jnp.sum(mid_low.astype(f32), axis=0)
    out_grad = jnp.einsum("rd,zrc->zdc", mid_low, mixed_low, preferred_element_type=f32)
    mixed_grad = jnp.einsum("rd,zdc->zrc", mid_low, proj[:, :, 3 * cols :], preferred_element_type=f32)
    mixed_grad = to_heads(mixed_grad.astype(bf16))
    dot_back = jnp.einsum("hqd,hkd->hqk", mixed_grad, value_rows, preferred_element_type=f32)
    score_grad = attention * (dot_back - jnp.sum(attention * dot_back, axis=-1, keepdims=True))
    score_low = score_grad.astype(bf16)
    table_grad = fold_bias_grad(score_low.astype(f32))
    query_grad = jnp.einsum("hqk,hkd->hqd", score_low, key_rows, preferred_element_type=f32) * score_scale
    key_grad = jnp.einsum("hqk,hqd->hkd", score_low, queries, preferred_element_type=f32) * score_scale
    value_grad = jnp.einsum("hqk,hqd->hkd", attention.astype(bf16), mixed_grad, preferred_element_type=f32)
    qkv_low = jnp.concatenate(
        [from_heads(item.astype(bf16), parts) for item in (query_grad, key_grad, value_grad)], axis=-1
    )
    spatial_grad = jnp.einsum("rd,zrc->zdc", normed_low, qkv_low, preferred_element_type=f32)
    proj_grad = jnp.concatenate([spatial_grad, out_grad], axis=-1)
    sums = jnp.sum(qkv_low.astype(f32), axis=1).reshape(parts, 3, cols).transpose(1, 0, 2).reshape(3, -1)
    normed_grad = jnp.einsum("zrc,zdc->rd", qkv_low, proj[:, :, : 3 * cols], preferred_element_type=f32)
    from_norm, gain_grad, shift_grad = layer_norm_back(normed_grad, unit, scale, norm_gain[0])
    return grad_mid + from_norm, proj_grad, sums, table_grad, (gain_grad, shift_grad, out_bias_grad)


class Place:
    def __init__(self):
        wide = lax.axis_index("wide")
        self.z = lax.axis_index("narrow")
        self.y, self.x, self.c = wide // 4, (wide // 2) % 2, wide % 2

    def wide(self, flip_y=0, flip_x=0, flip_c=0):
        y = 1 - self.y if flip_y else self.y
        x = 1 - self.x if flip_x else self.x
        c = 1 - self.c if flip_c else self.c
        return y * 4 + x * 2 + c

    def along_z(self, steps):
        return lax.rem(self.z + steps, 4)

    def peers(self):
        across = [(self.wide(1, 0, 0), self.z), (self.wide(0, 1, 0), self.z), (self.wide(0, 0, 1), self.z)]
        return across + [(self.wide(), self.along_z(k)) for k in (1, 2, 3)]

    def greet(self):
        barrier = pltpu.get_barrier_semaphore()
        for peer in self.peers():
            pl.semaphore_signal(barrier, inc=1, device_id=peer, device_id_type=MESH)
        pl.semaphore_wait(barrier, 6)


def unit_cut(unit, rows):
    low = rows // 32 * 16
    return low if unit % 2 == 0 else rows - low


class Line:
    def __init__(self, place, block, send, recv):
        self.place, self.block, self.send, self.recv = place, block, send, recv

    def copy(self, src, origin, step, slot):
        place = self.place
        return pltpu.make_async_remote_copy(
            src_ref=src, dst_ref=self.block(origin), send_sem=self.send.at[slot], recv_sem=self.recv.at[origin],
            device_id=(place.wide(), place.z + step), device_id_type=MESH,
        )

    def begin(self, own):
        z = self.place.z

        @pl.when(z < 3)
        def _():
            self.copy(own, z, 1, z).start()

        @pl.when(z > 0)
        def _():
            self.copy(own, z, -1, 4).start()

    def arrive(self, far, then=lambda origin: None):
        z = self.place.z
        for side, valid, room in ((-1, z - far >= 0, z < 3), (1, z + far <= 3, z > 0)):

            @pl.when(valid)
            def _(side=side, room=room):
                origin = z + side * far
                here = self.block(origin)
                self.copy(here, origin, -side, origin).wait_recv()

                @pl.when(room)
                def _():
                    self.copy(here, origin, -side, origin).start()

                then(origin)

    def finish(self):
        z = self.place.z
        for origin in range(4):
            sent = jnp.where(origin <= z, z < 3, z > 0)

            @pl.when(sent)
            def _(origin=origin):
                self.copy(self.block(origin), origin, 0, origin).wait_send()

        @pl.when(z > 0)
        def _():
            self.copy(self.block(0), 0, 0, 4).wait_send()


LINE_SEMS = 5
GATHER_SEMS = 58
Y_FIRST, X_LAST, X_NEAR, X_FAR, Y_NEAR, Y_FAR = 5, 9, 13, 17, 21, 25
C_OWN, C_Y, C_X, C_X_NEAR, C_Y_NEAR, C_X_FAR, C_Y_FAR = 29, 33, 37, 41, 45, 49, 53


class GatherUnit:
    def __init__(self, place, piece, whole, send, recv, cut):
        self.place, self.piece, self.whole = place, piece, whole
        self.send, self.recv = send, recv
        self.rows = piece.shape[0]
        self.first, self.last, self.every = pl.ds(0, cut), pl.ds(cut, self.rows - cut), pl.ds(0, self.rows)
        self.line = Line(place, lambda origin: self.block(origin, 0, 0, self.every), send, recv)
        self.peer = {
            "y": (place.wide(1, 0, 0), place.z), "x": (place.wide(0, 1, 0), place.z), "c": (place.wide(0, 0, 1), place.z)
        }
        self.order = [place.along_z(k) for k in (0, 1, 3, 2)]
        self.sent = []

    def block(self, origin, flip_y, flip_x, rows):
        first = pl.multiple_of(self.place.wide(flip_y, flip_x) * self.rows + rows.start, 16)
        return self.whole.at[origin, pl.ds(first, rows.size)]

    def copy(self, base, axis, origin, flip_y, flip_x, rows, own=None):
        block = self.block(origin, flip_y, flip_x, rows)
        return pltpu.make_async_remote_copy(
            src_ref=block if own is None else own, dst_ref=block, send_sem=self.send.at[base + origin],
            recv_sem=self.recv.at[base + origin], device_id=self.peer[axis], device_id_type=MESH,
        )

    def put(self, *where):
        self.copy(*where).start()

    def wait(self, *where):
        self.copy(*where).wait_recv()

    def begin(self):
        z = self.place.z
        self.line.begin(self.piece)
        self.put(Y_FIRST, "y", z, 0, 0, self.first, self.piece.at[self.first])
        self.put(X_LAST, "x", z, 0, 0, self.last, self.piece.at[self.last])
        self.put(C_OWN, "c", z, 0, 0, self.every, self.piece)
        self.local = pltpu.make_async_copy(self.piece, self.block(z, 0, 0, self.every), self.send.at[GATHER_SEMS - 1])
        self.local.start()

    def second(self):
        def then(origin):
            self.put(Y_FIRST, "y", origin, 0, 0, self.first)
            self.put(X_LAST, "x", origin, 0, 0, self.last)
            self.put(C_OWN, "c", origin, 0, 0, self.every)

        for far in (1, 2, 3):
            self.line.arrive(far, then)
            yield

    def third(self):
        self.local.wait()
        for origin in self.order:
            self.put(X_NEAR, "x", origin, 0, 0, self.first)
            self.put(Y_NEAR, "y", origin, 0, 0, self.last)
        for at, origin in enumerate(self.order):
            self.wait(Y_FIRST, "y", origin, 1, 0, self.first)
            self.put(X_FAR, "x", origin, 1, 0, self.first)
            self.put(C_Y, "c", origin, 1, 0, self.first)
            self.wait(X_LAST, "x", origin, 0, 1, self.last)
            self.put(Y_FAR, "y", origin, 0, 1, self.last)
            self.put(C_X, "c", origin, 0, 1, self.last)
            if at % 2:
                yield

    def fourth(self):
        for at, origin in enumerate(self.order):
            self.wait(X_NEAR, "x", origin, 0, 1, self.first)
            self.put(C_X_NEAR, "c", origin, 0, 1, self.first)
            self.wait(Y_NEAR, "y", origin, 1, 0, self.last)
            self.put(C_Y_NEAR, "c", origin, 1, 0, self.last)
            if at % 2:
                yield
        for at, origin in enumerate(self.order):
            self.wait(X_FAR, "x", origin, 1, 1, self.first)
            self.put(C_X_FAR, "c", origin, 1, 1, self.first)
            self.wait(Y_FAR, "y", origin, 1, 1, self.last)
            self.put(C_Y_FAR, "c", origin, 1, 1, self.last)
            if at % 2:
                yield

    def finish(self):
        firsts = (Y_FIRST, X_NEAR, X_FAR, C_Y, C_X_NEAR, C_X_FAR)
        lasts = (X_LAST, Y_NEAR, Y_FAR, C_X, C_Y_NEAR, C_Y_FAR)
        for origin in range(4):
            for base in (C_Y, C_X_NEAR, C_X_FAR):
                self.wait(base, "c", origin, 0, 0, self.first)
            for base in (C_X, C_Y_NEAR, C_Y_FAR):
                self.wait(base, "c", origin, 0, 0, self.last)
            self.wait(C_OWN, "c", origin, 0, 0, self.every)
        for origin in range(4):
            for base in firsts:
                self.copy(base, "c", origin, 0, 0, self.first).wait_send()
            for base in lasts:
                self.copy(base, "c", origin, 0, 0, self.last).wait_send()
            self.copy(C_OWN, "c", origin, 0, 0, self.every).wait_send()
        self.line.finish()


def column_ids(width):
    return lax.broadcasted_iota(jnp.int32, (1, width), 1)


def unit_rows(values):
    average = jnp.mean(values, axis=-1, keepdims=True)
    centred = values - average
    variance = jnp.mean(centred * centred, axis=-1, keepdims=True)
    scale = lax.rsqrt(variance + eps_norm)
    return centred * scale, scale


def dot_plain(left, right):
    return lax.dot_general(left, right, (((1,), (0,)), ((), ())), preferred_element_type=f32)


def dot_turned(left, right):
    return lax.dot_general(left, right, (((1,), (1,)), ((), ())), preferred_element_type=f32)


def remote(src, dst, send, recv, peer):
    copy = pltpu.make_async_remote_copy(
        src_ref=src, dst_ref=dst, send_sem=send, recv_sem=recv, device_id=peer, device_id_type=MESH
    )
    copy.start()
    return copy


def z_line(place, every, send, recv):
    return Line(place, lambda origin: every.at[origin], send, recv)


class Stream:
    def __init__(self, slots, sems, sources):
        self.slots, self.sems, self.sources = slots, sems, sources
        self.started = 0

    def ensure(self, upto):
        while self.started <= upto and self.started < len(self.sources):
            at = self.started
            pltpu.make_async_copy(self.sources[at], self.slots.at[at % 2], self.sems.at[at % 2]).start()
            self.started += 1

    def take(self, at):
        self.ensure(at)
        pltpu.make_async_copy(self.sources[at], self.slots.at[at % 2], self.sems.at[at % 2]).wait()
        return self.slots.at[at % 2]


FORWARD_IN = 17
LAYER_SAVED = 6


def gelu(values):
    inner = math.sqrt(2.0 / math.pi) * (values + 0.044715 * values * values * values)
    return 0.5 * values * (1.0 + jnp.tanh(inner))


def window_bias(windows, put):
    for grid_row in range(GRID):
        shift = (GRID - 1 - grid_row) * GRID
        moved = windows if shift == 0 else pltpu.roll(windows, 512 - shift, 1)
        put(grid_row, moved[:, :PATCHES])


def forward_kernel(layers, *refs):
    units = 3 * layers
    refs = list(refs)

    def take(count):
        out = refs[:count]
        del refs[:count]
        return out

    (tokens, cot, pick, time_own, time_weight, windows_own, small_own, gains, shifts, out_bias) = take(10)
    pieces = take(units)
    wholes = take(units)
    saved = [take(LAYER_SAVED) for _ in range(layers)]
    block_out, grad_out, time_out, time_sel_out = take(4)
    (
        send, recv, z_send, z_recv, t_send, t_recv, save_sem, w_sem,
        w_slots, tok_all, cot_all, windows_all, small_all, time_all, share, share_y, share_x, share_c, share_z,
        x_buf, mid_buf, low_buf, acc_buf, s_buf, att_buf, act_buf, hid_buf, bias_buf,
    ) = refs
    place = Place()
    place.greet()
    gather = [
        GatherUnit(place, pieces[u], wholes[u], send.at[u], recv.at[u], unit_cut(u, pieces[u].shape[0]))
        for u in range(units)
    ]
    state = {"done": 0}
    tokens_n, d_model = tokens.shape
    head_cols = d_model // 4
    yp, xp, cp = ((place.wide(1, 0, 0), place.z), (place.wide(0, 1, 0), place.z), (place.wide(0, 0, 1), place.z))
    py, px, pc = place.y, place.x, place.c

    def comm_steps():
        gather[0].begin()
        time_all[py, px, pc] = time_own[...]
        first = remote(time_all.at[py, px, pc], time_all.at[py, px, pc], t_send.at[0], t_recv.at[0], cp)
        tok, win, small, cots, rz = (
            z_line(place, every, z_send.at[at], z_recv.at[at])
            for at, every in enumerate((tok_all, windows_all, small_all, cot_all, share_z))
        )
        small.begin(small_own)
        tok.begin(tokens)
        win.begin(windows_own)
        own = [
            pltpu.make_async_copy(tokens, tok_all.at[place.z], save_sem.at[0]),
            pltpu.make_async_copy(windows_own, windows_all.at[place.z], save_sem.at[1]),
            pltpu.make_async_copy(small_own, small_all.at[place.z], save_sem.at[2]),
            pltpu.make_async_copy(cot, cot_all.at[place.z], save_sem.at[3]),
        ]
        for copy in own:
            copy.start()
        gather[1].begin()
        first.wait_recv()
        second = remote(time_all.at[py, px], time_all.at[py, px], t_send.at[1], t_recv.at[1], xp)
        yield from gather[0].second()
        small.arrive(1)
        tok.arrive(1)
        win.arrive(1)
        second.wait_recv()
        third = remote(time_all.at[py], time_all.at[py], t_send.at[2], t_recv.at[2], yp)
        yield from gather[0].third()
        third.wait_recv()
        rows = time_all[...].reshape(128, d_model)
        cut = time_weight.shape[1]
        at_row = lax.broadcasted_iota(jnp.int32, (d_model, cut), 0)
        at_col = lax.broadcasted_iota(jnp.int32, (d_model, cut), 1)
        select = (at_row == at_col + place.wide() * cut).astype(bf16)
        picked = dot_plain(rows, select).astype(bf16)
        time_sel_out[...] = picked
        time_out[...] = rows
        for layer in range(layers):
            part = dot_plain(picked, time_weight[layer]).reshape(2, 2, 2, 16, d_model)
            share[:, :, :, layer] = part[:, :, :, :8]
        ry = remote(share.at[1 - py], share_y, t_send.at[3], t_recv.at[3], yp)
        gather[2].begin()
        small.arrive(2)
        tok.arrive(2)
        win.arrive(2)
        ry.wait_recv()
        share[py] = share[py] + share_y[...]
        rx = remote(share.at[py, 1 - px], share_x, t_send.at[4], t_recv.at[4], xp)
        yield from gather[1].second()
        rx.wait_recv()
        share[py, px] = share[py, px] + share_x[...]
        rc = remote(share.at[py, px, 1 - pc], share_c, t_send.at[5], t_recv.at[5], cp)
        rc.wait_recv()
        share[py, px, pc] = share[py, px, pc] + share_c[...]
        share_z[place.z] = share[py, px, pc]
        rz.begin(share_z.at[place.z])
        yield from gather[0].fourth()
        rz.arrive(1)
        yield from gather[1].third()
        rz.arrive(2)
        gather[0].finish()
        for line in (small, tok, win, rz):
            line.arrive(3)
            line.finish()
        for copy in own:
            copy.wait()
        state["done"] = 1
        for copy in (first, second, third, ry, rx, rc):
            copy.wait_send()
        yield
        for unit in range(3, units + 3):
            if unit < units:
                gather[unit].begin()
                yield
            if unit - 1 < units:
                yield from gather[unit - 1].second()
                yield from gather[unit - 1].third()
            if unit - 2 < units:
                yield from gather[unit - 2].fourth()
                gather[unit - 2].finish()
                state["done"] = unit - 1
                yield
            if unit == 3:
                cots.begin(cot)
            elif unit <= 6:
                cots.arrive(unit - 3)
            if unit == 6:
                cots.finish()

    stream = Stream(w_slots, w_sem, [wholes[u].at[z] for u in range(units) for z in range(4)])
    pending = {}

    def save(slot, src, dst):
        copy = pltpu.make_async_copy(src, dst, save_sem.at[slot])
        copy.start()
        pending[slot] = copy

    def settle(slot):
        if slot in pending:
            pending.pop(slot).wait()

    def weights(unit, z):
        at = unit * 4 + z
        stream.ensure(at)
        ready = state["done"] * 4
        stream.ensure(min(at + 1, ready - 1))
        return stream.take(at)

    def compute_steps():
        columns = column_ids(d_model)
        for layer in range(layers):
            x_save, mid_save, s_save, att_save, hid_save, act_save = saved[layer]
            row = 2 * layer
            yield 3 * layer + 1
            if layer == 0:
                total = dot_plain(pick[:, 0:tokens_n], tok_all[0])
                for z in range(1, 4):
                    total = total + dot_plain(pick[:, z * tokens_n : (z + 1) * tokens_n], tok_all[z])
                x_buf[...] = total
            settle(4)
            settle(5)
            save(4, x_buf, x_save)
            unit, _ = unit_rows(x_buf[...])
            low_buf[...] = (unit * gains[row : row + 1, :] + shifts[row : row + 1, :]).astype(bf16)
            settle(6)
            for z in range(4):
                yield 3 * layer + 1
                w = weights(3 * layer, z)
                share_rows = share_z[z, layer]
                at_image = lax.broadcasted_iota(jnp.int32, share_rows.shape, 0) == place.z
                offset = jnp.sum(jnp.where(at_image, share_rows, 0.0), axis=0, keepdims=True)
                offset = offset + small_all[z, 2 + layer : 3 + layer, :]
                s_buf[z] = (dot_plain(low_buf[...], w[...]) + offset).astype(bf16)
                q = s_buf[z, :, 0:head_cols]
                k = s_buf[z, :, head_cols : 2 * head_cols]
                v = s_buf[z, :, 2 * head_cols : 3 * head_cols]
                head_of = column_ids(head_cols) // HEAD_DIM
                slot = z % 2
                settle(8 + slot)

                def one_head(head, mixed):
                    here = head_of == head

                    def put(grid_row, block):
                        bias_buf[grid_row * GRID : (grid_row + 1) * GRID, :] = block

                    first_row = pl.multiple_of(head * GRID, GRID)
                    window_bias(windows_all[z, layer, pl.ds(first_row, GRID), :], put)
                    scores = dot_turned(jnp.where(here, q, 0), k)
                    scores = scores * HEAD_DIM ** (-0.5) + bias_buf[...]
                    top = jnp.max(scores, axis=-1, keepdims=True)
                    exponent = jnp.exp(scores - top)
                    attention = exponent / jnp.sum(exponent, axis=-1, keepdims=True)
                    att_buf[slot, head] = attention
                    return mixed + dot_plain(attention.astype(bf16), jnp.where(here, v, 0))

                mixed = lax.fori_loop(0, 4, one_head, jnp.zeros((tokens_n, head_cols), f32))
                save(8 + slot, att_buf.at[slot], att_save.at[z])
                s_buf[z, :, 3 * head_cols :] = mixed.astype(bf16)
                branch = dot_turned(jnp.where(columns >= 3 * head_cols, s_buf[z], 0), w[...])
                acc_buf[...] = branch if z == 0 else acc_buf[...] + branch
            save(6, s_buf, s_save)
            settle(4)
            mid_buf[...] = x_buf[...] + (acc_buf[...] + out_bias[row : row + 1, :])
            save(5, mid_buf, mid_save)
            unit, _ = unit_rows(mid_buf[...])
            low_buf[...] = (unit * gains[row + 1 : row + 2, :] + shifts[row + 1 : row + 2, :]).astype(bf16)
            settle(7)
            for z in range(4):
                yield 3 * layer + 2
                w = weights(3 * layer + 1, z)
                slot = z % 2
                settle(10 + slot)
                hid_buf[slot] = dot_plain(low_buf[...], w[...]) + small_all[z, layer : layer + 1, :]
                save(10 + slot, hid_buf.at[slot], hid_save.at[z])
                act_buf[z] = gelu(hid_buf[slot]).astype(bf16)
            save(7, act_buf, act_save)
            for z in range(4):
                yield 3 * layer + 3
                w = weights(3 * layer + 2, z)
                branch = dot_turned(act_buf[z], w[...])
                acc_buf[...] = branch if z == 0 else acc_buf[...] + branch
            x_buf[...] = mid_buf[...] + (acc_buf[...] + out_bias[row + 1 : row + 2, :])
        block_out[...] = x_buf[...].astype(bf16)
        total = dot_plain(pick[:, 0:tokens_n], cot_all[0])
        for z in range(1, 4):
            total = total + dot_plain(pick[:, z * tokens_n : (z + 1) * tokens_n], cot_all[z])
        grad_out[...] = total
        for slot in list(pending):
            settle(slot)

    interleave(comm_steps(), compute_steps(), state)


def interleave(comm, compute, state, pace=1):
    need = next(compute)
    count = 0
    for _ in comm:
        count += 1
        if count % pace == 0 and need is not None and state["done"] >= need:
            need = next(compute, None)
    while need is not None:
        need = next(compute, None)


def forward_all(tokens, cot, pick, time_own, time_weight, windows_own, small_own, gains, shifts, out_bias, pieces):
    layers = len(pieces) // 3
    units = len(pieces)
    rows, d_model = tokens.shape
    piece_rows = pieces[0].shape[0]
    any_space = pl.BlockSpec(memory_space=pl.ANY)
    vmem = pl.BlockSpec(memory_space=pltpu.VMEM)
    layer_shapes = [
        ((rows, d_model), f32),
        ((rows, d_model), f32),
        ((4, rows, d_model), bf16),
        ((4, 4, rows, rows), f32),
        ((4, rows, d_model), f32),
        ((4, rows, d_model), bf16),
    ]
    out_shape = (
        [jax.ShapeDtypeStruct((4, 8 * piece_rows, d_model), bf16)] * units
        + [jax.ShapeDtypeStruct(*item) for item in layer_shapes] * layers
        + [
            jax.ShapeDtypeStruct((rows, d_model), bf16),
            jax.ShapeDtypeStruct((rows, d_model), f32),
            jax.ShapeDtypeStruct((128, d_model), bf16),
            jax.ShapeDtypeStruct((128, piece_rows), bf16),
        ]
    )
    share_tail = (layers, 8, d_model)
    scratch = [
        pltpu.SemaphoreType.DMA((units, GATHER_SEMS)),
        pltpu.SemaphoreType.DMA((units, GATHER_SEMS)),
        pltpu.SemaphoreType.DMA((5, LINE_SEMS)),
        pltpu.SemaphoreType.DMA((5, LINE_SEMS)),
        pltpu.SemaphoreType.DMA((6,)),
        pltpu.SemaphoreType.DMA((6,)),
        pltpu.SemaphoreType.DMA((12,)),
        pltpu.SemaphoreType.DMA((2,)),
        pltpu.VMEM((2, d_model, d_model), bf16),
        pltpu.VMEM((4, rows, d_model), bf16),
        pltpu.VMEM((4, rows, d_model), bf16),
        pltpu.VMEM((4,) + windows_own.shape, f32),
        pltpu.VMEM((4,) + small_own.shape, f32),
        pltpu.VMEM((2, 2, 2, 16, d_model), bf16),
        pltpu.VMEM((2, 2, 2) + share_tail, f32),
        pltpu.VMEM((2, 2) + share_tail, f32),
        pltpu.VMEM((2,) + share_tail, f32),
        pltpu.VMEM(share_tail, f32),
        pltpu.VMEM((4,) + share_tail, f32),
        pltpu.VMEM((rows, d_model), f32),
        pltpu.VMEM((rows, d_model), f32),
        pltpu.VMEM((rows, d_model), bf16),
        pltpu.VMEM((rows, d_model), f32),
        pltpu.VMEM((4, rows, d_model), bf16),
        pltpu.VMEM((2, 4, rows, rows), f32),
        pltpu.VMEM((4, rows, d_model), bf16),
        pltpu.VMEM((2, rows, d_model), f32),
        pltpu.VMEM((rows, rows), f32),
    ]
    out = pl.pallas_call(
        functools.partial(forward_kernel, layers),
        out_shape=out_shape,
        in_specs=[any_space] * 2 + [vmem] * 8 + [any_space] * units,
        out_specs=[any_space] * (units + LAYER_SAVED * layers) + [vmem] * 4,
        scratch_shapes=scratch,
        compiler_params=pltpu.CompilerParams(
            collective_id=0, has_side_effects=True, vmem_limit_bytes=60 * 2**20
        ),
        name="forward_all",
    )(tokens, cot, pick, time_own, time_weight, windows_own, small_own, gains, shifts, out_bias, *pieces)
    wholes = out[:units]
    saved = [out[units + LAYER_SAVED * at : units + LAYER_SAVED * (at + 1)] for at in range(layers)]
    return wholes, saved, out[units + LAYER_SAVED * layers :]


def gelu_slope(values):
    factor = math.sqrt(2.0 / math.pi)
    square = values * values
    bend = jnp.tanh(factor * (values + 0.044715 * square * values))
    return 0.5 * (1.0 + bend) + 0.5 * values * (1.0 - bend * bend) * factor * (1.0 + 3 * 0.044715 * square)


def dot_rows(left, right):
    return lax.dot_general(left, right, (((0,), (0,)), ((), ())), preferred_element_type=f32)


def norm_back(grad, unit, scale, norm_gain):
    weighted = grad * norm_gain
    first = jnp.mean(weighted, axis=-1, keepdims=True)
    second = jnp.mean(weighted * unit, axis=-1, keepdims=True)
    return scale * (weighted - first - unit * second)


def column_sums(values):
    return jnp.sum(values, axis=0, keepdims=True)


def fold_window(grads):
    total = None
    empty = jnp.zeros((GRID, 512 - PATCHES), f32)
    for grid_row in range(GRID):
        wide = jnp.concatenate([grads[grid_row * GRID : (grid_row + 1) * GRID, :], empty], axis=1)
        shift = (GRID - 1 - grid_row) * GRID
        moved = wide if shift == 0 else pltpu.roll(wide, shift, 1)
        total = moved if total is None else total + moved
    return total


SCATTER_SEMS = 23


def add_rows(total, part, rows):
    step = 16

    def one(at, carry):
        here = pl.ds(pl.multiple_of(at * step, step), step)
        both = total[here, :].astype(f32) + part[here, :].astype(f32)
        total[here, :] = both.astype(total.dtype)
        return carry

    lax.fori_loop(0, rows // step, one, 0)


class ScatterUnit:
    def __init__(self, place, out, total, far, near, from_z, send, recv, cut):
        self.place, self.out = place, out
        self.total, self.far, self.near, self.from_z = total, far, near, from_z
        self.send, self.recv = send, recv
        self.rows, self.cut = total.shape[3], cut
        self.first, self.last = pl.ds(0, cut), pl.ds(cut, self.rows - cut)
        self.copies, self.unsent, self.closed = {}, set(), set()

    def put(self, slot, peer, src, dst):
        self.copies[slot] = remote(src, dst, self.send.at[slot], self.recv.at[slot], peer)
        self.unsent.add(slot)

    def settle(self, slots):
        for slot in sorted(self.unsent.intersection(slots)):
            self.copies[slot].wait_send()
            self.unsent.remove(slot)

    def first_stage(self, k):
        p = self.place
        self.put(4 + k, (p.wide(0, 1), p.z), self.total.at[k, :, 1 - p.x, self.first], self.far.at[k, :, self.first])
        self.put(8 + k, (p.wide(1, 0), p.z), self.total.at[k, 1 - p.y, :, self.last], self.far.at[k, :, self.last])

    def second_stage(self, k):
        p = self.place
        self.copies[4 + k].wait_recv()
        for block in range(2):
            add_rows(self.total.at[k, block, p.x, self.first], self.far.at[k, block, self.first], self.cut)
        self.put(12 + k, (p.wide(1, 0), p.z), self.total.at[k, 1 - p.y, p.x, self.first], self.near.at[k, self.first])
        self.copies[8 + k].wait_recv()
        for block in range(2):
            add_rows(self.total.at[k, p.y, block, self.last], self.far.at[k, block, self.last], self.rows - self.cut)
        self.put(16 + k, (p.wide(0, 1), p.z), self.total.at[k, p.y, 1 - p.x, self.last], self.near.at[k, self.last])

    def third_stage(self, k):
        p = self.place
        self.copies[12 + k].wait_recv()
        self.copies[16 + k].wait_recv()
        add_rows(self.total.at[k, p.y, p.x], self.near.at[k], self.rows)
        if k:
            self.put(19 + k, (p.wide(), p.along_z(k)), self.total.at[k, p.y, p.x], self.from_z.at[k - 1])
            self.closed.add(k)

    def finish(self):
        p = self.place
        for k in (1, 2, 3):
            self.copies[19 + k].wait_recv()
        own = self.total.at[0, p.y, p.x]
        step = 16

        def one(at, carry):
            here = pl.ds(pl.multiple_of(at * step, step), step)
            both = own[here, :].astype(f32)
            for k in range(3):
                both = both + self.from_z[k, here, :].astype(f32)
            self.out[here, :] = both
            return carry

        lax.fori_loop(0, self.rows // step, one, 0)
        self.settle(list(self.copies))
        self.closed.add(0)


FAR_FIRST = (2, 1, 3, 0)


def scatter_step(unit, k, late):
    unit.second_stage(k)

    def third():
        unit.third_stage(k)
        if k == 0:
            return ((late, unit.finish),)

    return ((late, third),)


def backward_kernel(last_layer, *refs):
    refs = list(refs)

    def take(count):
        out = refs[:count]
        del refs[:count]
        return out

    (
        grad, x_in, mid_in, gains, shifts, pick, rows_in, s_all, att_all, hid_all, act_all, proj, up, down,
    ) = take(14)
    proj_out, up_out, down_out, grad_out, rows_out, small_out, table_out, rows_all = take(8)
    (
        total_a, total_b, far, near, from_z, right_a, right_b, left, turned,
        w_slots, s_slots, att_slots, hid_slots, acc_buf, mid_grad, low_buf, head_grads,
        send, recv, left_send, left_recv, line_send, line_recv, w_sem, s_sem, att_sem, hid_sem, load_sem, credit,
    ) = refs
    place = Place()
    place.greet()
    rows, d_model = grad.shape
    cut = down_out.shape[0]
    head_cols = d_model // 4
    core = (place.wide(0, 0, 1), place.z)
    zs = {k: place.along_z(k) for k in range(4)}
    columns = column_ids(d_model)
    units = {
        name: ScatterUnit(
            place, out, total, far.at[at], near.at[at], from_z.at[at], send.at[at], recv.at[at], unit_cut(at, cut)
        )
        for at, (name, out, total) in enumerate(
            (("down", down_out, total_a), ("up", up_out, total_b), ("proj", proj_out, total_a))
        )
    }
    line = z_line(place, rows_all, line_send, line_recv)

    right_copies = {}

    def give_right(name, at, k, src, buffer):
        right_copies[name, k] = remote(
            src, buffer.at[zs[k], pl.ds(rows, rows)], send.at[at, k], recv.at[at, k], core
        )

    left_copies = {}

    def make_left(at, values):
        if at > 1:
            for copy in left_copies[at - 2]:
                copy.wait_send()
        flipped = turned.at[at % 2]
        flipped[...] = values.astype(f32).T.astype(bf16)
        copies = []
        for block in range(4):
            mine = pl.multiple_of((2 * block + place.c) * cut, 16)
            other = pl.multiple_of((2 * block + 1 - place.c) * cut, 16)
            here = pl.ds(block * cut, cut)
            copies.append(
                remote(
                    flipped.at[pl.ds(other, cut)], left.at[at, here, pl.ds(rows, rows)],
                    left_send.at[at, block], left_recv.at[at, block], core,
                )
            )
            left[at, here, 0:rows] = flipped[pl.ds(mine, cut), :]
        left_copies[at] = copies

    def left_ready(at):
        for copy in left_copies[at]:
            copy.wait_recv()

    loads, keep = [], []
    if last_layer:
        line.begin(rows_in)
        keep.append(pltpu.make_async_copy(rows_in, rows_all.at[place.z], load_sem.at[4]))
        keep[0].start()
    for k in FAR_FIRST:
        give_right("down", 0, k, act_all.at[zs[k]], right_a)
        load = pltpu.make_async_copy(act_all.at[zs[k]], right_a.at[zs[k], pl.ds(0, rows)], load_sem.at[k])
        load.start()
        loads.append((k, load))
    w_sources = []
    for k in FAR_FIRST:
        w_sources += [down.at[zs[k]], up.at[zs[k]]]
    w_sources += [proj.at[zs[k]] for k in FAR_FIRST]
    weights = Stream(w_slots, w_sem, w_sources)
    hidden = Stream(hid_slots, hid_sem, [hid_all.at[zs[k]] for k in FAR_FIRST])
    saved = Stream(s_slots, s_sem, [s_all.at[zs[k]] for k in FAR_FIRST])
    attentions = Stream(att_slots, att_sem, [att_all.at[zs[k]] for k in FAR_FIRST])
    for stream in (weights, hidden, saved, attentions):
        stream.ensure(1)

    def weight_grad(name, k, buffer, *lefts):
        unit = units[name]
        part = dot_plain(left[lefts[0]], buffer[zs[k]])
        if len(lefts) > 1:
            part = jnp.where(columns < 3 * head_cols, part, dot_plain(left[lefts[1]], buffer[zs[k]]))
        low = part.astype(bf16)
        for block in range(4):
            unit.total[k, block // 2, block % 2] = low[block * cut : (block + 1) * cut]

    def compute():
        low_buf[0] = grad[...].astype(bf16)
        small_out[...] = jnp.zeros_like(small_out)
        small_out[5:6, :] = column_sums(low_buf[0].astype(f32))
        make_left(0, low_buf[0])
        left_ready(0)
        for k, load in loads:
            load.wait()
            right_copies["down", k].wait_recv()
            weight_grad("down", k, right_a, 0)
            yield 2.0, [(units["down"], k)]
        for k, load in loads:
            right_copies["down", k].wait_send()
        pl.semaphore_signal(credit, inc=1, device_id=core, device_id_type=MESH)
        unit, scale = unit_rows(mid_in[...])
        make_left(1, (unit * gains[1:2, :] + shifts[1:2, :]).astype(bf16))
        left_ready(1)
        yield 3.0, []
        for at, k in enumerate(FAR_FIRST):
            w = weights.take(2 * at)
            hid = hidden.take(at)
            act_grad = dot_plain(low_buf[0], w[...])
            hid_grad = (act_grad * gelu_slope(hid[...])).astype(bf16)
            right_b[zs[k], 0:rows] = hid_grad
            weights.ensure(2 * at + 2)
            hidden.ensure(at + 2)
            give_right("up", 1, k, right_b.at[zs[k], pl.ds(0, rows)], right_b)
            small_out[pl.ds(6 + zs[k], 1), :] = column_sums(hid_grad.astype(f32))
            yield 2.5, []
            w = weights.take(2 * at + 1)
            part = dot_turned(right_b[zs[k], 0:rows], w[...])
            acc_buf[...] = part if at == 0 else acc_buf[...] + part
            weights.ensure(2 * at + 3)
            yield 1.5, []
            right_copies["up", k].wait_recv()
            weight_grad("up", k, right_b, 1)
            yield 1.5, [(units["up"], k)]
        unit, scale = unit_rows(mid_in[...])
        from_norm = norm_back(acc_buf[...], unit, scale, gains[1:2, :])
        small_out[1:2, :] = column_sums(acc_buf[...] * unit)
        small_out[3:4, :] = column_sums(acc_buf[...])
        mid_grad[...] = grad[...] + from_norm
        low_buf[0] = mid_grad[...].astype(bf16)
        small_out[4:5, :] = column_sums(low_buf[0].astype(f32))
        yield 3.0, []
        make_left(2, low_buf[0])
        unit, scale = unit_rows(x_in[...])
        make_left(3, (unit * gains[0:1, :] + shifts[0:1, :]).astype(bf16))
        left_ready(2)
        left_ready(3)
        pl.semaphore_wait(credit, 1)
        yield 4.0, []
        head_of = column_ids(head_cols) // HEAD_DIM
        score_scale = HEAD_DIM ** (-0.5)
        for at, k in enumerate(FAR_FIRST):
            w = weights.take(8 + at)
            s = saved.take(at)
            attention_slot = attentions.take(at)
            low_buf[1] = dot_plain(low_buf[0], w[...]).astype(bf16)
            mixed_grad = low_buf[1, :, 3 * head_cols :]
            q = s[:, 0:head_cols]
            key = s[:, head_cols : 2 * head_cols]
            v = s[:, 2 * head_cols : 3 * head_cols]
            head_grads[...] = jnp.zeros_like(head_grads)

            def one_head(head, carry):
                here = head_of == head
                attention = attention_slot[head]
                own_grad = jnp.where(here, mixed_grad, 0)
                dot_back = dot_turned(own_grad, v)
                both = attention * dot_back
                score_low = (both - attention * jnp.sum(both, axis=-1, keepdims=True)).astype(bf16)
                first_row = pl.multiple_of(head * GRID, GRID)
                table_out[zs[k], pl.ds(first_row, GRID), :] = fold_window(score_low.astype(f32))
                head_grads[0] += dot_plain(score_low, jnp.where(here, key, 0))
                head_grads[1] += dot_rows(score_low, jnp.where(here, q, 0))
                head_grads[2] += dot_rows(attention.astype(bf16), own_grad)
                return carry

            lax.fori_loop(0, 4, one_head, 0)
            here = right_a.at[zs[k]]
            here[0:rows, 0:head_cols] = (head_grads[0] * score_scale).astype(bf16)
            here[0:rows, head_cols : 2 * head_cols] = (head_grads[1] * score_scale).astype(bf16)
            here[0:rows, 2 * head_cols : 3 * head_cols] = head_grads[2].astype(bf16)
            here[0:rows, 3 * head_cols :] = s[:, 3 * head_cols :]
            give_right("proj", 2, k, right_a.at[zs[k], pl.ds(0, rows)], right_a)
            saved.ensure(at + 2)
            attentions.ensure(at + 2)
            yield 6.0, []
            own = right_a[zs[k], 0:rows]
            small_out[pl.ds(10 + zs[k], 1), :] = column_sums(own.astype(f32))
            part = dot_turned(jnp.where(columns < 3 * head_cols, own, 0), w[...])
            acc_buf[...] = part if at == 0 else acc_buf[...] + part
            weights.ensure(8 + at + 2)
            right_copies["proj", k].wait_recv()
            yield 2.0, [], (units["down"], k)
            units["down"].settle((4 + k, 8 + k, 12 + k, 16 + k, 19 + k))
            weight_grad("proj", k, right_a, 3, 2)
            yield 2.0, [(units["proj"], k)]
        unit, scale = unit_rows(x_in[...])
        from_norm = norm_back(acc_buf[...], unit, scale, gains[0:1, :])
        small_out[0:1, :] = column_sums(acc_buf[...] * unit)
        small_out[2:3, :] = column_sums(acc_buf[...])
        grad_out[...] = mid_grad[...] + from_norm
        if not last_layer:
            low_buf[0] = grad_out[...].astype(bf16)
            line.begin(low_buf.at[0])
            keep.append(pltpu.make_async_copy(low_buf.at[0], rows_all.at[place.z], load_sem.at[4]))
            keep[0].start()
        yield 2.0, []

    def more_events():
        if last_layer:
            return [(20.0 * far_off, functools.partial(line.arrive, far_off)) for far_off in (1, 2, 3)]
        return []

    merge_steps(compute(), more_events(), 10.7, 9.0)
    for (name, k), copy in right_copies.items():
        if name != "down":
            copy.wait_send()
    for at in (2, 3):
        for copy in left_copies[at]:
            copy.wait_send()
    if not last_layer:
        for far_off in (1, 2, 3):
            line.arrive(far_off)
    line.finish()
    keep[0].wait()
    gathered = pltpu.make_async_copy(rows_all, right_b.at[:, pl.ds(0, rows)], load_sem.at[4])
    gathered.start()
    gathered.wait()
    total = dot_plain(pick[:, 0:rows], right_b[0, 0:rows])
    for z in range(1, 4):
        total = total + dot_plain(pick[:, z * rows : (z + 1) * rows], right_b[z, 0:rows])
    rows_out[...] = total.astype(bf16)


def merge_steps(compute, events, links, late):
    clock, link_free = 0.0, 0.0
    events = list(events)

    def run_first():
        events.sort(key=lambda item: item[0])
        at, step = events.pop(0)
        for delay, following in step() or ():
            events.append((max(clock, at) + delay, following))
        return max(clock, at)

    while True:
        while events and min(item[0] for item in events) <= clock:
            clock = run_first()
        made = next(compute, None)
        if made is None:
            break
        clock += made[0]
        for unit, k in made[1]:
            unit.first_stage(k)
            start = max(clock, link_free)
            link_free = start + links
            events.append((start + late, functools.partial(scatter_step, unit, k, late)))
        if len(made) > 2:
            unit, k = made[2]
            while k not in unit.closed:
                clock = run_first()
    while events:
        clock = run_first()


def backward_layer(last_layer, grad, saved, gains, shifts, pick, rows_in, weights):
    x_in, mid_in, s_all, att_all, hid_all, act_all = saved
    proj, up, down = weights
    rows, d_model = grad.shape
    cut = d_model // 8
    any_space = pl.BlockSpec(memory_space=pl.ANY)
    vmem = pl.BlockSpec(memory_space=pltpu.VMEM)
    block = jax.ShapeDtypeStruct((cut, d_model), f32)
    out_shape = [
        block,
        block,
        block,
        jax.ShapeDtypeStruct((rows, d_model), f32),
        jax.ShapeDtypeStruct((rows, d_model), bf16),
        jax.ShapeDtypeStruct((16, d_model), f32),
        jax.ShapeDtypeStruct((4, 4 * GRID, 512), f32),
        jax.ShapeDtypeStruct((4, rows, d_model), bf16),
    ]
    dma = pltpu.SemaphoreType.DMA
    scratch = [
        pltpu.VMEM((4, 2, 2, cut, d_model), bf16),
        pltpu.VMEM((4, 2, 2, cut, d_model), bf16),
        pltpu.VMEM((3, 4, 2, cut, d_model), bf16),
        pltpu.VMEM((3, 4, cut, d_model), bf16),
        pltpu.VMEM((3, 3, cut, d_model), bf16),
        pltpu.VMEM((4, 2 * rows, d_model), bf16),
        pltpu.VMEM((4, 2 * rows, d_model), bf16),
        pltpu.VMEM((4, 4 * cut, 2 * rows), bf16),
        pltpu.VMEM((2, d_model, rows), bf16),
        pltpu.VMEM((2, d_model, d_model), bf16),
        pltpu.VMEM((2, rows, d_model), bf16),
        pltpu.VMEM((2, 4, rows, rows), f32),
        pltpu.VMEM((2, rows, d_model), f32),
        pltpu.VMEM((rows, d_model), f32),
        pltpu.VMEM((rows, d_model), f32),
        pltpu.VMEM((2, rows, d_model), bf16),
        pltpu.VMEM((3, rows, d_model // 4), f32),
        dma((3, SCATTER_SEMS)),
        dma((3, SCATTER_SEMS)),
        dma((4, 4)),
        dma((4, 4)),
        dma((LINE_SEMS,)),
        dma((LINE_SEMS,)),
        dma((2,)),
        dma((2,)),
        dma((2,)),
        dma((2,)),
        dma((5,)),
        pltpu.SemaphoreType.REGULAR,
    ]
    return pl.pallas_call(
        functools.partial(backward_kernel, last_layer),
        out_shape=out_shape,
        in_specs=[vmem] * 6 + [any_space] * 8,
        out_specs=[vmem] * 7 + [any_space],
        scratch_shapes=scratch,
        compiler_params=pltpu.CompilerParams(
            collective_id=1 if last_layer else 2, has_side_effects=True, vmem_limit_bytes=63 * 2**20
        ),
        name="backward_last" if last_layer else "backward_first",
    )(grad, x_in, mid_in, gains, shifts, pick, rows_in, s_all, att_all, hid_all, act_all, proj, up, down)


def shards_plain(
    tokens,
    cotangent,
    segment_ids,
    patch_pos,
    time_index,
    time_table,
    norm_gain,
    norm_shift,
    attn_weight,
    out_weight,
    qkv_bias,
    out_bias,
    mlp_weight,
    up_bias,
    rel_table,
):
    image_count = time_index.shape[0]
    layer_count = attn_weight.shape[0]
    narrow_at = lax.axis_index("narrow")
    wide_at = lax.axis_index("wide")
    wide_size = lax.axis_size("wide")
    own_rows = tokens.shape[0]
    in_rows, cols = attn_weight.shape[2:]
    image_local = segment_ids % image_count
    grid_slot = image_local * PATCHES + patch_pos
    own_slots = narrow_at * own_rows + jnp.arange(own_rows, dtype=jnp.int32)
    pick_in = (own_slots[:, None] == grid_slot[None, :]).astype(bf16)
    own_grid = lax.dynamic_slice_in_dim(grid_slot, narrow_at * own_rows, own_rows)
    pick_out = (own_grid[:, None] == jnp.arange(grid_slot.shape[0], dtype=jnp.int32)[None, :]).astype(bf16)

    def to_images(rows):
        every = lax.all_gather(rows, "narrow", axis=0, tiled=True)
        return jnp.dot(pick_in, every, preferred_element_type=f32)

    def to_rows(rows):
        every = lax.all_gather(rows, "narrow", axis=0, tiled=True)
        return jnp.dot(pick_out, every, preferred_element_type=f32).astype(bf16)

    steps_all = lax.all_gather(time_index, "wide", axis=0, tiled=True)
    step_hot = (steps_all[:, None] == jnp.arange(time_table.shape[0], dtype=jnp.int32)[None, :]).astype(bf16)
    time_rows = jnp.dot(step_hot, time_table, preferred_element_type=f32).astype(bf16)
    time_slice = lax.dynamic_slice_in_dim(time_rows, wide_at * in_rows, in_rows, axis=1)
    time_weight = attn_weight[:, 3:6]
    time_share = jnp.einsum("id,ljdc->ljic", time_slice, time_weight, preferred_element_type=f32)
    time_share = lax.psum_scatter(time_share, "wide", scatter_dimension=2, tiled=True)
    time_share = lax.all_gather(time_share, "narrow", axis=3, tiled=True)
    time_part = lax.dynamic_index_in_dim(time_share, narrow_at, axis=2, keepdims=False)

    tables = lax.all_gather(rel_table, "narrow", axis=1, tiled=True)
    qkv_bias_all = lax.all_gather(qkv_bias, "narrow", axis=2, tiled=True)
    up_bias_all = lax.all_gather(up_bias, "narrow", axis=1, tiled=True)

    def layer_params(at):
        return (norm_gain[at], norm_shift[at], qkv_bias_all[at], out_bias[at])

    weights = []
    for at in range(layer_count):
        packed = jnp.concatenate([attn_weight[at, 0], attn_weight[at, 1], attn_weight[at, 2], out_weight[at]], axis=1)
        weights.append((gather_unit(packed), gather_unit(mlp_weight[at, 0]), gather_unit(mlp_weight[at, 1])))

    residual = to_images(tokens)
    kept = []
    for at in range(layer_count):
        pairs = pair_bias(tables[at])
        middle, attn_saved = attention_forward(residual, weights[at][0], time_part[at], layer_params(at), pairs)
        residual, mlp_saved = mlp_forward(middle, weights[at][1], weights[at][2], layer_params(at), up_bias_all[at])
        kept.append((attn_saved, mlp_saved))
    block_output = to_rows(residual.astype(bf16))
    gradient = to_images(cotangent)
    attn_grads, out_grads, mlp_grads = [], [], []
    time_sums, small = [], []
    for at in reversed(range(layer_count)):
        attn_saved, mlp_saved = kept[at]
        grad_mid, up_grad, down_grad, mlp_small = mlp_backward(
            gradient, weights[at][1], weights[at][2], layer_params(at), mlp_saved
        )
        mlp_grads.insert(0, jnp.stack([scatter_unit(up_grad), scatter_unit(down_grad)]))
        gradient, proj_grad, sums, table_grad, attn_small = attention_backward(
            grad_mid, weights[at][0], layer_params(at), attn_saved
        )
        packed = scatter_unit(proj_grad)
        attn_grads.insert(0, jnp.stack([packed[:, j * cols : (j + 1) * cols] for j in range(3)]))
        out_grads.insert(0, packed[:, 3 * cols :])
        time_sums.insert(0, sums)
        small.insert(
            0,
            (
                jnp.stack([attn_small[0], mlp_small[0]]),
                jnp.stack([attn_small[1], mlp_small[1]]),
                jnp.stack([attn_small[2], mlp_small[2]]),
                jnp.stack([sums[0], sums[2]]),
                mlp_small[3],
                table_grad,
            ),
        )
    input_grad = to_rows(gradient.astype(bf16))

    def stacked(index_at):
        return jnp.stack([entry[index_at] for entry in small])

    totals = lax.psum(tuple(stacked(index_at) for index_at in range(6)), ("wide", "narrow"))

    def own_part(array, axis):
        size = array.shape[axis] // lax.axis_size("narrow")
        return lax.dynamic_slice_in_dim(array, narrow_at * size, size, axis=axis)

    time_low = jnp.stack(time_sums).astype(bf16)
    time_all = lax.all_gather(time_low, ("wide", "narrow"), axis=0, tiled=False)
    time_own = own_part(time_all, 3)
    time_weight_grad = jnp.einsum("id,iljc->ljdc", time_slice, time_own, preferred_element_type=f32)
    trow_share = jnp.einsum("iljc,ljdc->id", time_own, time_weight, preferred_element_type=f32)
    trow_share = lax.psum(trow_share, "narrow")
    trow = lax.all_gather(trow_share, "wide", axis=1, tiled=True)
    time_grad = jnp.einsum("is,id->sd", step_hot.astype(f32), trow, precision=highest)
    attn_grad = jnp.concatenate([jnp.stack(attn_grads).astype(f32), time_weight_grad], axis=1)
    return (
        block_output,
        input_grad,
        time_grad,
        totals[0],
        totals[1],
        attn_grad,
        jnp.stack(out_grads).astype(f32),
        own_part(totals[3], 2),
        totals[2],
        jnp.stack(mlp_grads).astype(f32),
        own_part(totals[4], 1),
        own_part(totals[5], 1),
    )


def bias_windows(tables):
    layers, heads = tables.shape[:2]
    near = jnp.arange(GRID, dtype=jnp.int32)
    span = jnp.arange(SPAN, dtype=jnp.int32)
    steps = (span[None, :, None] == near[:, None, None] - near[None, None, :] + (GRID - 1)).astype(f32)
    grid = tables.reshape(layers, heads, SPAN, SPAN)[:, :, ::-1]
    windows = jnp.einsum("lhab,xby->lhxay", grid, steps, precision=highest)
    windows = windows.reshape(layers, heads * GRID, SPAN * GRID)
    return jnp.pad(windows, ((0, 0), (0, 0), (0, 512 - SPAN * GRID)))


def fold_windows(windows):
    layers, heads = windows.shape[0], windows.shape[1] // GRID
    near = jnp.arange(GRID, dtype=jnp.int32)
    span = jnp.arange(SPAN, dtype=jnp.int32)
    steps = (span[None, :, None] == near[:, None, None] - near[None, None, :] + (GRID - 1)).astype(f32)
    grid = windows[:, :, : SPAN * GRID].reshape(layers, heads, GRID, SPAN, GRID)
    tables = jnp.einsum("lhxay,xby->lhab", grid, steps, precision=highest)
    return tables[:, :, ::-1].reshape(layers, heads, SPAN * SPAN)


def shards(
    tokens,
    cotangent,
    segment_ids,
    patch_pos,
    time_index,
    time_table,
    norm_gain,
    norm_shift,
    attn_weight,
    out_weight,
    qkv_bias,
    out_bias,
    mlp_weight,
    up_bias,
    rel_table,
):
    image_count = time_index.shape[0]
    layer_count = attn_weight.shape[0]
    in_rows, cols = attn_weight.shape[2:]
    by_links = lax.axis_size("wide") == 8 and lax.axis_size("narrow") == 4 and in_rows % 16 == 0
    if not by_links:
        return shards_plain(
            tokens, cotangent, segment_ids, patch_pos, time_index, time_table, norm_gain, norm_shift,
            attn_weight, out_weight, qkv_bias, out_bias, mlp_weight, up_bias, rel_table,
        )
    narrow_at = lax.axis_index("narrow")
    wide_at = lax.axis_index("wide")
    own_rows, d_model = tokens.shape
    image_local = segment_ids % image_count
    grid_slot = image_local * PATCHES + patch_pos
    own_slots = narrow_at * own_rows + jnp.arange(own_rows, dtype=jnp.int32)
    pick_in = (own_slots[:, None] == grid_slot[None, :]).astype(bf16)
    own_grid = lax.dynamic_slice_in_dim(grid_slot, narrow_at * own_rows, own_rows)
    pick_out = (own_grid[:, None] == jnp.arange(grid_slot.shape[0], dtype=jnp.int32)[None, :]).astype(bf16)

    step_own = (time_index[:, None] == jnp.arange(time_table.shape[0], dtype=jnp.int32)[None, :]).astype(bf16)
    time_own = jnp.dot(step_own, time_table, preferred_element_type=f32).astype(bf16)
    digits = jnp.stack([time_index // 32, time_index % 32]).astype(bf16)
    digits = jnp.pad(digits, ((0, 16 - image_count - 2), (0, d_model - image_count)))
    time_own = jnp.concatenate([time_own, digits], axis=0)
    time_weight = attn_weight[:, 3:6]
    time_packed = jnp.concatenate(
        [time_weight[:, 0], time_weight[:, 1], time_weight[:, 2], jnp.zeros_like(time_weight[:, 0])], axis=2
    )
    qkv_packed = jnp.concatenate(
        [qkv_bias[:, 0], jnp.zeros_like(qkv_bias[:, 0]), qkv_bias[:, 1], jnp.zeros_like(qkv_bias[:, 0])], axis=1
    )
    small_own = jnp.pad(jnp.concatenate([up_bias, qkv_packed], axis=0), ((0, 8 - 2 * layer_count), (0, 0)))
    pieces = []
    for at in range(layer_count):
        packed = jnp.concatenate([attn_weight[at, 0], attn_weight[at, 1], attn_weight[at, 2], out_weight[at]], axis=1)
        pieces += [packed, mlp_weight[at, 0], mlp_weight[at, 1]]
    wholes, saved, (block_low, gradient, time_all, time_sel) = forward_all(
        tokens,
        cotangent,
        pick_in,
        time_own,
        time_packed,
        bias_windows(rel_table),
        small_own,
        norm_gain.reshape(-1, d_model),
        norm_shift.reshape(-1, d_model),
        out_bias.reshape(-1, d_model),
        pieces,
    )
    time_all = time_all.reshape(8, 16, d_model)
    steps_all = time_all[:, image_count : image_count + 2, :image_count].astype(f32)
    steps_all = (steps_all[:, 0] * 32 + steps_all[:, 1]).astype(jnp.int32).reshape(-1)
    step_hot = (steps_all[:, None] == jnp.arange(time_table.shape[0], dtype=jnp.int32)[None, :]).astype(f32)
    time_slice = time_sel.reshape(8, 16, in_rows)[:, :image_count].reshape(-1, in_rows)

    def layer_back(at, grad, rows_in):
        return backward_layer(
            at == layer_count - 1, grad, saved[at], norm_gain[at], norm_shift[at], pick_out, rows_in,
            wholes[3 * at : 3 * at + 3],
        )

    attn_grads, out_grads, mlp_grads = [], [], []
    time_sums, small = [], []
    block_output = None
    for at in reversed(range(layer_count)):
        packed, up_part, down_part, gradient, moved, sums, windows, _ = layer_back(at, gradient, block_low)
        if at == layer_count - 1:
            block_output = moved
        mlp_grads.insert(0, jnp.stack([up_part, down_part]))
        attn_grads.insert(0, jnp.stack([packed[:, j * cols : (j + 1) * cols] for j in range(3)]))
        out_grads.insert(0, packed[:, 3 * cols :])
        qkv_sums = jnp.stack([sums[10:14, j * cols : (j + 1) * cols].reshape(-1) for j in range(3)])
        time_sums.insert(0, qkv_sums)
        small.insert(
            0,
            (
                sums[0:2],
                sums[2:4],
                sums[4:6],
                jnp.stack([qkv_sums[0], qkv_sums[2]]),
                sums[6:10].reshape(-1),
                windows.reshape(-1, 512),
            ),
        )
    input_grad = moved

    def stacked(index_at):
        return jnp.stack([entry[index_at] for entry in small])

    tables = fold_windows(stacked(5))
    totals = lax.psum(tuple(stacked(index_at) for index_at in range(5)) + (tables,), ("wide", "narrow"))

    def own_part(array, axis):
        size = array.shape[axis] // lax.axis_size("narrow")
        return lax.dynamic_slice_in_dim(array, narrow_at * size, size, axis=axis)

    time_low = jnp.stack(time_sums).astype(bf16)
    time_every = lax.all_gather(time_low, ("wide", "narrow"), axis=0, tiled=False)
    time_part = own_part(time_every, 3)
    time_weight_grad = jnp.einsum("id,iljc->ljdc", time_slice, time_part, preferred_element_type=f32)
    trow_share = jnp.einsum("iljc,ljdc->id", time_part, time_weight, preferred_element_type=f32)
    trow_share = lax.psum(trow_share, "narrow")
    trow = lax.all_gather(trow_share, "wide", axis=1, tiled=True)
    time_grad = jnp.einsum("is,id->sd", step_hot, trow, precision=highest)
    attn_grad = jnp.concatenate([jnp.stack(attn_grads), time_weight_grad], axis=1)
    return (
        block_output,
        input_grad,
        time_grad,
        totals[0],
        totals[1],
        attn_grad,
        jnp.stack(out_grads),
        own_part(totals[3], 2),
        totals[2],
        jnp.stack(mlp_grads),
        own_part(totals[4], 1),
        own_part(totals[5], 1),
    )


def solution(mesh):
    return jax.shard_map(
        shards,
        mesh=mesh,
        in_specs=(
            P(("wide", "narrow"), None),
            P(("wide", "narrow"), None),
            P("wide"),
            P("wide"),
            P("wide"),
            P(),
            P(),
            P(),
            P(None, None, "wide", "narrow"),
            P(None, "wide", "narrow"),
            P(None, None, "narrow"),
            P(),
            P(None, None, "wide", "narrow"),
            P(None, "narrow"),
            P(None, "narrow", None),
        ),
        out_specs=(
            P(("wide", "narrow"), None),
            P(("wide", "narrow"), None),
            P(),
            P(),
            P(),
            P(None, None, "wide", "narrow"),
            P(None, "wide", "narrow"),
            P(None, None, "narrow"),
            P(),
            P(None, None, "wide", "narrow"),
            P(None, "narrow"),
            P(None, "narrow", None),
        ),
        check_vma=False,
    )
```

```python
import functools
import math

import jax
import jax.numpy as jnp
from jax import lax
from jax.experimental import pallas as pl
from jax.experimental.pallas import tpu as pltpu
from jax.sharding import PartitionSpec as P

HEAD_DIM = 72
GRID = 16
PATCHES = GRID * GRID
SPAN = 2 * GRID - 1


eps_norm = 1e-06
highest = lax.Precision.HIGHEST
f32 = jnp.float32
bf16 = jnp.bfloat16
ROWS_AXES = ("narrow", "wide")
MESH = pl.DeviceIdType.MESH


def layer_norm(values, norm_gain, norm_shift):
    average = jnp.mean(values, axis=-1, keepdims=True)
    centred = values - average
    variance = jnp.mean(centred * centred, axis=-1, keepdims=True)
    scale = lax.rsqrt(variance + eps_norm)
    unit = centred * scale
    return unit * norm_gain + norm_shift, unit, scale


def layer_norm_back(grad, unit, scale, norm_gain):
    weighted = grad * norm_gain
    first = jnp.mean(weighted, axis=-1, keepdims=True)
    second = jnp.mean(weighted * unit, axis=-1, keepdims=True)
    from_norm = scale * (weighted - first - unit * second)
    return from_norm, jnp.sum(grad * unit, axis=0), jnp.sum(grad, axis=0)


def offset_onehot():
    near = jnp.arange(GRID, dtype=jnp.int32)
    span = jnp.arange(SPAN, dtype=jnp.int32)
    return (span[None, None, :] == near[:, None, None] - near[None, :, None] + (GRID - 1)).astype(f32)


def pair_bias(bias_table):
    steps_hot = offset_onehot()
    head_count = bias_table.shape[0]
    table_grid = bias_table.reshape(head_count, SPAN, SPAN)
    row_part = jnp.einsum("ixa,hab->hixb", steps_hot, table_grid, precision=highest)
    pairs = jnp.einsum("jyb,hixb->hijxy", steps_hot, row_part, precision=highest)
    return pairs.reshape(head_count, PATCHES, PATCHES)


def fold_bias_grad(pair_grad):
    steps_hot = offset_onehot()
    head_count = pair_grad.shape[0]
    grid_grad = pair_grad.reshape(head_count, GRID, GRID, GRID, GRID)
    col_part = jnp.einsum("jyb,hijxy->hixb", steps_hot, grid_grad, precision=highest)
    table_grad = jnp.einsum("ixa,hixb->hab", steps_hot, col_part, precision=highest)
    return table_grad.reshape(head_count, SPAN * SPAN)


def gather_unit(piece):
    parts = lax.axis_size("narrow")
    whole = lax.all_gather(piece, ROWS_AXES, axis=0, tiled=True)
    return whole.reshape(parts, whole.shape[0] // parts, whole.shape[1])


def scatter_unit(grads):
    flat = grads.astype(bf16).reshape(-1, grads.shape[-1])
    return lax.psum_scatter(flat, ROWS_AXES, scatter_dimension=0, tiled=True)


def to_heads(values):
    parts, rows, cols = values.shape
    split = values.reshape(parts, rows, cols // HEAD_DIM, HEAD_DIM)
    return split.transpose(0, 2, 1, 3).reshape(-1, rows, HEAD_DIM)


def from_heads(values, parts):
    heads, rows, _ = values.shape
    split = values.reshape(parts, heads // parts, rows, HEAD_DIM).transpose(0, 2, 1, 3)
    return split.reshape(parts, rows, -1)


def attention_forward(residual, proj, time_part, params, pairs):
    norm_gain, norm_shift, qkv_bias, out_bias = params
    parts = proj.shape[0]
    cols = proj.shape[2] // 4
    normed, unit, scale = layer_norm(residual, norm_gain[0], norm_shift[0])
    normed_low = normed.astype(bf16)
    spatial = jnp.einsum("rd,zdc->zrc", normed_low, proj[:, :, : 3 * cols], preferred_element_type=f32)
    offsets = time_part + jnp.stack([qkv_bias[0], jnp.zeros_like(qkv_bias[0]), qkv_bias[1]])
    offsets = offsets.reshape(3, parts, 1, cols)
    queries, key_rows, value_rows = (
        to_heads((spatial[:, :, j * cols : (j + 1) * cols] + offsets[j]).astype(bf16)) for j in range(3)
    )
    scores = jnp.einsum("hqd,hkd->hqk", queries, key_rows, preferred_element_type=f32)
    scores = scores * HEAD_DIM ** (-0.5) + pairs
    attention = jax.nn.softmax(scores, axis=-1)
    attention_low = attention.astype(bf16)
    mixed = jnp.einsum("hqk,hkd->hqd", attention_low, value_rows, preferred_element_type=f32)
    mixed_low = from_heads(mixed.astype(bf16), parts)
    branch = jnp.einsum("zrc,zdc->rd", mixed_low, proj[:, :, 3 * cols :], preferred_element_type=f32)
    middle = residual + (branch + out_bias[0])
    saved = (normed_low, unit, scale, queries, key_rows, value_rows, attention, mixed_low)
    return middle, saved


def mlp_forward(middle, up, down, params, up_bias):
    norm_gain, norm_shift, qkv_bias, out_bias = params
    parts = up.shape[0]
    normed, unit, scale = layer_norm(middle, norm_gain[1], norm_shift[1])
    normed_low = normed.astype(bf16)
    hidden = jnp.einsum("rd,zdc->zrc", normed_low, up, preferred_element_type=f32)
    hidden = hidden + up_bias.reshape(parts, 1, -1)
    activated = jax.nn.gelu(hidden, approximate=True).astype(bf16)
    branch = jnp.einsum("zrc,zdc->rd", activated, down, preferred_element_type=f32)
    return middle + (branch + out_bias[1]), (normed_low, unit, scale, hidden, activated)


def mlp_backward(gradient, up, down, params, saved):
    norm_gain = params[0]
    normed_low, unit, scale, hidden, activated = saved
    grad_low = gradient.astype(bf16)
    out_bias_grad = jnp.sum(grad_low.astype(f32), axis=0)
    down_grad = jnp.einsum("rd,zrc->zdc", grad_low, activated, preferred_element_type=f32)
    act_grad = jnp.einsum("rd,zdc->zrc", grad_low, down, preferred_element_type=f32)
    _, gelu_back = jax.vjp(lambda values: jax.nn.gelu(values, approximate=True), hidden)
    hidden_low = gelu_back(act_grad)[0].astype(bf16)
    up_bias_grad = jnp.sum(hidden_low.astype(f32), axis=1).reshape(-1)
    up_grad = jnp.einsum("rd,zrc->zdc", normed_low, hidden_low, preferred_element_type=f32)
    normed_grad = jnp.einsum("zrc,zdc->rd", hidden_low, up, preferred_element_type=f32)
    from_norm, gain_grad, shift_grad = layer_norm_back(normed_grad, unit, scale, norm_gain[1])
    return gradient + from_norm, up_grad, down_grad, (gain_grad, shift_grad, out_bias_grad, up_bias_grad)


def attention_backward(grad_mid, proj, params, saved):
    norm_gain = params[0]
    normed_low, unit, scale, queries, key_rows, value_rows, attention, mixed_low = saved
    parts = proj.shape[0]
    cols = proj.shape[2] // 4
    score_scale = HEAD_DIM ** (-0.5)
    mid_low = grad_mid.astype(bf16)
    out_bias_grad = jnp.sum(mid_low.astype(f32), axis=0)
    out_grad = jnp.einsum("rd,zrc->zdc", mid_low, mixed_low, preferred_element_type=f32)
    mixed_grad = jnp.einsum("rd,zdc->zrc", mid_low, proj[:, :, 3 * cols :], preferred_element_type=f32)
    mixed_grad = to_heads(mixed_grad.astype(bf16))
    dot_back = jnp.einsum("hqd,hkd->hqk", mixed_grad, value_rows, preferred_element_type=f32)
    score_grad = attention * (dot_back - jnp.sum(attention * dot_back, axis=-1, keepdims=True))
    score_low = score_grad.astype(bf16)
    table_grad = fold_bias_grad(score_low.astype(f32))
    query_grad = jnp.einsum("hqk,hkd->hqd", score_low, key_rows, preferred_element_type=f32) * score_scale
    key_grad = jnp.einsum("hqk,hqd->hkd", score_low, queries, preferred_element_type=f32) * score_scale
    value_grad = jnp.einsum("hqk,hqd->hkd", attention.astype(bf16), mixed_grad, preferred_element_type=f32)
    qkv_low = jnp.concatenate(
        [from_heads(item.astype(bf16), parts) for item in (query_grad, key_grad, value_grad)], axis=-1
    )
    spatial_grad = jnp.einsum("rd,zrc->zdc", normed_low, qkv_low, preferred_element_type=f32)
    proj_grad = jnp.concatenate([spatial_grad, out_grad], axis=-1)
    sums = jnp.sum(qkv_low.astype(f32), axis=1).reshape(parts, 3, cols).transpose(1, 0, 2).reshape(3, -1)
    normed_grad = jnp.einsum("zrc,zdc->rd", qkv_low, proj[:, :, : 3 * cols], preferred_element_type=f32)
    from_norm, gain_grad, shift_grad = layer_norm_back(normed_grad, unit, scale, norm_gain[0])
    return grad_mid + from_norm, proj_grad, sums, table_grad, (gain_grad, shift_grad, out_bias_grad)


class Place:
    def __init__(self):
        wide = lax.axis_index("wide")
        self.z = lax.axis_index("narrow")
        self.y, self.x, self.c = wide // 4, (wide // 2) % 2, wide % 2

    def wide(self, flip_y=0, flip_x=0, flip_c=0):
        y = 1 - self.y if flip_y else self.y
        x = 1 - self.x if flip_x else self.x
        c = 1 - self.c if flip_c else self.c
        return y * 4 + x * 2 + c

    def along_z(self, steps):
        return lax.rem(self.z + steps, 4)

    def peers(self):
        across = [(self.wide(1, 0, 0), self.z), (self.wide(0, 1, 0), self.z), (self.wide(0, 0, 1), self.z)]
        return across + [(self.wide(), self.along_z(k)) for k in (1, 2, 3)]

    def greet(self):
        barrier = pltpu.get_barrier_semaphore()
        for peer in self.peers():
            pl.semaphore_signal(barrier, inc=1, device_id=peer, device_id_type=MESH)
        pl.semaphore_wait(barrier, 6)


def unit_cut(unit, rows):
    low = rows // 32 * 16
    return low if unit % 2 == 0 else rows - low


class Line:
    def __init__(self, place, block, send, recv):
        self.place, self.block, self.send, self.recv = place, block, send, recv

    def copy(self, src, origin, step, slot):
        place = self.place
        return pltpu.make_async_remote_copy(
            src_ref=src, dst_ref=self.block(origin), send_sem=self.send.at[slot], recv_sem=self.recv.at[origin],
            device_id=(place.wide(), place.z + step), device_id_type=MESH,
        )

    def begin(self, own):
        z = self.place.z

        @pl.when(z < 3)
        def _():
            self.copy(own, z, 1, z).start()

        @pl.when(z > 0)
        def _():
            self.copy(own, z, -1, 4).start()

    def arrive(self, far, then=lambda origin: None):
        z = self.place.z
        for side, valid, room in ((-1, z - far >= 0, z < 3), (1, z + far <= 3, z > 0)):

            @pl.when(valid)
            def _(side=side, room=room):
                origin = z + side * far
                here = self.block(origin)
                self.copy(here, origin, -side, origin).wait_recv()

                @pl.when(room)
                def _():
                    self.copy(here, origin, -side, origin).start()

                then(origin)

    def finish(self):
        z = self.place.z
        for origin in range(4):
            sent = jnp.where(origin <= z, z < 3, z > 0)

            @pl.when(sent)
            def _(origin=origin):
                self.copy(self.block(origin), origin, 0, origin).wait_send()

        @pl.when(z > 0)
        def _():
            self.copy(self.block(0), 0, 0, 4).wait_send()


LINE_SEMS = 5
Z_AHEAD = 43.0
UNIT_TIME = 43.0
GATHER_SEMS = 58
Y_FIRST, X_LAST, X_NEAR, X_FAR, Y_NEAR, Y_FAR = 5, 9, 13, 17, 21, 25
C_OWN, C_Y, C_X, C_X_NEAR, C_Y_NEAR, C_X_FAR, C_Y_FAR = 29, 33, 37, 41, 45, 49, 53


class GatherUnit:
    def __init__(self, place, piece, whole, send, recv, cut):
        self.place, self.piece, self.whole = place, piece, whole
        self.send, self.recv = send, recv
        self.rows = piece.shape[0]
        self.first, self.last, self.every = pl.ds(0, cut), pl.ds(cut, self.rows - cut), pl.ds(0, self.rows)
        self.line = Line(place, lambda origin: self.block(origin, 0, 0, self.every), send, recv)
        self.peer = {
            "y": (place.wide(1, 0, 0), place.z), "x": (place.wide(0, 1, 0), place.z), "c": (place.wide(0, 0, 1), place.z)
        }
        self.order = [place.along_z(k) for k in (0, 1, 3, 2)]
        self.sent = []

    def block(self, origin, flip_y, flip_x, rows):
        first = pl.multiple_of(self.place.wide(flip_y, flip_x) * self.rows + rows.start, 16)
        return self.whole.at[origin, pl.ds(first, rows.size)]

    def copy(self, base, axis, origin, flip_y, flip_x, rows, own=None):
        block = self.block(origin, flip_y, flip_x, rows)
        return pltpu.make_async_remote_copy(
            src_ref=block if own is None else own, dst_ref=block, send_sem=self.send.at[base + origin],
            recv_sem=self.recv.at[base + origin], device_id=self.peer[axis], device_id_type=MESH,
        )

    def put(self, *where):
        self.copy(*where).start()

    def wait(self, *where):
        self.copy(*where).wait_recv()

    def begin(self):
        z = self.place.z
        self.line.begin(self.piece)
        self.put(Y_FIRST, "y", z, 0, 0, self.first, self.piece.at[self.first])
        self.put(X_LAST, "x", z, 0, 0, self.last, self.piece.at[self.last])
        self.put(X_NEAR, "x", z, 0, 0, self.first, self.piece.at[self.first])
        self.put(Y_NEAR, "y", z, 0, 0, self.last, self.piece.at[self.last])
        self.put(C_OWN, "c", z, 0, 0, self.every, self.piece)
        self.local = pltpu.make_async_copy(self.piece, self.block(z, 0, 0, self.every), self.send.at[GATHER_SEMS - 1])
        self.local.start()

    def along_z(self, far):
        def then(origin):
            self.put(Y_FIRST, "y", origin, 0, 0, self.first)
            self.put(X_LAST, "x", origin, 0, 0, self.last)
            self.put(X_NEAR, "x", origin, 0, 0, self.first)
            self.put(Y_NEAR, "y", origin, 0, 0, self.last)
            self.put(C_OWN, "c", origin, 0, 0, self.every)

        self.line.arrive(far, then)

    def across(self, at):
        origin = self.order[at]
        self.wait(Y_FIRST, "y", origin, 1, 0, self.first)
        self.put(X_FAR, "x", origin, 1, 0, self.first)
        self.put(C_Y, "c", origin, 1, 0, self.first)
        self.wait(X_LAST, "x", origin, 0, 1, self.last)
        self.put(Y_FAR, "y", origin, 0, 1, self.last)
        self.put(C_X, "c", origin, 0, 1, self.last)

    def near_to_core(self, at):
        origin = self.order[at]
        self.wait(X_NEAR, "x", origin, 0, 1, self.first)
        self.put(C_X_NEAR, "c", origin, 0, 1, self.first)
        self.wait(Y_NEAR, "y", origin, 1, 0, self.last)
        self.put(C_Y_NEAR, "c", origin, 1, 0, self.last)

    def far_to_core(self, at):
        origin = self.order[at]
        self.wait(X_FAR, "x", origin, 1, 1, self.first)
        self.put(C_X_FAR, "c", origin, 1, 1, self.first)
        self.wait(Y_FAR, "y", origin, 1, 1, self.last)
        self.put(C_Y_FAR, "c", origin, 1, 1, self.last)

    def steps(self, base):
        start = max(0.0, base - Z_AHEAD)
        out = [(start, self.begin)]
        out += [(start + 1.0 + 7.5 * far, functools.partial(self.along_z, far)) for far in (1, 2, 3)]
        for at in range(4):
            known = start + 24.0 if at else 0.0
            out.append((max(known, base + 9.0 + 9.0 * at), functools.partial(self.across, at)))
            out.append((max(known + 1.0, base + 15.0 + 9.0 * at), functools.partial(self.near_to_core, at)))
            out.append((max(known + 2.0, base + 25.0 + 9.0 * at), functools.partial(self.far_to_core, at)))
        out.append((base + 56.0, self.finish))
        return out

    def finish(self):
        firsts = (Y_FIRST, X_NEAR, X_FAR, C_Y, C_X_NEAR, C_X_FAR)
        lasts = (X_LAST, Y_NEAR, Y_FAR, C_X, C_Y_NEAR, C_Y_FAR)
        for origin in range(4):
            for base in (C_Y, C_X_NEAR, C_X_FAR):
                self.wait(base, "c", origin, 0, 0, self.first)
            for base in (C_X, C_Y_NEAR, C_Y_FAR):
                self.wait(base, "c", origin, 0, 0, self.last)
            self.wait(C_OWN, "c", origin, 0, 0, self.every)
        for origin in range(4):
            for base in firsts:
                self.copy(base, "c", origin, 0, 0, self.first).wait_send()
            for base in lasts:
                self.copy(base, "c", origin, 0, 0, self.last).wait_send()
            self.copy(C_OWN, "c", origin, 0, 0, self.every).wait_send()
        self.line.finish()
        self.local.wait()


def column_ids(width):
    return lax.broadcasted_iota(jnp.int32, (1, width), 1)


def unit_rows(values):
    average = jnp.mean(values, axis=-1, keepdims=True)
    centred = values - average
    variance = jnp.mean(centred * centred, axis=-1, keepdims=True)
    scale = lax.rsqrt(variance + eps_norm)
    return centred * scale, scale


def dot_plain(left, right):
    return lax.dot_general(left, right, (((1,), (0,)), ((), ())), preferred_element_type=f32)


def dot_turned(left, right):
    return lax.dot_general(left, right, (((1,), (1,)), ((), ())), preferred_element_type=f32)


def remote(src, dst, send, recv, peer):
    copy = pltpu.make_async_remote_copy(
        src_ref=src, dst_ref=dst, send_sem=send, recv_sem=recv, device_id=peer, device_id_type=MESH
    )
    copy.start()
    return copy


def z_line(place, every, send, recv):
    return Line(place, lambda origin: every.at[origin], send, recv)


class Stream:
    def __init__(self, slots, sems, sources):
        self.slots, self.sems, self.sources = slots, sems, sources
        self.started = 0

    def ensure(self, upto):
        while self.started <= upto and self.started < len(self.sources):
            at = self.started
            pltpu.make_async_copy(self.sources[at], self.slots.at[at % 2], self.sems.at[at % 2]).start()
            self.started += 1

    def take(self, at):
        self.ensure(at)
        pltpu.make_async_copy(self.sources[at], self.slots.at[at % 2], self.sems.at[at % 2]).wait()
        return self.slots.at[at % 2]


FORWARD_IN = 17
LAYER_SAVED = 6


def edges(head_cols):
    return 3 * head_cols // 128 * 128, -(-3 * head_cols // 128) * 128


def gelu(values):
    inner = math.sqrt(2.0 / math.pi) * (values + 0.044715 * values * values * values)
    return 0.5 * values * (1.0 + jnp.tanh(inner))


def window_bias(windows, put):
    for grid_row in range(GRID):
        shift = (GRID - 1 - grid_row) * GRID
        moved = windows if shift == 0 else pltpu.roll(windows, 512 - shift, 1)
        put(grid_row, moved[:, :PATCHES])


def forward_kernel(layers, *refs):
    units = 3 * layers
    refs = list(refs)

    def take(count):
        out = refs[:count]
        del refs[:count]
        return out

    (tokens, cot, pick, time_own, time_weight, windows_own, small_own, gains, shifts, out_bias) = take(10)
    pieces = take(units)
    wholes = take(units)
    saved = [take(LAYER_SAVED) for _ in range(layers)]
    block_out, grad_out, time_out, time_sel_out = take(4)
    (
        send, recv, z_send, z_recv, t_send, t_recv, save_sem, w_sem,
        w_slots, tok_all, cot_all, windows_all, small_all, time_all, share, share_y, share_x, share_c, share_z,
        x_buf, mid_buf, low_buf, acc_buf, s_buf, att_buf, act_buf, hid_buf, bias_buf, mixed_buf,
    ) = refs
    place = Place()
    place.greet()
    gather = [
        GatherUnit(place, pieces[u], wholes[u], send.at[u], recv.at[u], unit_cut(u, pieces[u].shape[0]))
        for u in range(units)
    ]
    state = set()
    tokens_n, d_model = tokens.shape
    head_cols = d_model // 4
    yp, xp, cp = ((place.wide(1, 0, 0), place.z), (place.wide(0, 1, 0), place.z), (place.wide(0, 0, 1), place.z))
    py, px, pc = place.y, place.x, place.c

    tok, win, small, cots, rz = (
        z_line(place, every, z_send.at[at], z_recv.at[at])
        for at, every in enumerate((tok_all, windows_all, small_all, cot_all, share_z))
    )
    kept = [
        pltpu.make_async_copy(src, every.at[place.z], save_sem.at[at])
        for at, (src, every) in enumerate(
            ((tokens, tok_all), (windows_own, windows_all), (small_own, small_all), (cot, cot_all))
        )
    ]
    given = {}

    def give(slot, src, dst, peer):
        given[slot] = remote(src, dst, t_send.at[slot], t_recv.at[slot], peer)

    def time_core():
        for copy in kept:
            copy.start()
        time_all[py, px, pc] = time_own[...]
        give(0, time_all.at[py, px, pc], time_all.at[py, px, pc], cp)

    def time_x():
        given[0].wait_recv()
        give(1, time_all.at[py, px], time_all.at[py, px], xp)

    def time_y():
        given[1].wait_recv()
        give(2, time_all.at[py], time_all.at[py], yp)

    def time_share():
        given[2].wait_recv()
        rows = time_all[...].reshape(128, d_model)
        cut = time_weight.shape[1]
        at_row = lax.broadcasted_iota(jnp.int32, (d_model, cut), 0)
        at_col = lax.broadcasted_iota(jnp.int32, (d_model, cut), 1)
        select = (at_row == at_col + place.wide() * cut).astype(bf16)
        picked = dot_plain(rows, select).astype(bf16)
        time_sel_out[...] = picked
        time_out[...] = rows
        for layer in range(layers):
            part = dot_plain(picked, time_weight[layer]).reshape(2, 2, 2, 16, d_model)
            share[:, :, :, layer] = part[:, :, :, :8]
        give(3, share.at[1 - py], share_y, yp)

    def share_step_x():
        given[3].wait_recv()
        share[py] = share[py] + share_y[...]
        give(4, share.at[py, 1 - px], share_x, xp)

    def share_step_c():
        given[4].wait_recv()
        share[py, px] = share[py, px] + share_x[...]
        give(5, share.at[py, px, 1 - pc], share_c, cp)

    def share_step_z():
        given[5].wait_recv()
        share[py, px, pc] = share[py, px, pc] + share_c[...]
        share_z[place.z] = share[py, px, pc]
        rz.begin(share_z.at[place.z])
        for slot in range(6):
            given[slot].wait_send()

    def line_steps(line, own, start, pace):
        steps = [(start, functools.partial(line.begin, own))]
        steps += [(start + pace * far, functools.partial(line.arrive, far)) for far in (1, 2, 3)]
        return steps + [(start + 3 * pace + 4.0, line.finish)]

    def mark(key):
        if key == "rows":
            for copy in kept:
                copy.wait()
        state.add(key)

    events = [
        (0.1, time_core),
        (3.0, time_x),
        (7.0, time_y),
        (11.0, time_share),
        (18.0, share_step_x),
        (24.0, share_step_c),
        (28.0, share_step_z),
    ]
    events += line_steps(small, small_own, 0.2, 5.0)
    events += [(28.0 + 8.0 * far, functools.partial(rz.arrive, far)) for far in (1, 2, 3)] + [(56.0, rz.finish)]
    events += line_steps(win, windows_own, 34.0, 10.0)
    events += line_steps(tok, tokens, 36.0, 14.0)
    events += [(84.0, functools.partial(mark, "rows"))]
    events += line_steps(cots, cot, 130.0, 16.0)
    for at, unit in enumerate(gather):
        events += unit.steps(UNIT_TIME * at)
        events.append((UNIT_TIME * at + 56.5, functools.partial(mark, at)))

    stream = Stream(w_slots, w_sem, [wholes[u].at[z] for u in range(units) for z in range(4)])
    pending = {}

    def save(slot, src, dst):
        copy = pltpu.make_async_copy(src, dst, save_sem.at[slot])
        copy.start()
        pending[slot] = copy

    def settle(slot):
        if slot in pending:
            pending.pop(slot).wait()

    def weights(unit, z):
        at = unit * 4 + z
        stream.ensure(at)
        if (at + 1) // 4 in state:
            stream.ensure(at + 1)
        return stream.take(at)

    def compute_steps():
        columns = column_ids(d_model)
        out_start, qkv_end = edges(head_cols)
        for layer in range(layers):
            x_save, mid_save, s_save, att_save, hid_save, act_save = saved[layer]
            row = 2 * layer
            yield (3 * layer if layer else "rows"), 2.0
            if layer == 0:
                total = dot_plain(pick[:, 0:tokens_n], tok_all[0])
                for z in range(1, 4):
                    total = total + dot_plain(pick[:, z * tokens_n : (z + 1) * tokens_n], tok_all[z])
                x_buf[...] = total
            settle(4)
            settle(5)
            save(4, x_buf, x_save)
            unit, _ = unit_rows(x_buf[...])
            low_buf[...] = (unit * gains[row : row + 1, :] + shifts[row : row + 1, :]).astype(bf16)
            settle(6)
            for z in range(4):
                yield 3 * layer, 2.0
                w = weights(3 * layer, z)
                share_rows = share_z[z, layer]
                at_image = lax.broadcasted_iota(jnp.int32, share_rows.shape, 0) == place.z
                offset = jnp.sum(jnp.where(at_image, share_rows, 0.0), axis=0, keepdims=True)
                offset = offset + small_all[z, 2 + layer : 3 + layer, :]
                spatial = dot_plain(low_buf[...], w[:, :qkv_end]) + offset[:, :qkv_end]
                s_buf[z, :, :qkv_end] = spatial.astype(bf16)
                yield 3 * layer, 2.0
                q = s_buf[z, :, 0:head_cols]
                k = s_buf[z, :, head_cols : 2 * head_cols]
                v = s_buf[z, :, 2 * head_cols : 3 * head_cols]
                head_of = column_ids(head_cols) // HEAD_DIM
                slot = z % 2
                settle(8 + slot)

                def one_head(head, carry):
                    here = head_of == head

                    def put(grid_row, block):
                        bias_buf[grid_row * GRID : (grid_row + 1) * GRID, :] = block

                    first_row = pl.multiple_of(head * GRID, GRID)
                    window_bias(windows_all[z, layer, pl.ds(first_row, GRID), :], put)
                    scores = dot_turned(jnp.where(here, q, 0), k)
                    scores = scores * HEAD_DIM ** (-0.5) + bias_buf[...]
                    top = jnp.max(scores, axis=-1, keepdims=True)
                    exponent = jnp.exp(scores - top)
                    attention = exponent / jnp.sum(exponent, axis=-1, keepdims=True)
                    att_buf[slot, head] = attention
                    mixed_buf[...] += dot_plain(attention.astype(bf16), jnp.where(here, v, 0))
                    return carry

                mixed_buf[...] = jnp.zeros_like(mixed_buf)
                for pair in range(2):
                    lax.fori_loop(2 * pair, 2 * pair + 2, one_head, 0)
                    yield 3 * layer, 2.0
                save(8 + slot, att_buf.at[slot], att_save.at[z])
                s_buf[z, :, 3 * head_cols :] = mixed_buf[...].astype(bf16)
                heads = jnp.where(columns[:, out_start:] >= 3 * head_cols, s_buf[z, :, out_start:], 0)
                branch = dot_turned(heads, w[:, out_start:])
                acc_buf[...] = branch if z == 0 else acc_buf[...] + branch
            save(6, s_buf, s_save)
            settle(4)
            mid_buf[...] = x_buf[...] + (acc_buf[...] + out_bias[row : row + 1, :])
            save(5, mid_buf, mid_save)
            unit, _ = unit_rows(mid_buf[...])
            low_buf[...] = (unit * gains[row + 1 : row + 2, :] + shifts[row + 1 : row + 2, :]).astype(bf16)
            settle(7)
            for z in range(4):
                yield 3 * layer + 1, 2.5
                w = weights(3 * layer + 1, z)
                slot = z % 2
                settle(10 + slot)
                hid_buf[slot] = dot_plain(low_buf[...], w[...]) + small_all[z, layer : layer + 1, :]
                save(10 + slot, hid_buf.at[slot], hid_save.at[z])
                act_buf[z] = gelu(hid_buf[slot]).astype(bf16)
            save(7, act_buf, act_save)
            for z in range(4):
                yield 3 * layer + 2, 1.8
                w = weights(3 * layer + 2, z)
                branch = dot_turned(act_buf[z], w[...])
                acc_buf[...] = branch if z == 0 else acc_buf[...] + branch
            x_buf[...] = mid_buf[...] + (acc_buf[...] + out_bias[row + 1 : row + 2, :])
        block_out[...] = x_buf[...].astype(bf16)
        total = dot_plain(pick[:, 0:tokens_n], cot_all[0])
        for z in range(1, 4):
            total = total + dot_plain(pick[:, z * tokens_n : (z + 1) * tokens_n], cot_all[z])
        grad_out[...] = total
        for slot in list(pending):
            settle(slot)

    interleave(events, compute_steps(), state)


def interleave(events, compute, state):
    events = sorted(events, key=lambda item: item[0])
    clock = 0.0
    wanted = next(compute)
    while wanted is not None or events:
        if events and (events[0][0] <= clock or wanted is None or wanted[0] not in state):
            at, step = events.pop(0)
            clock = max(clock, at)
            step()
            continue
        clock += wanted[1]
        wanted = next(compute, None)


def forward_all(tokens, cot, pick, time_own, time_weight, windows_own, small_own, gains, shifts, out_bias, pieces):
    layers = len(pieces) // 3
    units = len(pieces)
    rows, d_model = tokens.shape
    piece_rows = pieces[0].shape[0]
    any_space = pl.BlockSpec(memory_space=pl.ANY)
    vmem = pl.BlockSpec(memory_space=pltpu.VMEM)
    layer_shapes = [
        ((rows, d_model), f32),
        ((rows, d_model), f32),
        ((4, rows, d_model), bf16),
        ((4, 4, rows, rows), f32),
        ((4, rows, d_model), f32),
        ((4, rows, d_model), bf16),
    ]
    out_shape = (
        [jax.ShapeDtypeStruct((4, 8 * piece_rows, d_model), bf16)] * units
        + [jax.ShapeDtypeStruct(*item) for item in layer_shapes] * layers
        + [
            jax.ShapeDtypeStruct((rows, d_model), bf16),
            jax.ShapeDtypeStruct((rows, d_model), f32),
            jax.ShapeDtypeStruct((128, d_model), bf16),
            jax.ShapeDtypeStruct((128, piece_rows), bf16),
        ]
    )
    share_tail = (layers, 8, d_model)
    scratch = [
        pltpu.SemaphoreType.DMA((units, GATHER_SEMS)),
        pltpu.SemaphoreType.DMA((units, GATHER_SEMS)),
        pltpu.SemaphoreType.DMA((5, LINE_SEMS)),
        pltpu.SemaphoreType.DMA((5, LINE_SEMS)),
        pltpu.SemaphoreType.DMA((6,)),
        pltpu.SemaphoreType.DMA((6,)),
        pltpu.SemaphoreType.DMA((12,)),
        pltpu.SemaphoreType.DMA((2,)),
        pltpu.VMEM((2, d_model, d_model), bf16),
        pltpu.VMEM((4, rows, d_model), bf16),
        pltpu.VMEM((4, rows, d_model), bf16),
        pltpu.VMEM((4,) + windows_own.shape, f32),
        pltpu.VMEM((4,) + small_own.shape, f32),
        pltpu.VMEM((2, 2, 2, 16, d_model), bf16),
        pltpu.VMEM((2, 2, 2) + share_tail, f32),
        pltpu.VMEM((2, 2) + share_tail, f32),
        pltpu.VMEM((2,) + share_tail, f32),
        pltpu.VMEM(share_tail, f32),
        pltpu.VMEM((4,) + share_tail, f32),
        pltpu.VMEM((rows, d_model), f32),
        pltpu.VMEM((rows, d_model), f32),
        pltpu.VMEM((rows, d_model), bf16),
        pltpu.VMEM((rows, d_model), f32),
        pltpu.VMEM((4, rows, d_model), bf16),
        pltpu.VMEM((2, 4, rows, rows), f32),
        pltpu.VMEM((4, rows, d_model), bf16),
        pltpu.VMEM((2, rows, d_model), f32),
        pltpu.VMEM((rows, rows), f32),
        pltpu.VMEM((rows, d_model // 4), f32),
    ]
    out = pl.pallas_call(
        functools.partial(forward_kernel, layers),
        out_shape=out_shape,
        in_specs=[any_space] * 2 + [vmem] * 8 + [any_space] * units,
        out_specs=[any_space] * (units + LAYER_SAVED * layers) + [vmem] * 4,
        scratch_shapes=scratch,
        compiler_params=pltpu.CompilerParams(
            collective_id=0, has_side_effects=True, vmem_limit_bytes=60 * 2**20
        ),
        name="forward_all",
    )(tokens, cot, pick, time_own, time_weight, windows_own, small_own, gains, shifts, out_bias, *pieces)
    wholes = out[:units]
    saved = [out[units + LAYER_SAVED * at : units + LAYER_SAVED * (at + 1)] for at in range(layers)]
    return wholes, saved, out[units + LAYER_SAVED * layers :]


def gelu_slope(values):
    factor = math.sqrt(2.0 / math.pi)
    square = values * values
    bend = jnp.tanh(factor * (values + 0.044715 * square * values))
    return 0.5 * (1.0 + bend) + 0.5 * values * (1.0 - bend * bend) * factor * (1.0 + 3 * 0.044715 * square)


def dot_rows(left, right):
    return lax.dot_general(left, right, (((0,), (0,)), ((), ())), preferred_element_type=f32)


def norm_back(grad, unit, scale, norm_gain):
    weighted = grad * norm_gain
    first = jnp.mean(weighted, axis=-1, keepdims=True)
    second = jnp.mean(weighted * unit, axis=-1, keepdims=True)
    return scale * (weighted - first - unit * second)


def column_sums(values):
    return jnp.sum(values, axis=0, keepdims=True)


def fold_window(grads):
    total = None
    empty = jnp.zeros((GRID, 512 - PATCHES), f32)
    for grid_row in range(GRID):
        wide = jnp.concatenate([grads[grid_row * GRID : (grid_row + 1) * GRID, :], empty], axis=1)
        shift = (GRID - 1 - grid_row) * GRID
        moved = wide if shift == 0 else pltpu.roll(wide, shift, 1)
        total = moved if total is None else total + moved
    return total


SCATTER_SEMS = 23


def add_into(total, part):
    total[...] = total[...] + part[...]


class ScatterUnit:
    def __init__(self, place, out, total, far, near, from_z, send, recv, cut):
        self.place, self.out = place, out
        self.total, self.far, self.near, self.from_z = total, far, near, from_z
        self.send, self.recv = send, recv
        self.rows, self.cut = total.shape[3], cut
        self.first, self.last = pl.ds(0, cut), pl.ds(cut, self.rows - cut)
        self.copies, self.unsent, self.closed = {}, set(), set()

    def put(self, slot, peer, src, dst):
        self.copies[slot] = remote(src, dst, self.send.at[slot], self.recv.at[slot], peer)
        self.unsent.add(slot)

    def settle(self, slots):
        for slot in sorted(self.unsent.intersection(slots)):
            self.copies[slot].wait_send()
            self.unsent.remove(slot)

    def first_stage(self, k):
        p = self.place
        self.put(4 + k, (p.wide(0, 1), p.z), self.total.at[k, :, 1 - p.x, self.first], self.far.at[k, :, self.first])
        self.put(8 + k, (p.wide(1, 0), p.z), self.total.at[k, 1 - p.y, :, self.last], self.far.at[k, :, self.last])

    def second_stage(self, k):
        p = self.place
        self.copies[4 + k].wait_recv()
        for block in range(2):
            add_into(self.total.at[k, block, p.x, self.first], self.far.at[k, block, self.first])
        self.put(12 + k, (p.wide(1, 0), p.z), self.total.at[k, 1 - p.y, p.x, self.first], self.near.at[k, self.first])
        self.copies[8 + k].wait_recv()
        for block in range(2):
            add_into(self.total.at[k, p.y, block, self.last], self.far.at[k, block, self.last])
        self.put(16 + k, (p.wide(0, 1), p.z), self.total.at[k, p.y, 1 - p.x, self.last], self.near.at[k, self.last])

    def third_stage(self, k):
        p = self.place
        self.copies[12 + k].wait_recv()
        self.copies[16 + k].wait_recv()
        add_into(self.total.at[k, p.y, p.x], self.near.at[k])
        if k:
            self.put(19 + k, (p.wide(), p.along_z(k)), self.total.at[k, p.y, p.x], self.from_z.at[k - 1])
            self.closed.add(k)

    def finish(self):
        p = self.place
        for k in (1, 2, 3):
            self.copies[19 + k].wait_recv()
        both = self.total[0, p.y, p.x].astype(f32)
        for k in range(3):
            both = both + self.from_z[k].astype(f32)
        self.out[...] = both
        self.settle(list(self.copies))
        self.closed.add(0)


FAR_FIRST = (2, 1, 3, 0)


def scatter_step(unit, k, late):
    unit.second_stage(k)

    def third():
        unit.third_stage(k)
        if k == 0:
            return ((late, unit.finish),)

    return ((late, third),)


def backward_kernel(last_layer, *refs):
    refs = list(refs)

    def take(count):
        out = refs[:count]
        del refs[:count]
        return out

    (
        grad, mid_in, gains, shifts, trow_in, x_in, pick_in, time_weight, rows_in, s_all, att_all, hid_all, act_all,
        proj, up, down,
    ) = take(16)
    proj_out, up_out, down_out, grad_out, rows_out, row_sums, table_sums, time_sums, trow_out, rows_all = take(10)
    (
        total_a, total_b, far, near, from_z, right_a, right_b, left, turned,
        w_slots, s_slots, att_slots, hid_slots, acc_buf, low_buf, head_grads,
        row_parts, rows_z, rows_w, table_parts, table_z, table_w, trow_z, small_send, small_recv,
        send, recv, left_send, left_recv, line_send, line_recv, w_sem, s_sem, att_sem, hid_sem, load_sem, credit,
    ) = refs
    place = Place()
    place.greet()
    rows, d_model = grad.shape
    cut = down_out.shape[0]
    head_cols = d_model // 4
    core = (place.wide(0, 0, 1), place.z)
    zs = {k: place.along_z(k) for k in range(4)}
    columns = column_ids(d_model)
    out_start, qkv_end = edges(head_cols)
    units = {
        name: ScatterUnit(
            place, out, total, far.at[at], near.at[at], from_z.at[at], send.at[at], recv.at[at], unit_cut(at, cut)
        )
        for at, (name, out, total) in enumerate(
            (("down", down_out, total_a), ("up", up_out, total_b), ("proj", proj_out, total_a))
        )
    }
    line = z_line(place, rows_all, line_send, line_recv)

    right_copies = {}

    def give_right(name, at, k, src, buffer):
        right_copies[name, k] = remote(
            src, buffer.at[zs[k], pl.ds(rows, rows)], send.at[at, k], recv.at[at, k], core
        )

    left_copies = {}

    def make_left(at, values):
        if at > 1:
            for copy in left_copies[at - 2]:
                copy.wait_send()
        flipped = turned.at[at % 2]
        flipped[...] = values.T
        copies = []
        for block in range(4):
            mine = pl.multiple_of((2 * block + place.c) * cut, 16)
            other = pl.multiple_of((2 * block + 1 - place.c) * cut, 16)
            here = pl.ds(block * cut, cut)
            copies.append(
                remote(
                    flipped.at[pl.ds(other, cut)], left.at[at, here, pl.ds(rows, rows)],
                    left_send.at[at, block], left_recv.at[at, block], core,
                )
            )
            left[at, here, 0:rows] = flipped[pl.ds(mine, cut), :]
        left_copies[at] = copies

    def left_ready(at):
        for copy in left_copies[at]:
            copy.wait_recv()

    loads, keep = [], []
    if last_layer:
        line.begin(rows_in)
        keep.append(pltpu.make_async_copy(rows_in, rows_all.at[place.z], load_sem.at[4]))
        keep[0].start()
    for k in FAR_FIRST:
        give_right("down", 0, k, act_all.at[zs[k]], right_a)
        load = pltpu.make_async_copy(act_all.at[zs[k]], right_a.at[zs[k], pl.ds(0, rows)], load_sem.at[k])
        load.start()
        loads.append((k, load))
    w_sources = []
    for k in FAR_FIRST:
        w_sources += [down.at[zs[k]], up.at[zs[k]]]
    w_sources += [proj.at[zs[k]] for k in FAR_FIRST]
    weights = Stream(w_slots, w_sem, w_sources)
    hidden = Stream(hid_slots, hid_sem, [hid_all.at[zs[k]] for k in FAR_FIRST])
    saved = Stream(s_slots, s_sem, [s_all.at[zs[k]] for k in FAR_FIRST])
    attentions = Stream(att_slots, att_sem, [att_all.at[zs[k]] for k in FAR_FIRST])
    for stream in (weights, hidden, saved, attentions):
        stream.ensure(1)

    def weight_grad(name, k, buffer, *lefts):
        unit = units[name]
        if len(lefts) == 1:
            ranges = [(0, d_model, dot_plain(left[lefts[0]], buffer[zs[k]]))]
        else:
            first = dot_plain(left[lefts[0]], buffer[zs[k], :, 0:qkv_end])
            last = dot_plain(left[lefts[1]], buffer[zs[k], :, out_start:])
            edge = jnp.where(
                columns[:, out_start:qkv_end] < 3 * head_cols, first[:, out_start:], last[:, : qkv_end - out_start]
            )
            ranges = [
                (0, out_start, first[:, :out_start]), (out_start, qkv_end, edge),
                (qkv_end, d_model, last[:, qkv_end - out_start :]),
            ]
        for start, stop, part in ranges:
            low = part.astype(bf16)
            for block in range(4):
                unit.total[k, block // 2, block % 2, :, start:stop] = low[block * cut : (block + 1) * cut]

    late = {}

    def late_load(src, dst, slot):
        late[slot] = pltpu.make_async_copy(src, dst, load_sem.at[slot])
        late[slot].start()

    def late_wait(slot):
        late[slot].wait()

    def put_row(row, values):
        for z in range(4):
            row_parts[z, row : row + 1, :] = values

    small = {}
    axes = ((core, 6), ((place.wide(0, 1, 0), place.z), 9), ((place.wide(1, 0, 0), place.z), 12))
    own_time = (
        time_sums.at[place.y, place.x, place.c], time_sums.at[place.y, place.x], time_sums.at[place.y]
    )
    own_trow = (trow_out.at[place.y, place.x, place.c], trow_out.at[place.y, place.x], trow_out.at[place.y])

    def give(slot, src, dst, peer):
        small[slot] = remote(src, dst, small_send.at[slot], small_recv.at[slot], peer)

    def small_begin():
        for k in (1, 2, 3):
            peer = (place.wide(), zs[k])
            give(k - 1, row_parts.at[zs[k]], rows_z.at[k - 1], peer)
            give(k + 2, table_parts.at[zs[k]], table_z.at[k - 1], peer)
        return ((9.0, small_along_z),)

    def small_along_z():
        for slot in range(6):
            small[slot].wait_recv()
        totals = row_parts[place.z]
        at_row = lax.broadcasted_iota(jnp.int32, (16, d_model), 0)
        times = jnp.where(at_row == place.z, totals[7:8, :], 0.0)
        tables = table_parts[place.z]
        for k in (1, 2, 3):
            part = rows_z[k - 1]
            times = jnp.where(at_row == place.along_z(4 - k), part[7:8, :], times)
            totals = totals + part
            tables = tables + table_z[k - 1]
        row_sums[...] = totals
        table_sums[...] = tables
        time_sums[place.y, place.x, place.c] = times.astype(bf16)
        small_across(0)
        return ((4.0, functools.partial(small_step, 0)),)

    def small_across(axis):
        peer, slot = axes[axis]
        give(slot, row_sums, rows_w.at[axis], peer)
        give(slot + 1, table_sums, table_w.at[axis], peer)
        give(slot + 2, own_time[axis], own_time[axis], peer)

    def small_step(axis):
        slot = axes[axis][1]
        for at in range(slot, slot + 3):
            small[at].wait_recv()
            small[at].wait_send()
        row_sums[...] = row_sums[...] + rows_w[axis]
        table_sums[...] = table_sums[...] + table_w[axis]
        if axis < 2:
            small_across(axis + 1)
            return ((5.0, functools.partial(small_step, axis + 1)),)
        late_wait(6)
        times = jnp.where(columns < 3 * head_cols, time_sums[...].reshape(128, d_model), 0)
        part = dot_turned(times, s_slots[0, 0:cut]).reshape(8, 16, cut)[:, :8]
        part = part + trow_in[...]
        trow_out[place.y, place.x, place.c] = part
        if last_layer:
            return None
        for k in (1, 2, 3):
            give(14 + k, own_trow[0], trow_z.at[k - 1], (place.wide(), zs[k]))
        return ((6.0, trow_along_z),)

    def trow_along_z():
        for slot in (15, 16, 17):
            small[slot].wait_recv()
            small[slot].wait_send()
        here = trow_out[place.y, place.x, place.c] + trow_z[0] + trow_z[1] + trow_z[2]
        trow_out[place.y, place.x, place.c] = here
        give(18, own_trow[0], own_trow[0], axes[0][0])
        return ((4.0, functools.partial(trow_step, 0)),)

    def trow_step(axis):
        small[18 + axis].wait_recv()
        small[18 + axis].wait_send()
        if axis < 2:
            give(19 + axis, own_trow[axis + 1], own_trow[axis + 1], axes[axis + 1][0])
            return ((5.0, functools.partial(trow_step, axis + 1)),)

    def compute():
        low_buf[0] = grad[...].astype(bf16)
        put_row(5, column_sums(low_buf[0].astype(f32)))
        make_left(0, low_buf[0])
        left_ready(0)
        for at, k in enumerate(FAR_FIRST):
            loads[at][1].wait()
            right_copies["down", k].wait_recv()
            weight_grad("down", k, right_a, 0)
            yield 1.8, [(units["down"], k)]
            w = weights.take(2 * at)
            hid = hidden.take(at)
            act_grad = dot_plain(low_buf[0], w[...])
            hid_grad = (act_grad * gelu_slope(hid[...])).astype(bf16)
            right_b[zs[k], 0:rows] = hid_grad
            weights.ensure(2 * at + 2)
            hidden.ensure(at + 2)
            give_right("up", 1, k, right_b.at[zs[k], pl.ds(0, rows)], right_b)
            row_parts[zs[k], 6:7, :] = column_sums(hid_grad.astype(f32))
            yield 2.5, []
            w = weights.take(2 * at + 1)
            part = dot_turned(right_b[zs[k], 0:rows], w[...])
            acc_buf[...] = part if at == 0 else acc_buf[...] + part
            weights.ensure(2 * at + 3)
            yield 1.5, []
        for k in FAR_FIRST:
            right_copies["down", k].wait_send()
        pl.semaphore_signal(credit, inc=1, device_id=core, device_id_type=MESH)
        unit, scale = unit_rows(mid_in[...])
        make_left(1, (unit * gains[1:2, :] + shifts[1:2, :]).astype(bf16))
        from_norm = norm_back(acc_buf[...], unit, scale, gains[1:2, :])
        put_row(1, column_sums(acc_buf[...] * unit))
        put_row(3, column_sums(acc_buf[...]))
        grad_out[...] = grad[...] + from_norm
        low_buf[0] = grad_out[...].astype(bf16)
        put_row(4, column_sums(low_buf[0].astype(f32)))
        late_load(x_in, hid_slots.at[0], 5)
        yield 4.0, []
        left_ready(1)
        right_copies["up", FAR_FIRST[0]].wait_recv()
        weight_grad("up", FAR_FIRST[0], right_b, 1)
        yield 1.5, [(units["up"], FAR_FIRST[0])]
        make_left(2, low_buf[0])
        late_wait(5)
        unit, scale = unit_rows(hid_slots[0])
        make_left(3, (unit * gains[0:1, :] + shifts[0:1, :]).astype(bf16))
        left_ready(2)
        left_ready(3)
        pl.semaphore_wait(credit, 1)
        yield 4.0, []
        head_of = column_ids(head_cols) // HEAD_DIM
        score_scale = HEAD_DIM ** (-0.5)
        for at, k in enumerate(FAR_FIRST):
            if at:
                right_copies["up", k].wait_recv()
                weight_grad("up", k, right_b, 1)
                yield 1.5, [(units["up"], k)]
            w = weights.take(8 + at)
            s = saved.take(at)
            attention_slot = attentions.take(at)
            low_buf[1, :, out_start:] = dot_plain(low_buf[0], w[:, out_start:]).astype(bf16)
            mixed_grad = low_buf[1, :, 3 * head_cols :]
            q = s[:, 0:head_cols]
            key = s[:, head_cols : 2 * head_cols]
            v = s[:, 2 * head_cols : 3 * head_cols]
            head_grads[...] = jnp.zeros_like(head_grads)

            def one_head(head, carry):
                here = head_of == head
                attention = attention_slot[head]
                own_grad = jnp.where(here, mixed_grad, 0)
                dot_back = dot_turned(own_grad, v)
                both = attention * dot_back
                score_low = (both - attention * jnp.sum(both, axis=-1, keepdims=True)).astype(bf16)
                first_row = pl.multiple_of(head * GRID, GRID)
                table_parts[zs[k], pl.ds(first_row, GRID), :] = fold_window(score_low.astype(f32))
                head_grads[0] += dot_plain(score_low, jnp.where(here, key, 0))
                head_grads[1] += dot_rows(score_low, jnp.where(here, q, 0))
                head_grads[2] += dot_rows(attention.astype(bf16), own_grad)
                return carry

            lax.fori_loop(0, 2, one_head, 0)
            yield 2.5, []
            lax.fori_loop(2, 4, one_head, 0)
            here = right_a.at[zs[k]]
            here[0:rows, 0:head_cols] = (head_grads[0] * score_scale).astype(bf16)
            here[0:rows, head_cols : 2 * head_cols] = (head_grads[1] * score_scale).astype(bf16)
            here[0:rows, 2 * head_cols : 3 * head_cols] = head_grads[2].astype(bf16)
            here[0:rows, 3 * head_cols :] = s[:, 3 * head_cols :]
            give_right("proj", 2, k, right_a.at[zs[k], pl.ds(0, rows)], right_a)
            saved.ensure(at + 2)
            attentions.ensure(at + 2)
            yield 2.5, []
            own = right_a[zs[k], 0:rows]
            row_parts[zs[k], 7:8, :] = column_sums(own.astype(f32))
            own = jnp.where(columns < 3 * head_cols, own, 0)
            part = dot_turned(own[:, :qkv_end], w[:, :qkv_end])
            acc_buf[...] = part if at == 0 else acc_buf[...] + part
            weights.ensure(8 + at + 2)
            yield 1.5, []
        for k in FAR_FIRST:
            right_copies["proj", k].wait_recv()
            yield 0.2, [], (units["down"], k)
            units["down"].settle((4 + k, 8 + k, 12 + k, 16 + k, 19 + k))
            weight_grad("proj", k, right_a, 3, 2)
            yield 2.0, [(units["proj"], k)]
        unit, scale = unit_rows(hid_slots[0])
        from_norm = norm_back(acc_buf[...], unit, scale, gains[0:1, :])
        put_row(0, column_sums(acc_buf[...] * unit))
        put_row(2, column_sums(acc_buf[...]))
        grad_out[...] = grad_out[...] + from_norm
        late_load(time_weight, s_slots.at[0, pl.ds(0, cut)], 6)
        late_load(pick_in, s_slots.at[1, :, pl.ds(0, 4 * rows)], 7)
        following = [(0.0, small_begin)]
        if not last_layer:
            low_buf[0] = grad_out[...].astype(bf16)
            line.begin(low_buf.at[0])
            keep.append(pltpu.make_async_copy(low_buf.at[0], rows_all.at[place.z], load_sem.at[4]))
            keep[0].start()
            following += [(14.0 * far_off, functools.partial(line.arrive, far_off)) for far_off in (1, 2, 3)]
        yield 2.0, [], None, following

    first_events = []
    if last_layer:
        first_events = [(20.0 * far_off, functools.partial(line.arrive, far_off)) for far_off in (1, 2, 3)]
    merge_steps(compute(), first_events, 10.7, 12.0)
    for slot in range(6):
        small[slot].wait_send()
    for (name, k), copy in right_copies.items():
        if name != "down":
            copy.wait_send()
    for at in (2, 3):
        for copy in left_copies[at]:
            copy.wait_send()
    line.finish()
    keep[0].wait()
    gathered = pltpu.make_async_copy(rows_all, right_b.at[:, pl.ds(0, rows)], load_sem.at[4])
    gathered.start()
    gathered.wait()
    late_wait(7)
    total = dot_plain(s_slots[1, :, 0:rows], right_b[0, 0:rows])
    for z in range(1, 4):
        total = total + dot_plain(s_slots[1, :, z * rows : (z + 1) * rows], right_b[z, 0:rows])
    rows_out[...] = total.astype(bf16)


def merge_steps(compute, events, links, late):
    clock, link_free = 0.0, 0.0
    events = list(events)

    def run_first():
        events.sort(key=lambda item: item[0])
        at, step = events.pop(0)
        for delay, following in step() or ():
            events.append((max(clock, at) + delay, following))
        return max(clock, at)

    while True:
        while events and min(item[0] for item in events) <= clock:
            clock = run_first()
        made = next(compute, None)
        if made is None:
            break
        clock += made[0]
        for unit, k in made[1]:
            unit.first_stage(k)
            start = max(clock, link_free)
            link_free = start + links
            events.append((start + late, functools.partial(scatter_step, unit, k, late)))
        if len(made) > 2 and made[2]:
            unit, k = made[2]
            while k not in unit.closed:
                clock = run_first()
        if len(made) > 3:
            events += [(clock + delay, step) for delay, step in made[3]]
    while events:
        clock = run_first()


def backward_layer(last_layer, grad, saved, gains, shifts, trow, pick, time_weight, rows_in, weights):
    x_in, mid_in, s_all, att_all, hid_all, act_all = saved
    proj, up, down = weights
    rows, d_model = grad.shape
    cut = d_model // 8
    any_space = pl.BlockSpec(memory_space=pl.ANY)
    vmem = pl.BlockSpec(memory_space=pltpu.VMEM)
    block = jax.ShapeDtypeStruct((cut, d_model), f32)
    out_shape = [
        block,
        block,
        block,
        jax.ShapeDtypeStruct((rows, d_model), f32),
        jax.ShapeDtypeStruct((rows, d_model), bf16),
        jax.ShapeDtypeStruct((8, d_model), f32),
        jax.ShapeDtypeStruct((4 * GRID, 512), f32),
        jax.ShapeDtypeStruct((2, 2, 2, 16, d_model), bf16),
        jax.ShapeDtypeStruct((2, 2, 2, 8, 8, cut), f32),
        jax.ShapeDtypeStruct((4, rows, d_model), bf16),
    ]
    dma = pltpu.SemaphoreType.DMA
    scratch = [
        pltpu.VMEM((4, 2, 2, cut, d_model), bf16),
        pltpu.VMEM((4, 2, 2, cut, d_model), bf16),
        pltpu.VMEM((3, 4, 2, cut, d_model), bf16),
        pltpu.VMEM((3, 4, cut, d_model), bf16),
        pltpu.VMEM((3, 3, cut, d_model), bf16),
        pltpu.VMEM((4, 2 * rows, d_model), bf16),
        pltpu.VMEM((4, 2 * rows, d_model), bf16),
        pltpu.VMEM((4, 4 * cut, 2 * rows), bf16),
        pltpu.VMEM((2, d_model, rows), bf16),
        pltpu.VMEM((2, d_model, d_model), bf16),
        pltpu.VMEM((2, rows, d_model), bf16),
        pltpu.VMEM((2, 4, rows, rows), f32),
        pltpu.VMEM((2, rows, d_model), f32),
        pltpu.VMEM((rows, d_model), f32),
        pltpu.VMEM((2, rows, d_model), bf16),
        pltpu.VMEM((3, rows, d_model // 4), f32),
        pltpu.VMEM((4, 8, d_model), f32),
        pltpu.VMEM((3, 8, d_model), f32),
        pltpu.VMEM((3, 8, d_model), f32),
        pltpu.VMEM((4, 4 * GRID, 512), f32),
        pltpu.VMEM((3, 4 * GRID, 512), f32),
        pltpu.VMEM((3, 4 * GRID, 512), f32),
        pltpu.VMEM((3, 8, 8, cut), f32),
        dma((21,)),
        dma((21,)),
        dma((3, SCATTER_SEMS)),
        dma((3, SCATTER_SEMS)),
        dma((4, 4)),
        dma((4, 4)),
        dma((LINE_SEMS,)),
        dma((LINE_SEMS,)),
        dma((2,)),
        dma((2,)),
        dma((2,)),
        dma((2,)),
        dma((8,)),
        pltpu.SemaphoreType.REGULAR,
    ]
    return pl.pallas_call(
        functools.partial(backward_kernel, last_layer),
        out_shape=out_shape,
        in_specs=[vmem] * 5 + [any_space] * 11,
        out_specs=[vmem] * 9 + [any_space],
        scratch_shapes=scratch,
        compiler_params=pltpu.CompilerParams(
            collective_id=1 if last_layer else 2, has_side_effects=True, vmem_limit_bytes=63 * 2**20
        ),
        name="backward_last" if last_layer else "backward_first",
    )(
        grad, mid_in, gains, shifts, trow, x_in, pick, time_weight, rows_in, s_all, att_all, hid_all, act_all,
        proj, up, down,
    )


def shards_plain(
    tokens,
    cotangent,
    segment_ids,
    patch_pos,
    time_index,
    time_table,
    norm_gain,
    norm_shift,
    attn_weight,
    out_weight,
    qkv_bias,
    out_bias,
    mlp_weight,
    up_bias,
    rel_table,
):
    image_count = time_index.shape[0]
    layer_count = attn_weight.shape[0]
    narrow_at = lax.axis_index("narrow")
    wide_at = lax.axis_index("wide")
    wide_size = lax.axis_size("wide")
    own_rows = tokens.shape[0]
    in_rows, cols = attn_weight.shape[2:]
    image_local = segment_ids % image_count
    grid_slot = image_local * PATCHES + patch_pos
    own_slots = narrow_at * own_rows + jnp.arange(own_rows, dtype=jnp.int32)
    pick_in = (own_slots[:, None] == grid_slot[None, :]).astype(bf16)
    own_grid = lax.dynamic_slice_in_dim(grid_slot, narrow_at * own_rows, own_rows)
    pick_out = (own_grid[:, None] == jnp.arange(grid_slot.shape[0], dtype=jnp.int32)[None, :]).astype(bf16)

    def to_images(rows):
        every = lax.all_gather(rows, "narrow", axis=0, tiled=True)
        return jnp.dot(pick_in, every, preferred_element_type=f32)

    def to_rows(rows):
        every = lax.all_gather(rows, "narrow", axis=0, tiled=True)
        return jnp.dot(pick_out, every, preferred_element_type=f32).astype(bf16)

    steps_all = lax.all_gather(time_index, "wide", axis=0, tiled=True)
    step_hot = (steps_all[:, None] == jnp.arange(time_table.shape[0], dtype=jnp.int32)[None, :]).astype(bf16)
    time_rows = jnp.dot(step_hot, time_table, preferred_element_type=f32).astype(bf16)
    time_slice = lax.dynamic_slice_in_dim(time_rows, wide_at * in_rows, in_rows, axis=1)
    time_weight = attn_weight[:, 3:6]
    time_share = jnp.einsum("id,ljdc->ljic", time_slice, time_weight, preferred_element_type=f32)
    time_share = lax.psum_scatter(time_share, "wide", scatter_dimension=2, tiled=True)
    time_share = lax.all_gather(time_share, "narrow", axis=3, tiled=True)
    time_part = lax.dynamic_index_in_dim(time_share, narrow_at, axis=2, keepdims=False)

    tables = lax.all_gather(rel_table, "narrow", axis=1, tiled=True)
    qkv_bias_all = lax.all_gather(qkv_bias, "narrow", axis=2, tiled=True)
    up_bias_all = lax.all_gather(up_bias, "narrow", axis=1, tiled=True)

    def layer_params(at):
        return (norm_gain[at], norm_shift[at], qkv_bias_all[at], out_bias[at])

    weights = []
    for at in range(layer_count):
        packed = jnp.concatenate([attn_weight[at, 0], attn_weight[at, 1], attn_weight[at, 2], out_weight[at]], axis=1)
        weights.append((gather_unit(packed), gather_unit(mlp_weight[at, 0]), gather_unit(mlp_weight[at, 1])))

    residual = to_images(tokens)
    kept = []
    for at in range(layer_count):
        pairs = pair_bias(tables[at])
        middle, attn_saved = attention_forward(residual, weights[at][0], time_part[at], layer_params(at), pairs)
        residual, mlp_saved = mlp_forward(middle, weights[at][1], weights[at][2], layer_params(at), up_bias_all[at])
        kept.append((attn_saved, mlp_saved))
    block_output = to_rows(residual.astype(bf16))
    gradient = to_images(cotangent)
    attn_grads, out_grads, mlp_grads = [], [], []
    time_sums, small = [], []
    for at in reversed(range(layer_count)):
        attn_saved, mlp_saved = kept[at]
        grad_mid, up_grad, down_grad, mlp_small = mlp_backward(
            gradient, weights[at][1], weights[at][2], layer_params(at), mlp_saved
        )
        mlp_grads.insert(0, jnp.stack([scatter_unit(up_grad), scatter_unit(down_grad)]))
        gradient, proj_grad, sums, table_grad, attn_small = attention_backward(
            grad_mid, weights[at][0], layer_params(at), attn_saved
        )
        packed = scatter_unit(proj_grad)
        attn_grads.insert(0, jnp.stack([packed[:, j * cols : (j + 1) * cols] for j in range(3)]))
        out_grads.insert(0, packed[:, 3 * cols :])
        time_sums.insert(0, sums)
        small.insert(
            0,
            (
                jnp.stack([attn_small[0], mlp_small[0]]),
                jnp.stack([attn_small[1], mlp_small[1]]),
                jnp.stack([attn_small[2], mlp_small[2]]),
                jnp.stack([sums[0], sums[2]]),
                mlp_small[3],
                table_grad,
            ),
        )
    input_grad = to_rows(gradient.astype(bf16))

    def stacked(index_at):
        return jnp.stack([entry[index_at] for entry in small])

    totals = lax.psum(tuple(stacked(index_at) for index_at in range(6)), ("wide", "narrow"))

    def own_part(array, axis):
        size = array.shape[axis] // lax.axis_size("narrow")
        return lax.dynamic_slice_in_dim(array, narrow_at * size, size, axis=axis)

    time_low = jnp.stack(time_sums).astype(bf16)
    time_all = lax.all_gather(time_low, ("wide", "narrow"), axis=0, tiled=False)
    time_own = own_part(time_all, 3)
    time_weight_grad = jnp.einsum("id,iljc->ljdc", time_slice, time_own, preferred_element_type=f32)
    trow_share = jnp.einsum("iljc,ljdc->id", time_own, time_weight, preferred_element_type=f32)
    trow_share = lax.psum(trow_share, "narrow")
    trow = lax.all_gather(trow_share, "wide", axis=1, tiled=True)
    time_grad = jnp.einsum("is,id->sd", step_hot.astype(f32), trow, precision=highest)
    attn_grad = jnp.concatenate([jnp.stack(attn_grads).astype(f32), time_weight_grad], axis=1)
    return (
        block_output,
        input_grad,
        time_grad,
        totals[0],
        totals[1],
        attn_grad,
        jnp.stack(out_grads).astype(f32),
        own_part(totals[3], 2),
        totals[2],
        jnp.stack(mlp_grads).astype(f32),
        own_part(totals[4], 1),
        own_part(totals[5], 1),
    )


def bias_windows(tables):
    layers, heads = tables.shape[:2]
    near = jnp.arange(GRID, dtype=jnp.int32)
    span = jnp.arange(SPAN, dtype=jnp.int32)
    steps = (span[None, :, None] == near[:, None, None] - near[None, None, :] + (GRID - 1)).astype(f32)
    grid = tables.reshape(layers, heads, SPAN, SPAN)[:, :, ::-1]
    windows = jnp.einsum("lhab,xby->lhxay", grid, steps, precision=highest)
    windows = windows.reshape(layers, heads * GRID, SPAN * GRID)
    return jnp.pad(windows, ((0, 0), (0, 0), (0, 512 - SPAN * GRID)))


def fold_windows(windows):
    layers, heads = windows.shape[0], windows.shape[1] // GRID
    near = jnp.arange(GRID, dtype=jnp.int32)
    span = jnp.arange(SPAN, dtype=jnp.int32)
    steps = (span[None, :, None] == near[:, None, None] - near[None, None, :] + (GRID - 1)).astype(f32)
    grid = windows[:, :, : SPAN * GRID].reshape(layers, heads, GRID, SPAN, GRID)
    tables = jnp.einsum("lhxay,xby->lhab", grid, steps, precision=highest)
    return tables[:, :, ::-1].reshape(layers, heads, SPAN * SPAN)


def shards(
    tokens,
    cotangent,
    segment_ids,
    patch_pos,
    time_index,
    time_table,
    norm_gain,
    norm_shift,
    attn_weight,
    out_weight,
    qkv_bias,
    out_bias,
    mlp_weight,
    up_bias,
    rel_table,
):
    image_count = time_index.shape[0]
    layer_count = attn_weight.shape[0]
    in_rows, cols = attn_weight.shape[2:]
    by_links = lax.axis_size("wide") == 8 and lax.axis_size("narrow") == 4 and in_rows % 16 == 0
    if not by_links:
        return shards_plain(
            tokens, cotangent, segment_ids, patch_pos, time_index, time_table, norm_gain, norm_shift,
            attn_weight, out_weight, qkv_bias, out_bias, mlp_weight, up_bias, rel_table,
        )
    narrow_at = lax.axis_index("narrow")
    wide_at = lax.axis_index("wide")
    own_rows, d_model = tokens.shape
    image_local = segment_ids % image_count
    grid_slot = image_local * PATCHES + patch_pos
    own_slots = narrow_at * own_rows + jnp.arange(own_rows, dtype=jnp.int32)
    pick_in = (own_slots[:, None] == grid_slot[None, :]).astype(bf16)
    own_grid = lax.dynamic_slice_in_dim(grid_slot, narrow_at * own_rows, own_rows)
    pick_out = (own_grid[:, None] == jnp.arange(grid_slot.shape[0], dtype=jnp.int32)[None, :]).astype(bf16)

    step_own = (time_index[:, None] == jnp.arange(time_table.shape[0], dtype=jnp.int32)[None, :]).astype(bf16)
    time_own = jnp.dot(step_own, time_table, preferred_element_type=f32).astype(bf16)
    digits = jnp.stack([time_index // 32, time_index % 32]).astype(bf16)
    digits = jnp.pad(digits, ((0, 16 - image_count - 2), (0, d_model - image_count)))
    time_own = jnp.concatenate([time_own, digits], axis=0)
    time_weight = attn_weight[:, 3:6]
    time_packed = jnp.concatenate(
        [time_weight[:, 0], time_weight[:, 1], time_weight[:, 2], jnp.zeros_like(time_weight[:, 0])], axis=2
    )
    qkv_packed = jnp.concatenate(
        [qkv_bias[:, 0], jnp.zeros_like(qkv_bias[:, 0]), qkv_bias[:, 1], jnp.zeros_like(qkv_bias[:, 0])], axis=1
    )
    small_own = jnp.pad(jnp.concatenate([up_bias, qkv_packed], axis=0), ((0, 8 - 2 * layer_count), (0, 0)))
    pieces = []
    for at in range(layer_count):
        packed = jnp.concatenate([attn_weight[at, 0], attn_weight[at, 1], attn_weight[at, 2], out_weight[at]], axis=1)
        pieces += [packed, mlp_weight[at, 0], mlp_weight[at, 1]]
    wholes, saved, (block_low, gradient, time_all, time_sel) = forward_all(
        tokens,
        cotangent,
        pick_in,
        time_own,
        time_packed,
        bias_windows(rel_table),
        small_own,
        norm_gain.reshape(-1, d_model),
        norm_shift.reshape(-1, d_model),
        out_bias.reshape(-1, d_model),
        pieces,
    )
    time_all = time_all.reshape(8, 16, d_model)
    steps_all = time_all[:, image_count : image_count + 2, :image_count].astype(f32)
    steps_all = (steps_all[:, 0] * 32 + steps_all[:, 1]).astype(jnp.int32).reshape(-1)
    step_hot = (steps_all[:, None] == jnp.arange(time_table.shape[0], dtype=jnp.int32)[None, :]).astype(f32)
    time_slice = time_sel.reshape(8, 16, in_rows)[:, :image_count].reshape(-1, in_rows)

    attn_grads, out_grads, mlp_grads = [], [], []
    row_sums, table_sums, time_sums = [], [], []
    block_output = None
    trow = jnp.zeros((8, 8, in_rows), f32)
    for at in reversed(range(layer_count)):
        last_layer = at == layer_count - 1
        packed, up_part, down_part, gradient, moved, rows_part, tables_part, times_part, trow, _ = backward_layer(
            last_layer, gradient, saved[at], norm_gain[at], norm_shift[at], trow, pick_out, time_packed[at], block_low,
            wholes[3 * at : 3 * at + 3],
        )
        if last_layer:
            block_output = moved
            trow = lax.dynamic_index_in_dim(trow.reshape(8, 8, 8, in_rows), wide_at, axis=0, keepdims=False)
        mlp_grads.insert(0, jnp.stack([up_part, down_part]))
        attn_grads.insert(0, jnp.stack([packed[:, j * cols : (j + 1) * cols] for j in range(3)]))
        out_grads.insert(0, packed[:, 3 * cols :])
        row_sums.insert(0, rows_part)
        table_sums.insert(0, tables_part)
        time_sums.insert(0, times_part.reshape(8, 16, d_model)[:, :image_count].reshape(-1, d_model))
    input_grad = moved
    row_sums = jnp.stack(row_sums)
    table_grad = fold_windows(jnp.stack(table_sums))
    time_weight_grad = jnp.einsum("id,lic->ldc", time_slice, jnp.stack(time_sums), preferred_element_type=f32)
    time_weight_grad = jnp.stack([time_weight_grad[:, :, j * cols : (j + 1) * cols] for j in range(3)], axis=1)
    trow = trow.reshape(8, 8, 8, in_rows)[:, :, :image_count].transpose(1, 2, 0, 3).reshape(-1, d_model)
    time_grad = jnp.einsum("is,id->sd", step_hot, trow, precision=highest)
    attn_grad = jnp.concatenate([jnp.stack(attn_grads), time_weight_grad], axis=1)
    qkv_bias_grad = jnp.stack([row_sums[:, 7, :cols], row_sums[:, 7, 2 * cols : 3 * cols]], axis=1)
    return (
        block_output,
        input_grad,
        time_grad,
        row_sums[:, 0:2],
        row_sums[:, 2:4],
        attn_grad,
        jnp.stack(out_grads),
        qkv_bias_grad,
        row_sums[:, 4:6],
        jnp.stack(mlp_grads),
        row_sums[:, 6],
        table_grad,
    )


def solution(mesh):
    return jax.shard_map(
        shards,
        mesh=mesh,
        in_specs=(
            P(("wide", "narrow"), None),
            P(("wide", "narrow"), None),
            P("wide"),
            P("wide"),
            P("wide"),
            P(),
            P(),
            P(),
            P(None, None, "wide", "narrow"),
            P(None, "wide", "narrow"),
            P(None, None, "narrow"),
            P(),
            P(None, None, "wide", "narrow"),
            P(None, "narrow"),
            P(None, "narrow", None),
        ),
        out_specs=(
            P(("wide", "narrow"), None),
            P(("wide", "narrow"), None),
            P(),
            P(),
            P(),
            P(None, None, "wide", "narrow"),
            P(None, "wide", "narrow"),
            P(None, None, "narrow"),
            P(),
            P(None, None, "wide", "narrow"),
            P(None, "narrow"),
            P(None, "narrow", None),
        ),
        check_vma=False,
    )
```

```python
import functools
import math

import jax
import jax.numpy as jnp
from jax import lax
from jax.experimental import pallas as pl
from jax.experimental.pallas import tpu as pltpu
from jax.sharding import PartitionSpec as P

HEAD_DIM = 72
GRID = 16
PATCHES = GRID * GRID
SPAN = 2 * GRID - 1


eps_norm = 1e-06
highest = lax.Precision.HIGHEST
f32 = jnp.float32
bf16 = jnp.bfloat16
ROWS_AXES = ("narrow", "wide")
MESH = pl.DeviceIdType.MESH


def layer_norm(values, norm_gain, norm_shift):
    average = jnp.mean(values, axis=-1, keepdims=True)
    centred = values - average
    variance = jnp.mean(centred * centred, axis=-1, keepdims=True)
    scale = lax.rsqrt(variance + eps_norm)
    unit = centred * scale
    return unit * norm_gain + norm_shift, unit, scale


def layer_norm_back(grad, unit, scale, norm_gain):
    weighted = grad * norm_gain
    first = jnp.mean(weighted, axis=-1, keepdims=True)
    second = jnp.mean(weighted * unit, axis=-1, keepdims=True)
    from_norm = scale * (weighted - first - unit * second)
    return from_norm, jnp.sum(grad * unit, axis=0), jnp.sum(grad, axis=0)


def offset_onehot():
    near = jnp.arange(GRID, dtype=jnp.int32)
    span = jnp.arange(SPAN, dtype=jnp.int32)
    return (span[None, None, :] == near[:, None, None] - near[None, :, None] + (GRID - 1)).astype(f32)


def pair_bias(bias_table):
    steps_hot = offset_onehot()
    head_count = bias_table.shape[0]
    table_grid = bias_table.reshape(head_count, SPAN, SPAN)
    row_part = jnp.einsum("ixa,hab->hixb", steps_hot, table_grid, precision=highest)
    pairs = jnp.einsum("jyb,hixb->hijxy", steps_hot, row_part, precision=highest)
    return pairs.reshape(head_count, PATCHES, PATCHES)


def fold_bias_grad(pair_grad):
    steps_hot = offset_onehot()
    head_count = pair_grad.shape[0]
    grid_grad = pair_grad.reshape(head_count, GRID, GRID, GRID, GRID)
    col_part = jnp.einsum("jyb,hijxy->hixb", steps_hot, grid_grad, precision=highest)
    table_grad = jnp.einsum("ixa,hixb->hab", steps_hot, col_part, precision=highest)
    return table_grad.reshape(head_count, SPAN * SPAN)


def gather_unit(piece):
    parts = lax.axis_size("narrow")
    whole = lax.all_gather(piece, ROWS_AXES, axis=0, tiled=True)
    return whole.reshape(parts, whole.shape[0] // parts, whole.shape[1])


def scatter_unit(grads):
    flat = grads.astype(bf16).reshape(-1, grads.shape[-1])
    return lax.psum_scatter(flat, ROWS_AXES, scatter_dimension=0, tiled=True)


def to_heads(values):
    parts, rows, cols = values.shape
    split = values.reshape(parts, rows, cols // HEAD_DIM, HEAD_DIM)
    return split.transpose(0, 2, 1, 3).reshape(-1, rows, HEAD_DIM)


def from_heads(values, parts):
    heads, rows, _ = values.shape
    split = values.reshape(parts, heads // parts, rows, HEAD_DIM).transpose(0, 2, 1, 3)
    return split.reshape(parts, rows, -1)


def attention_forward(residual, proj, time_part, params, pairs):
    norm_gain, norm_shift, qkv_bias, out_bias = params
    parts = proj.shape[0]
    cols = proj.shape[2] // 4
    normed, unit, scale = layer_norm(residual, norm_gain[0], norm_shift[0])
    normed_low = normed.astype(bf16)
    spatial = jnp.einsum("rd,zdc->zrc", normed_low, proj[:, :, : 3 * cols], preferred_element_type=f32)
    offsets = time_part + jnp.stack([qkv_bias[0], jnp.zeros_like(qkv_bias[0]), qkv_bias[1]])
    offsets = offsets.reshape(3, parts, 1, cols)
    queries, key_rows, value_rows = (
        to_heads((spatial[:, :, j * cols : (j + 1) * cols] + offsets[j]).astype(bf16)) for j in range(3)
    )
    scores = jnp.einsum("hqd,hkd->hqk", queries, key_rows, preferred_element_type=f32)
    scores = scores * HEAD_DIM ** (-0.5) + pairs
    attention = jax.nn.softmax(scores, axis=-1)
    attention_low = attention.astype(bf16)
    mixed = jnp.einsum("hqk,hkd->hqd", attention_low, value_rows, preferred_element_type=f32)
    mixed_low = from_heads(mixed.astype(bf16), parts)
    branch = jnp.einsum("zrc,zdc->rd", mixed_low, proj[:, :, 3 * cols :], preferred_element_type=f32)
    middle = residual + (branch + out_bias[0])
    saved = (normed_low, unit, scale, queries, key_rows, value_rows, attention, mixed_low)
    return middle, saved


def mlp_forward(middle, up, down, params, up_bias):
    norm_gain, norm_shift, qkv_bias, out_bias = params
    parts = up.shape[0]
    normed, unit, scale = layer_norm(middle, norm_gain[1], norm_shift[1])
    normed_low = normed.astype(bf16)
    hidden = jnp.einsum("rd,zdc->zrc", normed_low, up, preferred_element_type=f32)
    hidden = hidden + up_bias.reshape(parts, 1, -1)
    activated = jax.nn.gelu(hidden, approximate=True).astype(bf16)
    branch = jnp.einsum("zrc,zdc->rd", activated, down, preferred_element_type=f32)
    return middle + (branch + out_bias[1]), (normed_low, unit, scale, hidden, activated)


def mlp_backward(gradient, up, down, params, saved):
    norm_gain = params[0]
    normed_low, unit, scale, hidden, activated = saved
    grad_low = gradient.astype(bf16)
    out_bias_grad = jnp.sum(grad_low.astype(f32), axis=0)
    down_grad = jnp.einsum("rd,zrc->zdc", grad_low, activated, preferred_element_type=f32)
    act_grad = jnp.einsum("rd,zdc->zrc", grad_low, down, preferred_element_type=f32)
    _, gelu_back = jax.vjp(lambda values: jax.nn.gelu(values, approximate=True), hidden)
    hidden_low = gelu_back(act_grad)[0].astype(bf16)
    up_bias_grad = jnp.sum(hidden_low.astype(f32), axis=1).reshape(-1)
    up_grad = jnp.einsum("rd,zrc->zdc", normed_low, hidden_low, preferred_element_type=f32)
    normed_grad = jnp.einsum("zrc,zdc->rd", hidden_low, up, preferred_element_type=f32)
    from_norm, gain_grad, shift_grad = layer_norm_back(normed_grad, unit, scale, norm_gain[1])
    return gradient + from_norm, up_grad, down_grad, (gain_grad, shift_grad, out_bias_grad, up_bias_grad)


def attention_backward(grad_mid, proj, params, saved):
    norm_gain = params[0]
    normed_low, unit, scale, queries, key_rows, value_rows, attention, mixed_low = saved
    parts = proj.shape[0]
    cols = proj.shape[2] // 4
    score_scale = HEAD_DIM ** (-0.5)
    mid_low = grad_mid.astype(bf16)
    out_bias_grad = jnp.sum(mid_low.astype(f32), axis=0)
    out_grad = jnp.einsum("rd,zrc->zdc", mid_low, mixed_low, preferred_element_type=f32)
    mixed_grad = jnp.einsum("rd,zdc->zrc", mid_low, proj[:, :, 3 * cols :], preferred_element_type=f32)
    mixed_grad = to_heads(mixed_grad.astype(bf16))
    dot_back = jnp.einsum("hqd,hkd->hqk", mixed_grad, value_rows, preferred_element_type=f32)
    score_grad = attention * (dot_back - jnp.sum(attention * dot_back, axis=-1, keepdims=True))
    score_low = score_grad.astype(bf16)
    table_grad = fold_bias_grad(score_low.astype(f32))
    query_grad = jnp.einsum("hqk,hkd->hqd", score_low, key_rows, preferred_element_type=f32) * score_scale
    key_grad = jnp.einsum("hqk,hqd->hkd", score_low, queries, preferred_element_type=f32) * score_scale
    value_grad = jnp.einsum("hqk,hqd->hkd", attention.astype(bf16), mixed_grad, preferred_element_type=f32)
    qkv_low = jnp.concatenate(
        [from_heads(item.astype(bf16), parts) for item in (query_grad, key_grad, value_grad)], axis=-1
    )
    spatial_grad = jnp.einsum("rd,zrc->zdc", normed_low, qkv_low, preferred_element_type=f32)
    proj_grad = jnp.concatenate([spatial_grad, out_grad], axis=-1)
    sums = jnp.sum(qkv_low.astype(f32), axis=1).reshape(parts, 3, cols).transpose(1, 0, 2).reshape(3, -1)
    normed_grad = jnp.einsum("zrc,zdc->rd", qkv_low, proj[:, :, : 3 * cols], preferred_element_type=f32)
    from_norm, gain_grad, shift_grad = layer_norm_back(normed_grad, unit, scale, norm_gain[0])
    return grad_mid + from_norm, proj_grad, sums, table_grad, (gain_grad, shift_grad, out_bias_grad)


class Place:
    def __init__(self):
        wide = lax.axis_index("wide")
        self.z = lax.axis_index("narrow")
        self.y, self.x, self.c = wide // 4, (wide // 2) % 2, wide % 2

    def wide(self, flip_y=0, flip_x=0, flip_c=0):
        y = 1 - self.y if flip_y else self.y
        x = 1 - self.x if flip_x else self.x
        c = 1 - self.c if flip_c else self.c
        return y * 4 + x * 2 + c

    def along_z(self, steps):
        return lax.rem(self.z + steps, 4)

    def peers(self):
        across = [(self.wide(1, 0, 0), self.z), (self.wide(0, 1, 0), self.z), (self.wide(0, 0, 1), self.z)]
        return across + [(self.wide(), self.along_z(k)) for k in (1, 2, 3)]

    def greet(self):
        barrier = pltpu.get_barrier_semaphore()
        for peer in self.peers():
            pl.semaphore_signal(barrier, inc=1, device_id=peer, device_id_type=MESH)
        pl.semaphore_wait(barrier, 6)


def unit_cut(unit, rows):
    low = rows // 32 * 16
    return low if unit % 2 == 0 else rows - low


class Line:
    def __init__(self, place, block, send, recv):
        self.place, self.block, self.send, self.recv = place, block, send, recv

    def copy(self, src, origin, step, slot):
        place = self.place
        return pltpu.make_async_remote_copy(
            src_ref=src, dst_ref=self.block(origin), send_sem=self.send.at[slot], recv_sem=self.recv.at[origin],
            device_id=(place.wide(), place.z + step), device_id_type=MESH,
        )

    def begin(self, own):
        z = self.place.z

        @pl.when(z < 3)
        def _():
            self.copy(own, z, 1, z).start()

        @pl.when(z > 0)
        def _():
            self.copy(own, z, -1, 4).start()

    def arrive(self, far, then=lambda origin: None):
        z = self.place.z
        for side, valid, room in ((-1, z - far >= 0, z < 3), (1, z + far <= 3, z > 0)):

            @pl.when(valid)
            def _(side=side, room=room):
                origin = z + side * far
                here = self.block(origin)
                self.copy(here, origin, -side, origin).wait_recv()

                @pl.when(room)
                def _():
                    self.copy(here, origin, -side, origin).start()

                then(origin)

    def finish(self):
        z = self.place.z
        for origin in range(4):
            sent = jnp.where(origin <= z, z < 3, z > 0)

            @pl.when(sent)
            def _(origin=origin):
                self.copy(self.block(origin), origin, 0, origin).wait_send()

        @pl.when(z > 0)
        def _():
            self.copy(self.block(0), 0, 0, 4).wait_send()


LINE_SEMS = 5
Z_AHEAD = 43.0
UNIT_TIME = 46.0
GATHER_SEMS = 58
Y_FIRST, X_LAST, X_NEAR, X_FAR, Y_NEAR, Y_FAR = 5, 9, 13, 17, 21, 25
C_OWN, C_Y, C_X, C_X_NEAR, C_Y_NEAR, C_X_FAR, C_Y_FAR = 29, 33, 37, 41, 45, 49, 53


class GatherUnit:
    def __init__(self, place, piece, whole, send, recv, cut):
        self.place, self.piece, self.whole = place, piece, whole
        self.send, self.recv = send, recv
        self.rows = piece.shape[0]
        self.first, self.last, self.every = pl.ds(0, cut), pl.ds(cut, self.rows - cut), pl.ds(0, self.rows)
        self.line = Line(place, lambda origin: self.block(origin, 0, 0, self.every), send, recv)
        self.peer = {
            "y": (place.wide(1, 0, 0), place.z), "x": (place.wide(0, 1, 0), place.z), "c": (place.wide(0, 0, 1), place.z)
        }
        self.order = [place.along_z(k) for k in (0, 1, 3, 2)]
        self.sent = []

    def block(self, origin, flip_y, flip_x, rows):
        first = pl.multiple_of(self.place.wide(flip_y, flip_x) * self.rows + rows.start, 16)
        return self.whole.at[origin, pl.ds(first, rows.size)]

    def copy(self, base, axis, origin, flip_y, flip_x, rows, own=None):
        block = self.block(origin, flip_y, flip_x, rows)
        return pltpu.make_async_remote_copy(
            src_ref=block if own is None else own, dst_ref=block, send_sem=self.send.at[base + origin],
            recv_sem=self.recv.at[base + origin], device_id=self.peer[axis], device_id_type=MESH,
        )

    def put(self, *where):
        self.copy(*where).start()

    def wait(self, *where):
        self.copy(*where).wait_recv()

    def begin(self):
        z = self.place.z
        self.line.begin(self.piece)
        self.put(Y_FIRST, "y", z, 0, 0, self.first, self.piece.at[self.first])
        self.put(X_LAST, "x", z, 0, 0, self.last, self.piece.at[self.last])
        self.put(X_NEAR, "x", z, 0, 0, self.first, self.piece.at[self.first])
        self.put(Y_NEAR, "y", z, 0, 0, self.last, self.piece.at[self.last])
        self.put(C_OWN, "c", z, 0, 0, self.every, self.piece)
        self.local = pltpu.make_async_copy(self.piece, self.block(z, 0, 0, self.every), self.send.at[GATHER_SEMS - 1])
        self.local.start()

    def along_z(self, far):
        def then(origin):
            self.put(Y_FIRST, "y", origin, 0, 0, self.first)
            self.put(X_LAST, "x", origin, 0, 0, self.last)
            self.put(X_NEAR, "x", origin, 0, 0, self.first)
            self.put(Y_NEAR, "y", origin, 0, 0, self.last)
            self.put(C_OWN, "c", origin, 0, 0, self.every)

        self.line.arrive(far, then)

    def across(self, at):
        origin = self.order[at]
        self.wait(Y_FIRST, "y", origin, 1, 0, self.first)
        self.put(X_FAR, "x", origin, 1, 0, self.first)
        self.put(C_Y, "c", origin, 1, 0, self.first)
        self.wait(X_LAST, "x", origin, 0, 1, self.last)
        self.put(Y_FAR, "y", origin, 0, 1, self.last)
        self.put(C_X, "c", origin, 0, 1, self.last)

    def near_to_core(self, at):
        origin = self.order[at]
        self.wait(X_NEAR, "x", origin, 0, 1, self.first)
        self.put(C_X_NEAR, "c", origin, 0, 1, self.first)
        self.wait(Y_NEAR, "y", origin, 1, 0, self.last)
        self.put(C_Y_NEAR, "c", origin, 1, 0, self.last)

    def far_to_core(self, at):
        origin = self.order[at]
        self.wait(X_FAR, "x", origin, 1, 1, self.first)
        self.put(C_X_FAR, "c", origin, 1, 1, self.first)
        self.wait(Y_FAR, "y", origin, 1, 1, self.last)
        self.put(C_Y_FAR, "c", origin, 1, 1, self.last)

    def steps(self, base):
        start = max(0.0, base - Z_AHEAD)
        out = [(start, self.begin)]
        out += [(start + 1.0 + 7.5 * far, functools.partial(self.along_z, far)) for far in (1, 2, 3)]
        for at in range(4):
            known = start + 24.0 if at else 0.0
            out.append((max(known, base + 9.0 + 9.0 * at), functools.partial(self.across, at)))
            out.append((max(known + 1.0, base + 15.0 + 9.0 * at), functools.partial(self.near_to_core, at)))
            out.append((max(known + 2.0, base + 25.0 + 9.0 * at), functools.partial(self.far_to_core, at)))
        out.append((base + 56.0, self.finish))
        return out

    def finish(self):
        firsts = (Y_FIRST, X_NEAR, X_FAR, C_Y, C_X_NEAR, C_X_FAR)
        lasts = (X_LAST, Y_NEAR, Y_FAR, C_X, C_Y_NEAR, C_Y_FAR)
        for origin in range(4):
            for base in (C_Y, C_X_NEAR, C_X_FAR):
                self.wait(base, "c", origin, 0, 0, self.first)
            for base in (C_X, C_Y_NEAR, C_Y_FAR):
                self.wait(base, "c", origin, 0, 0, self.last)
            self.wait(C_OWN, "c", origin, 0, 0, self.every)
        for origin in range(4):
            for base in firsts:
                self.copy(base, "c", origin, 0, 0, self.first).wait_send()
            for base in lasts:
                self.copy(base, "c", origin, 0, 0, self.last).wait_send()
            self.copy(C_OWN, "c", origin, 0, 0, self.every).wait_send()
        self.line.finish()
        self.local.wait()


def column_ids(width):
    return lax.broadcasted_iota(jnp.int32, (1, width), 1)


def unit_rows(values):
    average = jnp.mean(values, axis=-1, keepdims=True)
    centred = values - average
    variance = jnp.mean(centred * centred, axis=-1, keepdims=True)
    scale = lax.rsqrt(variance + eps_norm)
    return centred * scale, scale


def dot_plain(left, right):
    return lax.dot_general(left, right, (((1,), (0,)), ((), ())), preferred_element_type=f32)


def dot_turned(left, right):
    return lax.dot_general(left, right, (((1,), (1,)), ((), ())), preferred_element_type=f32)


def remote(src, dst, send, recv, peer):
    copy = pltpu.make_async_remote_copy(
        src_ref=src, dst_ref=dst, send_sem=send, recv_sem=recv, device_id=peer, device_id_type=MESH
    )
    copy.start()
    return copy


def z_line(place, every, send, recv):
    return Line(place, lambda origin: every.at[origin], send, recv)


class Stream:
    def __init__(self, slots, sems, sources):
        self.slots, self.sems, self.sources = slots, sems, sources
        self.started = 0

    def ensure(self, upto):
        while self.started <= upto and self.started < len(self.sources):
            at = self.started
            pltpu.make_async_copy(self.sources[at], self.slots.at[at % 2], self.sems.at[at % 2]).start()
            self.started += 1

    def take(self, at):
        self.ensure(at)
        pltpu.make_async_copy(self.sources[at], self.slots.at[at % 2], self.sems.at[at % 2]).wait()
        return self.slots.at[at % 2]


FORWARD_IN = 17
LAYER_SAVED = 6


def edges(head_cols):
    return 3 * head_cols // 128 * 128, -(-3 * head_cols // 128) * 128


def gelu(values):
    inner = math.sqrt(2.0 / math.pi) * (values + 0.044715 * values * values * values)
    return 0.5 * values * (1.0 + jnp.tanh(inner))


def window_bias(windows, put):
    for grid_row in range(GRID):
        shift = (GRID - 1 - grid_row) * GRID
        moved = windows if shift == 0 else pltpu.roll(windows, 512 - shift, 1)
        put(grid_row, moved[:, :PATCHES])


def forward_kernel(layers, *refs):
    units = 3 * layers
    refs = list(refs)

    def take(count):
        out = refs[:count]
        del refs[:count]
        return out

    (tokens, cot, pick, time_own, time_weight, windows_own, small_own, gains, shifts, out_bias) = take(10)
    packed = take(layers)
    (mlp_weight,) = take(1)
    pieces = []
    for layer in range(layers):
        pieces += [packed[layer], mlp_weight.at[layer, 0], mlp_weight.at[layer, 1]]
    wholes = take(units)
    saved = [take(LAYER_SAVED) for _ in range(layers)]
    block_out, grad_out, time_out, time_sel_out = take(4)
    (
        send, recv, z_send, z_recv, t_send, t_recv, save_sem, w_sem,
        w_slots, tok_all, cot_all, windows_all, small_all, time_all, share, share_y, share_x, share_c, share_z,
        x_buf, mid_buf, low_buf, acc_buf, s_buf, att_buf, act_buf, hid_buf, bias_buf, mixed_buf,
    ) = refs
    place = Place()
    place.greet()
    gather = [
        GatherUnit(place, pieces[u], wholes[u], send.at[u], recv.at[u], unit_cut(u, pieces[u].shape[0]))
        for u in range(units)
    ]
    state = set()
    tokens_n, d_model = tokens.shape
    head_cols = d_model // 4
    yp, xp, cp = ((place.wide(1, 0, 0), place.z), (place.wide(0, 1, 0), place.z), (place.wide(0, 0, 1), place.z))
    py, px, pc = place.y, place.x, place.c

    tok, win, small, cots, rz = (
        z_line(place, every, z_send.at[at], z_recv.at[at])
        for at, every in enumerate((tok_all, windows_all, small_all, cot_all, share_z))
    )
    kept = [
        pltpu.make_async_copy(src, every.at[place.z], save_sem.at[at])
        for at, (src, every) in enumerate(
            ((tokens, tok_all), (windows_own, windows_all), (small_own, small_all), (cot, cot_all))
        )
    ]
    given = {}

    def give(slot, src, dst, peer):
        given[slot] = remote(src, dst, t_send.at[slot], t_recv.at[slot], peer)

    def time_core():
        for copy in kept:
            copy.start()
        time_all[py, px, pc] = time_own[...]
        give(0, time_all.at[py, px, pc], time_all.at[py, px, pc], cp)

    def time_x():
        given[0].wait_recv()
        give(1, time_all.at[py, px], time_all.at[py, px], xp)

    def time_y():
        given[1].wait_recv()
        give(2, time_all.at[py], time_all.at[py], yp)

    def time_share():
        given[2].wait_recv()
        rows = time_all[...].reshape(128, d_model)
        cut = time_weight.shape[1]
        at_row = lax.broadcasted_iota(jnp.int32, (d_model, cut), 0)
        at_col = lax.broadcasted_iota(jnp.int32, (d_model, cut), 1)
        select = (at_row == at_col + place.wide() * cut).astype(bf16)
        picked = dot_plain(rows, select).astype(bf16)
        time_sel_out[...] = picked
        time_out[...] = rows
        for layer in range(layers):
            part = dot_plain(picked, time_weight[layer]).reshape(2, 2, 2, 16, d_model)
            share[:, :, :, layer] = part[:, :, :, :8]
        give(3, share.at[1 - py], share_y, yp)

    def share_step_x():
        given[3].wait_recv()
        share[py] = share[py] + share_y[...]
        give(4, share.at[py, 1 - px], share_x, xp)

    def share_step_c():
        given[4].wait_recv()
        share[py, px] = share[py, px] + share_x[...]
        give(5, share.at[py, px, 1 - pc], share_c, cp)

    def share_step_z():
        given[5].wait_recv()
        share[py, px, pc] = share[py, px, pc] + share_c[...]
        share_z[place.z] = share[py, px, pc]
        rz.begin(share_z.at[place.z])
        for slot in range(6):
            given[slot].wait_send()

    def line_steps(line, own, start, pace):
        steps = [(start, functools.partial(line.begin, own))]
        steps += [(start + pace * far, functools.partial(line.arrive, far)) for far in (1, 2, 3)]
        return steps + [(start + 3 * pace + 4.0, line.finish)]

    def mark(key):
        if key == "rows":
            for copy in kept:
                copy.wait()
        state.add(key)

    events = [
        (0.1, time_core),
        (3.0, time_x),
        (7.0, time_y),
        (11.0, time_share),
        (18.0, share_step_x),
        (24.0, share_step_c),
        (28.0, share_step_z),
    ]
    events += line_steps(small, small_own, 0.2, 5.0)
    events += [(28.0 + 8.0 * far, functools.partial(rz.arrive, far)) for far in (1, 2, 3)] + [(56.0, rz.finish)]
    events += line_steps(win, windows_own, 34.0, 10.0)
    events += line_steps(tok, tokens, 36.0, 14.0)
    events += [(84.0, functools.partial(mark, "rows"))]
    events += line_steps(cots, cot, 130.0, 16.0)
    for at, unit in enumerate(gather):
        events += unit.steps(UNIT_TIME * at)
        events.append((UNIT_TIME * at + 56.5, functools.partial(mark, at)))

    stream = Stream(w_slots, w_sem, [wholes[u].at[z] for u in range(units) for z in range(4)])
    pending = {}

    def save(slot, src, dst):
        copy = pltpu.make_async_copy(src, dst, save_sem.at[slot])
        copy.start()
        pending[slot] = copy

    def settle(slot):
        if slot in pending:
            pending.pop(slot).wait()

    def weights(unit, z):
        at = unit * 4 + z
        stream.ensure(at)
        if (at + 1) // 4 in state:
            stream.ensure(at + 1)
        return stream.take(at)

    def compute_steps():
        columns = column_ids(d_model)
        out_start, qkv_end = edges(head_cols)
        for layer in range(layers):
            x_save, mid_save, s_save, att_save, hid_save, act_save = saved[layer]
            row = 2 * layer
            yield (3 * layer if layer else "rows"), 2.0
            if layer == 0:
                total = dot_plain(pick[:, 0:tokens_n], tok_all[0])
                for z in range(1, 4):
                    total = total + dot_plain(pick[:, z * tokens_n : (z + 1) * tokens_n], tok_all[z])
                x_buf[...] = total
            settle(4)
            settle(5)
            save(4, x_buf, x_save)
            unit, _ = unit_rows(x_buf[...])
            low_buf[...] = (unit * gains[row : row + 1, :] + shifts[row : row + 1, :]).astype(bf16)
            settle(6)
            for z in range(4):
                yield 3 * layer, 2.0
                w = weights(3 * layer, z)
                share_rows = share_z[z, layer]
                at_image = lax.broadcasted_iota(jnp.int32, share_rows.shape, 0) == place.z
                offset = jnp.sum(jnp.where(at_image, share_rows, 0.0), axis=0, keepdims=True)
                offset = offset + small_all[z, 2 + layer : 3 + layer, :]
                spatial = dot_plain(low_buf[...], w[:, :qkv_end]) + offset[:, :qkv_end]
                s_buf[z, :, :qkv_end] = spatial.astype(bf16)
                yield 3 * layer, 2.0
                q = s_buf[z, :, 0:head_cols]
                k = s_buf[z, :, head_cols : 2 * head_cols]
                v = s_buf[z, :, 2 * head_cols : 3 * head_cols]
                head_of = column_ids(head_cols) // HEAD_DIM
                slot = z % 2
                settle(8 + slot)

                def one_head(head, carry):
                    here = head_of == head

                    def put(grid_row, block):
                        bias_buf[grid_row * GRID : (grid_row + 1) * GRID, :] = block

                    first_row = pl.multiple_of(head * GRID, GRID)
                    window_bias(windows_all[z, layer, pl.ds(first_row, GRID), :], put)
                    scores = dot_turned(jnp.where(here, q, 0), k)
                    scores = scores * HEAD_DIM ** (-0.5) + bias_buf[...]
                    top = jnp.max(scores, axis=-1, keepdims=True)
                    exponent = jnp.exp(scores - top)
                    attention = exponent / jnp.sum(exponent, axis=-1, keepdims=True)
                    att_buf[slot, head] = attention
                    mixed_buf[...] += dot_plain(attention.astype(bf16), jnp.where(here, v, 0))
                    return carry

                mixed_buf[...] = jnp.zeros_like(mixed_buf)
                for pair in range(2):
                    lax.fori_loop(2 * pair, 2 * pair + 2, one_head, 0)
                    yield 3 * layer, 2.0
                save(8 + slot, att_buf.at[slot], att_save.at[z])
                s_buf[z, :, 3 * head_cols :] = mixed_buf[...].astype(bf16)
                heads = jnp.where(columns[:, out_start:] >= 3 * head_cols, s_buf[z, :, out_start:], 0)
                branch = dot_turned(heads, w[:, out_start:])
                acc_buf[...] = branch if z == 0 else acc_buf[...] + branch
            save(6, s_buf, s_save)
            settle(4)
            mid_buf[...] = x_buf[...] + (acc_buf[...] + out_bias[row : row + 1, :])
            save(5, mid_buf, mid_save)
            unit, _ = unit_rows(mid_buf[...])
            low_buf[...] = (unit * gains[row + 1 : row + 2, :] + shifts[row + 1 : row + 2, :]).astype(bf16)
            settle(7)
            for z in range(4):
                yield 3 * layer + 1, 2.5
                w = weights(3 * layer + 1, z)
                slot = z % 2
                settle(10 + slot)
                hid_buf[slot] = dot_plain(low_buf[...], w[...]) + small_all[z, layer : layer + 1, :]
                save(10 + slot, hid_buf.at[slot], hid_save.at[z])
                act_buf[z] = gelu(hid_buf[slot]).astype(bf16)
            save(7, act_buf, act_save)
            for z in range(4):
                yield 3 * layer + 2, 1.8
                w = weights(3 * layer + 2, z)
                branch = dot_turned(act_buf[z], w[...])
                acc_buf[...] = branch if z == 0 else acc_buf[...] + branch
            x_buf[...] = mid_buf[...] + (acc_buf[...] + out_bias[row + 1 : row + 2, :])
        block_out[...] = x_buf[...].astype(bf16)
        total = dot_plain(pick[:, 0:tokens_n], cot_all[0])
        for z in range(1, 4):
            total = total + dot_plain(pick[:, z * tokens_n : (z + 1) * tokens_n], cot_all[z])
        grad_out[...] = total
        for slot in list(pending):
            settle(slot)

    interleave(events, compute_steps(), state)


def interleave(events, compute, state):
    events = sorted(events, key=lambda item: item[0])
    clock = 0.0
    wanted = next(compute)
    while wanted is not None or events:
        if events and (events[0][0] <= clock or wanted is None or wanted[0] not in state):
            at, step = events.pop(0)
            clock = max(clock, at)
            step()
            continue
        clock += wanted[1]
        wanted = next(compute, None)


def forward_all(
    tokens, cot, pick, time_own, time_weight, windows_own, small_own, gains, shifts, out_bias, packed, mlp_weight
):
    layers = len(packed)
    units = 3 * layers
    rows, d_model = tokens.shape
    piece_rows = packed[0].shape[0]
    any_space = pl.BlockSpec(memory_space=pl.ANY)
    vmem = pl.BlockSpec(memory_space=pltpu.VMEM)
    layer_shapes = [
        ((rows, d_model), f32),
        ((rows, d_model), f32),
        ((4, rows, d_model), bf16),
        ((4, 4, rows, rows), f32),
        ((4, rows, d_model), f32),
        ((4, rows, d_model), bf16),
    ]
    out_shape = (
        [jax.ShapeDtypeStruct((4, 8 * piece_rows, d_model), bf16)] * units
        + [jax.ShapeDtypeStruct(*item) for item in layer_shapes] * layers
        + [
            jax.ShapeDtypeStruct((rows, d_model), bf16),
            jax.ShapeDtypeStruct((rows, d_model), f32),
            jax.ShapeDtypeStruct((128, d_model), bf16),
            jax.ShapeDtypeStruct((128, piece_rows), bf16),
        ]
    )
    share_tail = (layers, 8, d_model)
    scratch = [
        pltpu.SemaphoreType.DMA((units, GATHER_SEMS)),
        pltpu.SemaphoreType.DMA((units, GATHER_SEMS)),
        pltpu.SemaphoreType.DMA((5, LINE_SEMS)),
        pltpu.SemaphoreType.DMA((5, LINE_SEMS)),
        pltpu.SemaphoreType.DMA((6,)),
        pltpu.SemaphoreType.DMA((6,)),
        pltpu.SemaphoreType.DMA((12,)),
        pltpu.SemaphoreType.DMA((2,)),
        pltpu.VMEM((2, d_model, d_model), bf16),
        pltpu.VMEM((4, rows, d_model), bf16),
        pltpu.VMEM((4, rows, d_model), bf16),
        pltpu.VMEM((4,) + windows_own.shape, f32),
        pltpu.VMEM((4,) + small_own.shape, f32),
        pltpu.VMEM((2, 2, 2, 16, d_model), bf16),
        pltpu.VMEM((2, 2, 2) + share_tail, f32),
        pltpu.VMEM((2, 2) + share_tail, f32),
        pltpu.VMEM((2,) + share_tail, f32),
        pltpu.VMEM(share_tail, f32),
        pltpu.VMEM((4,) + share_tail, f32),
        pltpu.VMEM((rows, d_model), f32),
        pltpu.VMEM((rows, d_model), f32),
        pltpu.VMEM((rows, d_model), bf16),
        pltpu.VMEM((rows, d_model), f32),
        pltpu.VMEM((4, rows, d_model), bf16),
        pltpu.VMEM((2, 4, rows, rows), f32),
        pltpu.VMEM((4, rows, d_model), bf16),
        pltpu.VMEM((2, rows, d_model), f32),
        pltpu.VMEM((rows, rows), f32),
        pltpu.VMEM((rows, d_model // 4), f32),
    ]
    out = pl.pallas_call(
        functools.partial(forward_kernel, layers),
        out_shape=out_shape,
        in_specs=[any_space] * 2 + [vmem] * 8 + [any_space] * (layers + 1),
        out_specs=[any_space] * (units + LAYER_SAVED * layers) + [vmem] * 4,
        scratch_shapes=scratch,
        compiler_params=pltpu.CompilerParams(
            collective_id=0, has_side_effects=True, vmem_limit_bytes=60 * 2**20
        ),
        name="forward_all",
    )(tokens, cot, pick, time_own, time_weight, windows_own, small_own, gains, shifts, out_bias, *packed, mlp_weight)
    wholes = out[:units]
    saved = [out[units + LAYER_SAVED * at : units + LAYER_SAVED * (at + 1)] for at in range(layers)]
    return wholes, saved, out[units + LAYER_SAVED * layers :]


def gelu_slope(values):
    factor = math.sqrt(2.0 / math.pi)
    square = values * values
    bend = jnp.tanh(factor * (values + 0.044715 * square * values))
    return 0.5 * (1.0 + bend) + 0.5 * values * (1.0 - bend * bend) * factor * (1.0 + 3 * 0.044715 * square)


def dot_rows(left, right):
    return lax.dot_general(left, right, (((0,), (0,)), ((), ())), preferred_element_type=f32)


def norm_back(grad, unit, scale, norm_gain):
    weighted = grad * norm_gain
    first = jnp.mean(weighted, axis=-1, keepdims=True)
    second = jnp.mean(weighted * unit, axis=-1, keepdims=True)
    return scale * (weighted - first - unit * second)


def column_sums(values):
    return jnp.sum(values, axis=0, keepdims=True)


def fold_window(grads):
    total = None
    empty = jnp.zeros((GRID, 512 - PATCHES), f32)
    for grid_row in range(GRID):
        wide = jnp.concatenate([grads[grid_row * GRID : (grid_row + 1) * GRID, :], empty], axis=1)
        shift = (GRID - 1 - grid_row) * GRID
        moved = wide if shift == 0 else pltpu.roll(wide, shift, 1)
        total = moved if total is None else total + moved
    return total


SCATTER_SEMS = 23


def add_into(total, part):
    total[...] = total[...] + part[...]


class ScatterUnit:
    def __init__(self, place, out, total, far, near, from_z, send, recv, cut):
        self.place, self.out = place, out
        self.total, self.far, self.near, self.from_z = total, far, near, from_z
        self.send, self.recv = send, recv
        self.rows, self.cut = total.shape[3], cut
        self.first, self.last = pl.ds(0, cut), pl.ds(cut, self.rows - cut)
        self.copies, self.unsent, self.closed = {}, set(), set()

    def put(self, slot, peer, src, dst):
        self.copies[slot] = remote(src, dst, self.send.at[slot], self.recv.at[slot], peer)
        self.unsent.add(slot)

    def settle(self, slots):
        for slot in sorted(self.unsent.intersection(slots)):
            self.copies[slot].wait_send()
            self.unsent.remove(slot)

    def first_stage(self, k):
        p = self.place
        self.put(4 + k, (p.wide(0, 1), p.z), self.total.at[k, :, 1 - p.x, self.first], self.far.at[k, :, self.first])
        self.put(8 + k, (p.wide(1, 0), p.z), self.total.at[k, 1 - p.y, :, self.last], self.far.at[k, :, self.last])

    def second_stage(self, k):
        p = self.place
        self.copies[4 + k].wait_recv()
        for block in range(2):
            add_into(self.total.at[k, block, p.x, self.first], self.far.at[k, block, self.first])
        self.put(12 + k, (p.wide(1, 0), p.z), self.total.at[k, 1 - p.y, p.x, self.first], self.near.at[k, self.first])
        self.copies[8 + k].wait_recv()
        for block in range(2):
            add_into(self.total.at[k, p.y, block, self.last], self.far.at[k, block, self.last])
        self.put(16 + k, (p.wide(0, 1), p.z), self.total.at[k, p.y, 1 - p.x, self.last], self.near.at[k, self.last])

    def third_stage(self, k):
        p = self.place
        self.copies[12 + k].wait_recv()
        self.copies[16 + k].wait_recv()
        add_into(self.total.at[k, p.y, p.x], self.near.at[k])
        if k:
            self.put(19 + k, (p.wide(), p.along_z(k)), self.total.at[k, p.y, p.x], self.from_z.at[k - 1])
            self.closed.add(k)

    def finish(self):
        p = self.place
        for k in (1, 2, 3):
            self.copies[19 + k].wait_recv()
        both = self.total[0, p.y, p.x].astype(f32)
        for k in range(3):
            both = both + self.from_z[k].astype(f32)
        self.out[...] = both
        self.settle(list(self.copies))
        self.closed.add(0)


FAR_FIRST = (2, 1, 3, 0)


def scatter_step(unit, k, late):
    unit.second_stage(k)

    def third():
        unit.third_stage(k)
        if k == 0:
            return ((late, unit.finish),)

    return ((late, third),)


def backward_kernel(last_layer, *refs):
    refs = list(refs)

    def take(count):
        out = refs[:count]
        del refs[:count]
        return out

    (
        grad, mid_in, gains, shifts, trow_in, x_in, pick_in, time_weight, rows_in, s_all, att_all, hid_all, act_all,
        proj, up, down,
    ) = take(16)
    proj_out, up_out, down_out, grad_out, rows_out, row_sums, table_sums, time_sums, trow_out, rows_all = take(10)
    (
        total_a, total_b, far, near, from_z, right_a, right_b, left, turned,
        w_slots, s_slots, att_slots, hid_slots, acc_buf, low_buf, head_grads,
        row_parts, rows_z, rows_w, table_parts, table_low, table_z, table_w, trow_z, trow_kept, small_send, small_recv,
        send, recv, left_send, left_recv, line_send, line_recv, w_sem, s_sem, att_sem, hid_sem, load_sem, credit,
    ) = refs
    place = Place()
    place.greet()
    rows, d_model = grad.shape
    cut = down_out.shape[0]
    head_cols = d_model // 4
    core = (place.wide(0, 0, 1), place.z)
    zs = {k: place.along_z(k) for k in range(4)}
    columns = column_ids(d_model)
    out_start, qkv_end = edges(head_cols)
    units = {
        name: ScatterUnit(
            place, out, total, far.at[at], near.at[at], from_z.at[at], send.at[at], recv.at[at], unit_cut(at, cut)
        )
        for at, (name, out, total) in enumerate(
            (("down", down_out, total_a), ("up", up_out, total_b), ("proj", proj_out, total_a))
        )
    }
    line = z_line(place, rows_all, line_send, line_recv)

    right_copies = {}

    def give_right(name, at, k, src, buffer):
        right_copies[name, k] = remote(
            src, buffer.at[zs[k], pl.ds(rows, rows)], send.at[at, k], recv.at[at, k], core
        )

    left_copies = {}

    def make_left(at, values):
        if at > 1:
            for copy in left_copies[at - 2]:
                copy.wait_send()
        flipped = turned.at[at % 2]
        flipped[...] = values.T
        copies = []
        for block in range(4):
            mine = pl.multiple_of((2 * block + place.c) * cut, 16)
            other = pl.multiple_of((2 * block + 1 - place.c) * cut, 16)
            here = pl.ds(block * cut, cut)
            copies.append(
                remote(
                    flipped.at[pl.ds(other, cut)], left.at[at, here, pl.ds(rows, rows)],
                    left_send.at[at, block], left_recv.at[at, block], core,
                )
            )
            left[at, here, 0:rows] = flipped[pl.ds(mine, cut), :]
        left_copies[at] = copies

    def left_ready(at):
        for copy in left_copies[at]:
            copy.wait_recv()

    loads, keep = [], []
    if last_layer:
        line.begin(rows_in)
        keep.append(pltpu.make_async_copy(rows_in, rows_all.at[place.z], load_sem.at[4]))
        keep[0].start()
    for k in FAR_FIRST:
        give_right("down", 0, k, act_all.at[zs[k]], right_a)
        load = pltpu.make_async_copy(act_all.at[zs[k]], right_a.at[zs[k], pl.ds(0, rows)], load_sem.at[k])
        load.start()
        loads.append((k, load))
    w_sources = []
    for k in FAR_FIRST:
        w_sources += [down.at[zs[k]], up.at[zs[k]]]
    w_sources += [proj.at[zs[k]] for k in FAR_FIRST]
    weights = Stream(w_slots, w_sem, w_sources)
    hidden = Stream(hid_slots, hid_sem, [hid_all.at[zs[k]] for k in FAR_FIRST])
    saved = Stream(s_slots, s_sem, [s_all.at[zs[k]] for k in FAR_FIRST])
    attentions = Stream(att_slots, att_sem, [att_all.at[zs[k]] for k in FAR_FIRST])
    for stream in (weights, hidden, saved, attentions):
        stream.ensure(1)

    def weight_grad(name, k, buffer, *lefts):
        unit = units[name]
        if len(lefts) == 1:
            ranges = [(0, d_model, dot_plain(left[lefts[0]], buffer[zs[k]]))]
        else:
            first = dot_plain(left[lefts[0]], buffer[zs[k], :, 0:qkv_end])
            last = dot_plain(left[lefts[1]], buffer[zs[k], :, out_start:])
            edge = jnp.where(
                columns[:, out_start:qkv_end] < 3 * head_cols, first[:, out_start:], last[:, : qkv_end - out_start]
            )
            ranges = [
                (0, out_start, first[:, :out_start]), (out_start, qkv_end, edge),
                (qkv_end, d_model, last[:, qkv_end - out_start :]),
            ]
        for start, stop, part in ranges:
            low = part.astype(bf16)
            for block in range(4):
                unit.total[k, block // 2, block % 2, :, start:stop] = low[block * cut : (block + 1) * cut]

    late = {}

    def late_load(src, dst, slot):
        late[slot] = pltpu.make_async_copy(src, dst, load_sem.at[slot])
        late[slot].start()

    def late_wait(slot):
        late[slot].wait()

    def put_row(row, values):
        for z in range(4):
            row_parts[z, row : row + 1, :] = values

    small = {}
    axes = ((core, 6), ((place.wide(0, 1, 0), place.z), 9), ((place.wide(1, 0, 0), place.z), 12))
    own_time = (
        time_sums.at[place.y, place.x, place.c], time_sums.at[place.y, place.x], time_sums.at[place.y]
    )
    own_trow = (trow_out.at[place.y, place.x, place.c], trow_out.at[place.y, place.x], trow_out.at[place.y])

    def give(slot, src, dst, peer):
        small[slot] = remote(src, dst, small_send.at[slot], small_recv.at[slot], peer)

    def small_begin():
        table_low[...] = table_parts[...].astype(bf16)
        for k in (1, 2, 3):
            peer = (place.wide(), zs[k])
            give(k - 1, row_parts.at[zs[k]], rows_z.at[k - 1], peer)
            give(k + 2, table_low.at[zs[k]], table_z.at[k - 1], peer)
        return ((9.0, small_along_z),)

    def small_along_z():
        for slot in range(6):
            small[slot].wait_recv()
        totals = row_parts[place.z]
        at_row = lax.broadcasted_iota(jnp.int32, (16, d_model), 0)
        times = jnp.where(at_row == place.z, totals[7:8, :], 0.0)
        tables = table_parts[place.z]
        for k in (1, 2, 3):
            part = rows_z[k - 1]
            times = jnp.where(at_row == place.along_z(4 - k), part[7:8, :], times)
            totals = totals + part
            tables = tables + table_z[k - 1].astype(f32)
        row_sums[...] = totals
        table_sums[...] = tables
        time_sums[place.y, place.x, place.c] = times.astype(bf16)
        small_across(0)
        return ((4.0, functools.partial(small_step, 0)),)

    def small_across(axis):
        peer, slot = axes[axis]
        give(slot, row_sums, rows_w.at[axis], peer)
        table_low[place.z] = table_sums[...].astype(bf16)
        give(slot + 1, table_low.at[place.z], table_w.at[axis], peer)
        give(slot + 2, own_time[axis], own_time[axis], peer)

    def small_step(axis):
        slot = axes[axis][1]
        for at in range(slot, slot + 3):
            small[at].wait_recv()
            small[at].wait_send()
        row_sums[...] = row_sums[...] + rows_w[axis]
        table_sums[...] = table_low[place.z].astype(f32) + table_w[axis].astype(f32)
        if axis < 2:
            small_across(axis + 1)
            return ((5.0, functools.partial(small_step, axis + 1)),)
        late_wait(6)
        times = jnp.where(columns < 3 * head_cols, time_sums[...].reshape(128, d_model), 0)
        part = dot_turned(times, s_slots[0, 0:cut]).reshape(8, 16, cut)[:, :8]
        late_wait(8)
        part = part + trow_kept[...]
        trow_out[place.y, place.x, place.c] = part
        if last_layer:
            return None
        for k in (1, 2, 3):
            give(14 + k, own_trow[0], trow_z.at[k - 1], (place.wide(), zs[k]))
        return ((6.0, trow_along_z),)

    def trow_along_z():
        for slot in (15, 16, 17):
            small[slot].wait_recv()
            small[slot].wait_send()
        here = trow_out[place.y, place.x, place.c] + trow_z[0] + trow_z[1] + trow_z[2]
        trow_out[place.y, place.x, place.c] = here
        give(18, own_trow[0], own_trow[0], axes[0][0])
        return ((4.0, functools.partial(trow_step, 0)),)

    def trow_step(axis):
        small[18 + axis].wait_recv()
        small[18 + axis].wait_send()
        if axis < 2:
            give(19 + axis, own_trow[axis + 1], own_trow[axis + 1], axes[axis + 1][0])
            return ((5.0, functools.partial(trow_step, axis + 1)),)

    def close_rows():
        unit, scale = unit_rows(hid_slots[0])
        from_norm = norm_back(acc_buf[...], unit, scale, gains[0:1, :])
        put_row(0, column_sums(acc_buf[...] * unit))
        put_row(2, column_sums(acc_buf[...]))
        grad_out[...] = grad_out[...] + from_norm
        late_load(time_weight, s_slots.at[0, pl.ds(0, cut)], 6)
        late_load(trow_in.at[place.y, place.x, place.c], trow_kept, 8)
        late_load(pick_in, s_slots.at[1, :, pl.ds(0, 4 * rows)], 7)
        following = [(0.0, small_begin)]
        if not last_layer:
            low_buf[0] = grad_out[...].astype(bf16)
            line.begin(low_buf.at[0])
            keep.append(pltpu.make_async_copy(low_buf.at[0], rows_all.at[place.z], load_sem.at[4]))
            keep[0].start()
            following += [(14.0 * far_off, functools.partial(line.arrive, far_off)) for far_off in (1, 2, 3)]
        return following

    def compute():
        low_buf[0] = grad[...].astype(bf16)
        put_row(5, column_sums(low_buf[0].astype(f32)))
        make_left(0, low_buf[0])
        left_ready(0)
        for at, k in enumerate(FAR_FIRST):
            loads[at][1].wait()
            right_copies["down", k].wait_recv()
            weight_grad("down", k, right_a, 0)
            yield 1.8, [(units["down"], k)]
            w = weights.take(2 * at)
            hid = hidden.take(at)
            act_grad = dot_plain(low_buf[0], w[...])
            hid_grad = (act_grad * gelu_slope(hid[...])).astype(bf16)
            right_b[zs[k], 0:rows] = hid_grad
            weights.ensure(2 * at + 2)
            hidden.ensure(at + 2)
            give_right("up", 1, k, right_b.at[zs[k], pl.ds(0, rows)], right_b)
            row_parts[zs[k], 6:7, :] = column_sums(hid_grad.astype(f32))
            yield 2.5, []
            w = weights.take(2 * at + 1)
            part = dot_turned(right_b[zs[k], 0:rows], w[...])
            acc_buf[...] = part if at == 0 else acc_buf[...] + part
            weights.ensure(2 * at + 3)
            yield 1.5, []
        for k in FAR_FIRST:
            right_copies["down", k].wait_send()
        pl.semaphore_signal(credit, inc=1, device_id=core, device_id_type=MESH)
        unit, scale = unit_rows(mid_in[...])
        make_left(1, (unit * gains[1:2, :] + shifts[1:2, :]).astype(bf16))
        from_norm = norm_back(acc_buf[...], unit, scale, gains[1:2, :])
        put_row(1, column_sums(acc_buf[...] * unit))
        put_row(3, column_sums(acc_buf[...]))
        grad_out[...] = grad[...] + from_norm
        low_buf[0] = grad_out[...].astype(bf16)
        put_row(4, column_sums(low_buf[0].astype(f32)))
        late_load(x_in, hid_slots.at[0], 5)
        yield 4.0, []
        left_ready(1)
        right_copies["up", FAR_FIRST[0]].wait_recv()
        weight_grad("up", FAR_FIRST[0], right_b, 1)
        yield 1.5, [(units["up"], FAR_FIRST[0])]
        make_left(2, low_buf[0])
        late_wait(5)
        unit, scale = unit_rows(hid_slots[0])
        make_left(3, (unit * gains[0:1, :] + shifts[0:1, :]).astype(bf16))
        left_ready(2)
        left_ready(3)
        pl.semaphore_wait(credit, 1)
        yield 4.0, []
        head_of = column_ids(head_cols) // HEAD_DIM
        score_scale = HEAD_DIM ** (-0.5)
        for at, k in enumerate(FAR_FIRST):
            if at:
                right_copies["up", k].wait_recv()
                weight_grad("up", k, right_b, 1)
                yield 1.5, [(units["up"], k)]
            w = weights.take(8 + at)
            s = saved.take(at)
            attention_slot = attentions.take(at)
            low_buf[1, :, out_start:] = dot_plain(low_buf[0], w[:, out_start:]).astype(bf16)
            mixed_grad = low_buf[1, :, 3 * head_cols :]
            q = s[:, 0:head_cols]
            key = s[:, head_cols : 2 * head_cols]
            v = s[:, 2 * head_cols : 3 * head_cols]
            head_grads[...] = jnp.zeros_like(head_grads)

            def one_head(head, carry):
                here = head_of == head
                attention = attention_slot[head]
                own_grad = jnp.where(here, mixed_grad, 0)
                dot_back = dot_turned(own_grad, v)
                both = attention * dot_back
                score_low = (both - attention * jnp.sum(both, axis=-1, keepdims=True)).astype(bf16)
                first_row = pl.multiple_of(head * GRID, GRID)
                table_parts[zs[k], pl.ds(first_row, GRID), :] = fold_window(score_low.astype(f32))
                head_grads[0] += dot_plain(score_low, jnp.where(here, key, 0))
                head_grads[1] += dot_rows(score_low, jnp.where(here, q, 0))
                head_grads[2] += dot_rows(attention.astype(bf16), own_grad)
                return carry

            lax.fori_loop(0, 2, one_head, 0)
            yield 2.5, []
            lax.fori_loop(2, 4, one_head, 0)
            here = right_a.at[zs[k]]
            here[0:rows, 0:head_cols] = (head_grads[0] * score_scale).astype(bf16)
            here[0:rows, head_cols : 2 * head_cols] = (head_grads[1] * score_scale).astype(bf16)
            here[0:rows, 2 * head_cols : 3 * head_cols] = head_grads[2].astype(bf16)
            here[0:rows, 3 * head_cols :] = s[:, 3 * head_cols :]
            give_right("proj", 2, k, right_a.at[zs[k], pl.ds(0, rows)], right_a)
            saved.ensure(at + 2)
            attentions.ensure(at + 2)
            yield 2.5, []
            own = right_a[zs[k], 0:rows]
            row_parts[zs[k], 7:8, :] = column_sums(own.astype(f32))
            own = jnp.where(columns < 3 * head_cols, own, 0)
            part = dot_turned(own[:, :qkv_end], w[:, :qkv_end])
            acc_buf[...] = part if at == 0 else acc_buf[...] + part
            weights.ensure(8 + at + 2)
            yield 1.5, []
        yield 2.0, [], None, close_rows()
        for k in FAR_FIRST:
            right_copies["proj", k].wait_recv()
            yield 0.2, [], (units["down"], k)
            units["down"].settle((4 + k, 8 + k, 12 + k, 16 + k, 19 + k))
            weight_grad("proj", k, right_a, 3, 2)
            yield 2.0, [(units["proj"], k)]

    first_events = []
    if last_layer:
        first_events = [(20.0 * far_off, functools.partial(line.arrive, far_off)) for far_off in (1, 2, 3)]
    merge_steps(compute(), first_events, 10.7, 12.0 if last_layer else 12.0, 12.0)
    for slot in range(6):
        small[slot].wait_send()
    for (name, k), copy in right_copies.items():
        if name != "down":
            copy.wait_send()
    for at in (2, 3):
        for copy in left_copies[at]:
            copy.wait_send()
    line.finish()
    keep[0].wait()
    gathered = pltpu.make_async_copy(rows_all, right_b.at[:, pl.ds(0, rows)], load_sem.at[4])
    gathered.start()
    gathered.wait()
    late_wait(7)
    total = dot_plain(s_slots[1, :, 0:rows], right_b[0, 0:rows])
    for z in range(1, 4):
        total = total + dot_plain(s_slots[1, :, z * rows : (z + 1) * rows], right_b[z, 0:rows])
    rows_out[...] = total.astype(bf16)


def merge_steps(compute, events, links, late, follow):
    clock, link_free = 0.0, 0.0
    events = list(events)

    def run_first():
        events.sort(key=lambda item: item[0])
        at, step = events.pop(0)
        for delay, following in step() or ():
            events.append((max(clock, at) + delay, following))
        return max(clock, at)

    while True:
        while events and min(item[0] for item in events) <= clock:
            clock = run_first()
        made = next(compute, None)
        if made is None:
            break
        clock += made[0]
        for unit, k in made[1]:
            unit.first_stage(k)
            start = max(clock, link_free)
            link_free = start + links
            events.append((start + late, functools.partial(scatter_step, unit, k, follow)))
        if len(made) > 2 and made[2]:
            unit, k = made[2]
            while k not in unit.closed:
                clock = run_first()
        if len(made) > 3:
            events += [(clock + delay, step) for delay, step in made[3]]
    while events:
        clock = run_first()


def backward_layer(last_layer, grad, saved, gains, shifts, trow, pick, time_weight, rows_in, weights):
    x_in, mid_in, s_all, att_all, hid_all, act_all = saved
    proj, up, down = weights
    rows, d_model = grad.shape
    cut = d_model // 8
    any_space = pl.BlockSpec(memory_space=pl.ANY)
    vmem = pl.BlockSpec(memory_space=pltpu.VMEM)
    block = jax.ShapeDtypeStruct((cut, d_model), f32)
    out_shape = [
        block,
        block,
        block,
        jax.ShapeDtypeStruct((rows, d_model), f32),
        jax.ShapeDtypeStruct((rows, d_model), bf16),
        jax.ShapeDtypeStruct((8, d_model), f32),
        jax.ShapeDtypeStruct((4 * GRID, 512), f32),
        jax.ShapeDtypeStruct((2, 2, 2, 16, d_model), bf16),
        jax.ShapeDtypeStruct((2, 2, 2, 8, 8, cut), f32),
        jax.ShapeDtypeStruct((4, rows, d_model), bf16),
    ]
    dma = pltpu.SemaphoreType.DMA
    scratch = [
        pltpu.VMEM((4, 2, 2, cut, d_model), bf16),
        pltpu.VMEM((4, 2, 2, cut, d_model), bf16),
        pltpu.VMEM((3, 4, 2, cut, d_model), bf16),
        pltpu.VMEM((3, 4, cut, d_model), bf16),
        pltpu.VMEM((3, 3, cut, d_model), bf16),
        pltpu.VMEM((4, 2 * rows, d_model), bf16),
        pltpu.VMEM((4, 2 * rows, d_model), bf16),
        pltpu.VMEM((4, 4 * cut, 2 * rows), bf16),
        pltpu.VMEM((2, d_model, rows), bf16),
        pltpu.VMEM((2, d_model, d_model), bf16),
        pltpu.VMEM((2, rows, d_model), bf16),
        pltpu.VMEM((2, 4, rows, rows), f32),
        pltpu.VMEM((2, rows, d_model), f32),
        pltpu.VMEM((rows, d_model), f32),
        pltpu.VMEM((2, rows, d_model), bf16),
        pltpu.VMEM((3, rows, d_model // 4), f32),
        pltpu.VMEM((4, 8, d_model), f32),
        pltpu.VMEM((3, 8, d_model), f32),
        pltpu.VMEM((3, 8, d_model), f32),
        pltpu.VMEM((4, 4 * GRID, 512), f32),
        pltpu.VMEM((4, 4 * GRID, 512), bf16),
        pltpu.VMEM((3, 4 * GRID, 512), bf16),
        pltpu.VMEM((3, 4 * GRID, 512), bf16),
        pltpu.VMEM((3, 8, 8, cut), f32),
        pltpu.VMEM((8, 8, cut), f32),
        dma((21,)),
        dma((21,)),
        dma((3, SCATTER_SEMS)),
        dma((3, SCATTER_SEMS)),
        dma((4, 4)),
        dma((4, 4)),
        dma((LINE_SEMS,)),
        dma((LINE_SEMS,)),
        dma((2,)),
        dma((2,)),
        dma((2,)),
        dma((2,)),
        dma((9,)),
        pltpu.SemaphoreType.REGULAR,
    ]
    return pl.pallas_call(
        functools.partial(backward_kernel, last_layer),
        out_shape=out_shape,
        in_specs=[vmem] * 4 + [any_space] * 12,
        out_specs=[vmem] * 9 + [any_space],
        scratch_shapes=scratch,
        compiler_params=pltpu.CompilerParams(
            collective_id=1 if last_layer else 2, has_side_effects=True, vmem_limit_bytes=63 * 2**20
        ),
        name="backward_last" if last_layer else "backward_first",
    )(
        grad, mid_in, gains, shifts, trow, x_in, pick, time_weight, rows_in, s_all, att_all, hid_all, act_all,
        proj, up, down,
    )


def shards_plain(
    tokens,
    cotangent,
    segment_ids,
    patch_pos,
    time_index,
    time_table,
    norm_gain,
    norm_shift,
    attn_weight,
    out_weight,
    qkv_bias,
    out_bias,
    mlp_weight,
    up_bias,
    rel_table,
):
    image_count = time_index.shape[0]
    layer_count = attn_weight.shape[0]
    narrow_at = lax.axis_index("narrow")
    wide_at = lax.axis_index("wide")
    wide_size = lax.axis_size("wide")
    own_rows = tokens.shape[0]
    in_rows, cols = attn_weight.shape[2:]
    image_local = segment_ids % image_count
    grid_slot = image_local * PATCHES + patch_pos
    own_slots = narrow_at * own_rows + jnp.arange(own_rows, dtype=jnp.int32)
    pick_in = (own_slots[:, None] == grid_slot[None, :]).astype(bf16)
    own_grid = lax.dynamic_slice_in_dim(grid_slot, narrow_at * own_rows, own_rows)
    pick_out = (own_grid[:, None] == jnp.arange(grid_slot.shape[0], dtype=jnp.int32)[None, :]).astype(bf16)

    def to_images(rows):
        every = lax.all_gather(rows, "narrow", axis=0, tiled=True)
        return jnp.dot(pick_in, every, preferred_element_type=f32)

    def to_rows(rows):
        every = lax.all_gather(rows, "narrow", axis=0, tiled=True)
        return jnp.dot(pick_out, every, preferred_element_type=f32).astype(bf16)

    steps_all = lax.all_gather(time_index, "wide", axis=0, tiled=True)
    step_hot = (steps_all[:, None] == jnp.arange(time_table.shape[0], dtype=jnp.int32)[None, :]).astype(bf16)
    time_rows = jnp.dot(step_hot, time_table, preferred_element_type=f32).astype(bf16)
    time_slice = lax.dynamic_slice_in_dim(time_rows, wide_at * in_rows, in_rows, axis=1)
    time_weight = attn_weight[:, 3:6]
    time_share = jnp.einsum("id,ljdc->ljic", time_slice, time_weight, preferred_element_type=f32)
    time_share = lax.psum_scatter(time_share, "wide", scatter_dimension=2, tiled=True)
    time_share = lax.all_gather(time_share, "narrow", axis=3, tiled=True)
    time_part = lax.dynamic_index_in_dim(time_share, narrow_at, axis=2, keepdims=False)

    tables = lax.all_gather(rel_table, "narrow", axis=1, tiled=True)
    qkv_bias_all = lax.all_gather(qkv_bias, "narrow", axis=2, tiled=True)
    up_bias_all = lax.all_gather(up_bias, "narrow", axis=1, tiled=True)

    def layer_params(at):
        return (norm_gain[at], norm_shift[at], qkv_bias_all[at], out_bias[at])

    weights = []
    for at in range(layer_count):
        packed = jnp.concatenate([attn_weight[at, 0], attn_weight[at, 1], attn_weight[at, 2], out_weight[at]], axis=1)
        weights.append((gather_unit(packed), gather_unit(mlp_weight[at, 0]), gather_unit(mlp_weight[at, 1])))

    residual = to_images(tokens)
    kept = []
    for at in range(layer_count):
        pairs = pair_bias(tables[at])
        middle, attn_saved = attention_forward(residual, weights[at][0], time_part[at], layer_params(at), pairs)
        residual, mlp_saved = mlp_forward(middle, weights[at][1], weights[at][2], layer_params(at), up_bias_all[at])
        kept.append((attn_saved, mlp_saved))
    block_output = to_rows(residual.astype(bf16))
    gradient = to_images(cotangent)
    attn_grads, out_grads, mlp_grads = [], [], []
    time_sums, small = [], []
    for at in reversed(range(layer_count)):
        attn_saved, mlp_saved = kept[at]
        grad_mid, up_grad, down_grad, mlp_small = mlp_backward(
            gradient, weights[at][1], weights[at][2], layer_params(at), mlp_saved
        )
        mlp_grads.insert(0, jnp.stack([scatter_unit(up_grad), scatter_unit(down_grad)]))
        gradient, proj_grad, sums, table_grad, attn_small = attention_backward(
            grad_mid, weights[at][0], layer_params(at), attn_saved
        )
        packed = scatter_unit(proj_grad)
        attn_grads.insert(0, jnp.stack([packed[:, j * cols : (j + 1) * cols] for j in range(3)]))
        out_grads.insert(0, packed[:, 3 * cols :])
        time_sums.insert(0, sums)
        small.insert(
            0,
            (
                jnp.stack([attn_small[0], mlp_small[0]]),
                jnp.stack([attn_small[1], mlp_small[1]]),
                jnp.stack([attn_small[2], mlp_small[2]]),
                jnp.stack([sums[0], sums[2]]),
                mlp_small[3],
                table_grad,
            ),
        )
    input_grad = to_rows(gradient.astype(bf16))

    def stacked(index_at):
        return jnp.stack([entry[index_at] for entry in small])

    totals = lax.psum(tuple(stacked(index_at) for index_at in range(6)), ("wide", "narrow"))

    def own_part(array, axis):
        size = array.shape[axis] // lax.axis_size("narrow")
        return lax.dynamic_slice_in_dim(array, narrow_at * size, size, axis=axis)

    time_low = jnp.stack(time_sums).astype(bf16)
    time_all = lax.all_gather(time_low, ("wide", "narrow"), axis=0, tiled=False)
    time_own = own_part(time_all, 3)
    time_weight_grad = jnp.einsum("id,iljc->ljdc", time_slice, time_own, preferred_element_type=f32)
    trow_share = jnp.einsum("iljc,ljdc->id", time_own, time_weight, preferred_element_type=f32)
    trow_share = lax.psum(trow_share, "narrow")
    trow = lax.all_gather(trow_share, "wide", axis=1, tiled=True)
    time_grad = jnp.einsum("is,id->sd", step_hot.astype(f32), trow, precision=highest)
    attn_grad = jnp.concatenate([jnp.stack(attn_grads).astype(f32), time_weight_grad], axis=1)
    return (
        block_output,
        input_grad,
        time_grad,
        totals[0],
        totals[1],
        attn_grad,
        jnp.stack(out_grads).astype(f32),
        own_part(totals[3], 2),
        totals[2],
        jnp.stack(mlp_grads).astype(f32),
        own_part(totals[4], 1),
        own_part(totals[5], 1),
    )


def bias_windows(tables):
    layers, heads = tables.shape[:2]
    near = jnp.arange(GRID, dtype=jnp.int32)
    span = jnp.arange(SPAN, dtype=jnp.int32)
    steps = (span[None, :, None] == near[:, None, None] - near[None, None, :] + (GRID - 1)).astype(f32)
    grid = tables.reshape(layers, heads, SPAN, SPAN)[:, :, ::-1]
    windows = jnp.einsum("lhab,xby->lhxay", grid, steps, precision=highest)
    windows = windows.reshape(layers, heads * GRID, SPAN * GRID)
    return jnp.pad(windows, ((0, 0), (0, 0), (0, 512 - SPAN * GRID)))


def fold_windows(windows):
    layers, heads = windows.shape[0], windows.shape[1] // GRID
    near = jnp.arange(GRID, dtype=jnp.int32)
    span = jnp.arange(SPAN, dtype=jnp.int32)
    steps = (span[None, :, None] == near[:, None, None] - near[None, None, :] + (GRID - 1)).astype(f32)
    grid = windows[:, :, : SPAN * GRID].reshape(layers, heads, GRID, SPAN, GRID)
    tables = jnp.einsum("lhxay,xby->lhab", grid, steps, precision=highest)
    return tables[:, :, ::-1].reshape(layers, heads, SPAN * SPAN)


def shards(
    tokens,
    cotangent,
    segment_ids,
    patch_pos,
    time_index,
    time_table,
    norm_gain,
    norm_shift,
    attn_weight,
    out_weight,
    qkv_bias,
    out_bias,
    mlp_weight,
    up_bias,
    rel_table,
):
    image_count = time_index.shape[0]
    layer_count = attn_weight.shape[0]
    in_rows, cols = attn_weight.shape[2:]
    by_links = lax.axis_size("wide") == 8 and lax.axis_size("narrow") == 4 and in_rows % 16 == 0
    if not by_links:
        return shards_plain(
            tokens, cotangent, segment_ids, patch_pos, time_index, time_table, norm_gain, norm_shift,
            attn_weight, out_weight, qkv_bias, out_bias, mlp_weight, up_bias, rel_table,
        )
    narrow_at = lax.axis_index("narrow")
    wide_at = lax.axis_index("wide")
    own_rows, d_model = tokens.shape
    image_local = segment_ids % image_count
    grid_slot = image_local * PATCHES + patch_pos
    own_slots = narrow_at * own_rows + jnp.arange(own_rows, dtype=jnp.int32)
    pick_in = (own_slots[:, None] == grid_slot[None, :]).astype(bf16)
    own_grid = lax.dynamic_slice_in_dim(grid_slot, narrow_at * own_rows, own_rows)
    pick_out = (own_grid[:, None] == jnp.arange(grid_slot.shape[0], dtype=jnp.int32)[None, :]).astype(bf16)

    step_own = (time_index[:, None] == jnp.arange(time_table.shape[0], dtype=jnp.int32)[None, :]).astype(bf16)
    time_own = jnp.dot(step_own, time_table, preferred_element_type=f32).astype(bf16)
    digits = jnp.stack([time_index // 32, time_index % 32]).astype(bf16)
    digits = jnp.pad(digits, ((0, 16 - image_count - 2), (0, d_model - image_count)))
    time_own = jnp.concatenate([time_own, digits], axis=0)
    time_weight = attn_weight[:, 3:6]
    time_packed = jnp.concatenate(
        [time_weight[:, 0], time_weight[:, 1], time_weight[:, 2], jnp.zeros_like(time_weight[:, 0])], axis=2
    )
    qkv_packed = jnp.concatenate(
        [qkv_bias[:, 0], jnp.zeros_like(qkv_bias[:, 0]), qkv_bias[:, 1], jnp.zeros_like(qkv_bias[:, 0])], axis=1
    )
    small_own = jnp.pad(jnp.concatenate([up_bias, qkv_packed], axis=0), ((0, 8 - 2 * layer_count), (0, 0)))
    packed_own = [
        jnp.concatenate([attn_weight[at, 0], attn_weight[at, 1], attn_weight[at, 2], out_weight[at]], axis=1)
        for at in range(layer_count)
    ]
    wholes, saved, (block_low, gradient, time_all, time_sel) = forward_all(
        tokens,
        cotangent,
        pick_in,
        time_own,
        time_packed,
        bias_windows(rel_table),
        small_own,
        norm_gain.reshape(-1, d_model),
        norm_shift.reshape(-1, d_model),
        out_bias.reshape(-1, d_model),
        packed_own,
        mlp_weight,
    )
    time_all = time_all.reshape(8, 16, d_model)
    steps_all = time_all[:, image_count : image_count + 2, :image_count].astype(f32)
    steps_all = (steps_all[:, 0] * 32 + steps_all[:, 1]).astype(jnp.int32).reshape(-1)
    step_hot = (steps_all[:, None] == jnp.arange(time_table.shape[0], dtype=jnp.int32)[None, :]).astype(f32)
    time_slice = time_sel.reshape(8, 16, in_rows)[:, :image_count].reshape(-1, in_rows)

    attn_grads, out_grads, mlp_grads = [], [], []
    row_sums, table_sums, time_sums = [], [], []
    block_output = None
    trow = jnp.zeros((2, 2, 2, 8, 8, in_rows), f32)
    for at in reversed(range(layer_count)):
        last_layer = at == layer_count - 1
        packed, up_part, down_part, gradient, moved, rows_part, tables_part, times_part, trow, _ = backward_layer(
            last_layer, gradient, saved[at], norm_gain[at], norm_shift[at], trow, pick_out, time_packed[at], block_low,
            wholes[3 * at : 3 * at + 3],
        )
        if last_layer:
            block_output = moved
        mlp_grads.insert(0, jnp.stack([up_part, down_part]))
        attn_grads.insert(0, jnp.stack([packed[:, j * cols : (j + 1) * cols] for j in range(3)]))
        out_grads.insert(0, packed[:, 3 * cols :])
        row_sums.insert(0, rows_part)
        table_sums.insert(0, tables_part)
        time_sums.insert(0, times_part.reshape(8, 16, d_model)[:, :image_count].reshape(-1, d_model))
    input_grad = moved
    row_sums = jnp.stack(row_sums)
    table_grad = fold_windows(jnp.stack(table_sums))
    time_weight_grad = jnp.einsum("id,lic->ldc", time_slice, jnp.stack(time_sums), preferred_element_type=f32)
    time_weight_grad = jnp.stack([time_weight_grad[:, :, j * cols : (j + 1) * cols] for j in range(3)], axis=1)
    trow = trow.reshape(8, 8, 8, in_rows)[:, :, :image_count].transpose(1, 2, 0, 3).reshape(-1, d_model)
    time_grad = jnp.einsum("is,id->sd", step_hot, trow, precision=highest)
    attn_grad = jnp.concatenate([jnp.stack(attn_grads), time_weight_grad], axis=1)
    qkv_bias_grad = jnp.stack([row_sums[:, 7, :cols], row_sums[:, 7, 2 * cols : 3 * cols]], axis=1)
    return (
        block_output,
        input_grad,
        time_grad,
        row_sums[:, 0:2],
        row_sums[:, 2:4],
        attn_grad,
        jnp.stack(out_grads),
        qkv_bias_grad,
        row_sums[:, 4:6],
        jnp.stack(mlp_grads),
        row_sums[:, 6],
        table_grad,
    )


def solution(mesh):
    return jax.shard_map(
        shards,
        mesh=mesh,
        in_specs=(
            P(("wide", "narrow"), None),
            P(("wide", "narrow"), None),
            P("wide"),
            P("wide"),
            P("wide"),
            P(),
            P(),
            P(),
            P(None, None, "wide", "narrow"),
            P(None, "wide", "narrow"),
            P(None, None, "narrow"),
            P(),
            P(None, None, "wide", "narrow"),
            P(None, "narrow"),
            P(None, "narrow", None),
        ),
        out_specs=(
            P(("wide", "narrow"), None),
            P(("wide", "narrow"), None),
            P(),
            P(),
            P(),
            P(None, None, "wide", "narrow"),
            P(None, "wide", "narrow"),
            P(None, None, "narrow"),
            P(),
            P(None, None, "wide", "narrow"),
            P(None, "narrow"),
            P(None, "narrow", None),
        ),
        check_vma=False,
    )
```

```python
import functools
import math

import jax
import jax.numpy as jnp
from jax import lax
from jax.experimental import pallas as pl
from jax.experimental.pallas import tpu as pltpu
from jax.sharding import PartitionSpec as P

HEAD_DIM = 72
GRID = 16
PATCHES = GRID * GRID
SPAN = 2 * GRID - 1


eps_norm = 1e-06
highest = lax.Precision.HIGHEST
f32 = jnp.float32
bf16 = jnp.bfloat16
ROWS_AXES = ("narrow", "wide")
MESH = pl.DeviceIdType.MESH


def layer_norm(values, norm_gain, norm_shift):
    average = jnp.mean(values, axis=-1, keepdims=True)
    centred = values - average
    variance = jnp.mean(centred * centred, axis=-1, keepdims=True)
    scale = lax.rsqrt(variance + eps_norm)
    unit = centred * scale
    return unit * norm_gain + norm_shift, unit, scale


def layer_norm_back(grad, unit, scale, norm_gain):
    weighted = grad * norm_gain
    first = jnp.mean(weighted, axis=-1, keepdims=True)
    second = jnp.mean(weighted * unit, axis=-1, keepdims=True)
    from_norm = scale * (weighted - first - unit * second)
    return from_norm, jnp.sum(grad * unit, axis=0), jnp.sum(grad, axis=0)


def offset_onehot():
    near = jnp.arange(GRID, dtype=jnp.int32)
    span = jnp.arange(SPAN, dtype=jnp.int32)
    return (span[None, None, :] == near[:, None, None] - near[None, :, None] + (GRID - 1)).astype(f32)


def pair_bias(bias_table):
    steps_hot = offset_onehot()
    head_count = bias_table.shape[0]
    table_grid = bias_table.reshape(head_count, SPAN, SPAN)
    row_part = jnp.einsum("ixa,hab->hixb", steps_hot, table_grid, precision=highest)
    pairs = jnp.einsum("jyb,hixb->hijxy", steps_hot, row_part, precision=highest)
    return pairs.reshape(head_count, PATCHES, PATCHES)


def fold_bias_grad(pair_grad):
    steps_hot = offset_onehot()
    head_count = pair_grad.shape[0]
    grid_grad = pair_grad.reshape(head_count, GRID, GRID, GRID, GRID)
    col_part = jnp.einsum("jyb,hijxy->hixb", steps_hot, grid_grad, precision=highest)
    table_grad = jnp.einsum("ixa,hixb->hab", steps_hot, col_part, precision=highest)
    return table_grad.reshape(head_count, SPAN * SPAN)


def gather_unit(piece):
    parts = lax.axis_size("narrow")
    whole = lax.all_gather(piece, ROWS_AXES, axis=0, tiled=True)
    return whole.reshape(parts, whole.shape[0] // parts, whole.shape[1])


def scatter_unit(grads):
    flat = grads.astype(bf16).reshape(-1, grads.shape[-1])
    return lax.psum_scatter(flat, ROWS_AXES, scatter_dimension=0, tiled=True)


def to_heads(values):
    parts, rows, cols = values.shape
    split = values.reshape(parts, rows, cols // HEAD_DIM, HEAD_DIM)
    return split.transpose(0, 2, 1, 3).reshape(-1, rows, HEAD_DIM)


def from_heads(values, parts):
    heads, rows, _ = values.shape
    split = values.reshape(parts, heads // parts, rows, HEAD_DIM).transpose(0, 2, 1, 3)
    return split.reshape(parts, rows, -1)


def attention_forward(residual, proj, time_part, params, pairs):
    norm_gain, norm_shift, qkv_bias, out_bias = params
    parts = proj.shape[0]
    cols = proj.shape[2] // 4
    normed, unit, scale = layer_norm(residual, norm_gain[0], norm_shift[0])
    normed_low = normed.astype(bf16)
    spatial = jnp.einsum("rd,zdc->zrc", normed_low, proj[:, :, : 3 * cols], preferred_element_type=f32)
    offsets = time_part + jnp.stack([qkv_bias[0], jnp.zeros_like(qkv_bias[0]), qkv_bias[1]])
    offsets = offsets.reshape(3, parts, 1, cols)
    queries, key_rows, value_rows = (
        to_heads((spatial[:, :, j * cols : (j + 1) * cols] + offsets[j]).astype(bf16)) for j in range(3)
    )
    scores = jnp.einsum("hqd,hkd->hqk", queries, key_rows, preferred_element_type=f32)
    scores = scores * HEAD_DIM ** (-0.5) + pairs
    attention = jax.nn.softmax(scores, axis=-1)
    attention_low = attention.astype(bf16)
    mixed = jnp.einsum("hqk,hkd->hqd", attention_low, value_rows, preferred_element_type=f32)
    mixed_low = from_heads(mixed.astype(bf16), parts)
    branch = jnp.einsum("zrc,zdc->rd", mixed_low, proj[:, :, 3 * cols :], preferred_element_type=f32)
    middle = residual + (branch + out_bias[0])
    saved = (normed_low, unit, scale, queries, key_rows, value_rows, attention, mixed_low)
    return middle, saved


def mlp_forward(middle, up, down, params, up_bias):
    norm_gain, norm_shift, qkv_bias, out_bias = params
    parts = up.shape[0]
    normed, unit, scale = layer_norm(middle, norm_gain[1], norm_shift[1])
    normed_low = normed.astype(bf16)
    hidden = jnp.einsum("rd,zdc->zrc", normed_low, up, preferred_element_type=f32)
    hidden = hidden + up_bias.reshape(parts, 1, -1)
    activated = jax.nn.gelu(hidden, approximate=True).astype(bf16)
    branch = jnp.einsum("zrc,zdc->rd", activated, down, preferred_element_type=f32)
    return middle + (branch + out_bias[1]), (normed_low, unit, scale, hidden, activated)


def mlp_backward(gradient, up, down, params, saved):
    norm_gain = params[0]
    normed_low, unit, scale, hidden, activated = saved
    grad_low = gradient.astype(bf16)
    out_bias_grad = jnp.sum(grad_low.astype(f32), axis=0)
    down_grad = jnp.einsum("rd,zrc->zdc", grad_low, activated, preferred_element_type=f32)
    act_grad = jnp.einsum("rd,zdc->zrc", grad_low, down, preferred_element_type=f32)
    _, gelu_back = jax.vjp(lambda values: jax.nn.gelu(values, approximate=True), hidden)
    hidden_low = gelu_back(act_grad)[0].astype(bf16)
    up_bias_grad = jnp.sum(hidden_low.astype(f32), axis=1).reshape(-1)
    up_grad = jnp.einsum("rd,zrc->zdc", normed_low, hidden_low, preferred_element_type=f32)
    normed_grad = jnp.einsum("zrc,zdc->rd", hidden_low, up, preferred_element_type=f32)
    from_norm, gain_grad, shift_grad = layer_norm_back(normed_grad, unit, scale, norm_gain[1])
    return gradient + from_norm, up_grad, down_grad, (gain_grad, shift_grad, out_bias_grad, up_bias_grad)


def attention_backward(grad_mid, proj, params, saved):
    norm_gain = params[0]
    normed_low, unit, scale, queries, key_rows, value_rows, attention, mixed_low = saved
    parts = proj.shape[0]
    cols = proj.shape[2] // 4
    score_scale = HEAD_DIM ** (-0.5)
    mid_low = grad_mid.astype(bf16)
    out_bias_grad = jnp.sum(mid_low.astype(f32), axis=0)
    out_grad = jnp.einsum("rd,zrc->zdc", mid_low, mixed_low, preferred_element_type=f32)
    mixed_grad = jnp.einsum("rd,zdc->zrc", mid_low, proj[:, :, 3 * cols :], preferred_element_type=f32)
    mixed_grad = to_heads(mixed_grad.astype(bf16))
    dot_back = jnp.einsum("hqd,hkd->hqk", mixed_grad, value_rows, preferred_element_type=f32)
    score_grad = attention * (dot_back - jnp.sum(attention * dot_back, axis=-1, keepdims=True))
    score_low = score_grad.astype(bf16)
    table_grad = fold_bias_grad(score_low.astype(f32))
    query_grad = jnp.einsum("hqk,hkd->hqd", score_low, key_rows, preferred_element_type=f32) * score_scale
    key_grad = jnp.einsum("hqk,hqd->hkd", score_low, queries, preferred_element_type=f32) * score_scale
    value_grad = jnp.einsum("hqk,hqd->hkd", attention.astype(bf16), mixed_grad, preferred_element_type=f32)
    qkv_low = jnp.concatenate(
        [from_heads(item.astype(bf16), parts) for item in (query_grad, key_grad, value_grad)], axis=-1
    )
    spatial_grad = jnp.einsum("rd,zrc->zdc", normed_low, qkv_low, preferred_element_type=f32)
    proj_grad = jnp.concatenate([spatial_grad, out_grad], axis=-1)
    sums = jnp.sum(qkv_low.astype(f32), axis=1).reshape(parts, 3, cols).transpose(1, 0, 2).reshape(3, -1)
    normed_grad = jnp.einsum("zrc,zdc->rd", qkv_low, proj[:, :, : 3 * cols], preferred_element_type=f32)
    from_norm, gain_grad, shift_grad = layer_norm_back(normed_grad, unit, scale, norm_gain[0])
    return grad_mid + from_norm, proj_grad, sums, table_grad, (gain_grad, shift_grad, out_bias_grad)


class Place:
    def __init__(self):
        wide = lax.axis_index("wide")
        self.z = lax.axis_index("narrow")
        self.y, self.x, self.c = wide // 4, (wide // 2) % 2, wide % 2

    def wide(self, flip_y=0, flip_x=0, flip_c=0):
        y = 1 - self.y if flip_y else self.y
        x = 1 - self.x if flip_x else self.x
        c = 1 - self.c if flip_c else self.c
        return y * 4 + x * 2 + c

    def along_z(self, steps):
        return lax.rem(self.z + steps, 4)

    def peers(self):
        across = [(self.wide(1, 0, 0), self.z), (self.wide(0, 1, 0), self.z), (self.wide(0, 0, 1), self.z)]
        return across + [(self.wide(), self.along_z(k)) for k in (1, 2, 3)]

    def greet(self):
        barrier = pltpu.get_barrier_semaphore()
        for peer in self.peers():
            pl.semaphore_signal(barrier, inc=1, device_id=peer, device_id_type=MESH)
        pl.semaphore_wait(barrier, 6)


def unit_cut(unit, rows):
    low = rows // 32 * 16
    return low if unit % 2 == 0 else rows - low


class Line:
    def __init__(self, place, block, send, recv):
        self.place, self.block, self.send, self.recv = place, block, send, recv

    def copy(self, src, origin, step, slot):
        place = self.place
        return pltpu.make_async_remote_copy(
            src_ref=src, dst_ref=self.block(origin), send_sem=self.send.at[slot], recv_sem=self.recv.at[origin],
            device_id=(place.wide(), place.z + step), device_id_type=MESH,
        )

    def begin(self, own):
        z = self.place.z

        @pl.when(z < 3)
        def _():
            self.copy(own, z, 1, z).start()

        @pl.when(z > 0)
        def _():
            self.copy(own, z, -1, 4).start()

    def arrive(self, far, then=lambda origin: None):
        z = self.place.z
        for side, valid, room in ((-1, z - far >= 0, z < 3), (1, z + far <= 3, z > 0)):

            @pl.when(valid)
            def _(side=side, room=room):
                origin = z + side * far
                here = self.block(origin)
                self.copy(here, origin, -side, origin).wait_recv()

                @pl.when(room)
                def _():
                    self.copy(here, origin, -side, origin).start()

                then(origin)

    def finish(self):
        z = self.place.z
        for origin in range(4):
            sent = jnp.where(origin <= z, z < 3, z > 0)

            @pl.when(sent)
            def _(origin=origin):
                self.copy(self.block(origin), origin, 0, origin).wait_send()

        @pl.when(z > 0)
        def _():
            self.copy(self.block(0), 0, 0, 4).wait_send()


LINE_SEMS = 5
Z_AHEAD = 43.0
UNIT_TIME = 46.0
GATHER_SEMS = 58
Y_FIRST, X_LAST, X_NEAR, X_FAR, Y_NEAR, Y_FAR = 5, 9, 13, 17, 21, 25
C_OWN, C_Y, C_X, C_X_NEAR, C_Y_NEAR, C_X_FAR, C_Y_FAR = 29, 33, 37, 41, 45, 49, 53


class GatherUnit:
    def __init__(self, place, piece, whole, send, recv, cut):
        self.place, self.piece, self.whole = place, piece, whole
        self.send, self.recv = send, recv
        self.rows = piece.shape[0]
        self.first, self.last, self.every = pl.ds(0, cut), pl.ds(cut, self.rows - cut), pl.ds(0, self.rows)
        self.line = Line(place, lambda origin: self.block(origin, 0, 0, self.every), send, recv)
        self.peer = {
            "y": (place.wide(1, 0, 0), place.z), "x": (place.wide(0, 1, 0), place.z), "c": (place.wide(0, 0, 1), place.z)
        }
        self.order = [place.along_z(k) for k in (0, 1, 3, 2)]
        self.sent = []

    def block(self, origin, flip_y, flip_x, rows):
        first = pl.multiple_of(self.place.wide(flip_y, flip_x) * self.rows + rows.start, 16)
        return self.whole.at[origin, pl.ds(first, rows.size)]

    def copy(self, base, axis, origin, flip_y, flip_x, rows, own=None):
        block = self.block(origin, flip_y, flip_x, rows)
        return pltpu.make_async_remote_copy(
            src_ref=block if own is None else own, dst_ref=block, send_sem=self.send.at[base + origin],
            recv_sem=self.recv.at[base + origin], device_id=self.peer[axis], device_id_type=MESH,
        )

    def put(self, *where):
        self.copy(*where).start()

    def wait(self, *where):
        self.copy(*where).wait_recv()

    def begin(self):
        z = self.place.z
        self.line.begin(self.piece)
        self.put(Y_FIRST, "y", z, 0, 0, self.first, self.piece.at[self.first])
        self.put(X_LAST, "x", z, 0, 0, self.last, self.piece.at[self.last])
        self.put(X_NEAR, "x", z, 0, 0, self.first, self.piece.at[self.first])
        self.put(Y_NEAR, "y", z, 0, 0, self.last, self.piece.at[self.last])
        self.put(C_OWN, "c", z, 0, 0, self.every, self.piece)
        self.local = pltpu.make_async_copy(self.piece, self.block(z, 0, 0, self.every), self.send.at[GATHER_SEMS - 1])
        self.local.start()

    def along_z(self, far):
        def then(origin):
            self.put(Y_FIRST, "y", origin, 0, 0, self.first)
            self.put(X_LAST, "x", origin, 0, 0, self.last)
            self.put(X_NEAR, "x", origin, 0, 0, self.first)
            self.put(Y_NEAR, "y", origin, 0, 0, self.last)
            self.put(C_OWN, "c", origin, 0, 0, self.every)

        self.line.arrive(far, then)

    def across(self, at):
        origin = self.order[at]
        self.wait(Y_FIRST, "y", origin, 1, 0, self.first)
        self.put(X_FAR, "x", origin, 1, 0, self.first)
        self.put(C_Y, "c", origin, 1, 0, self.first)
        self.wait(X_LAST, "x", origin, 0, 1, self.last)
        self.put(Y_FAR, "y", origin, 0, 1, self.last)
        self.put(C_X, "c", origin, 0, 1, self.last)

    def near_to_core(self, at):
        origin = self.order[at]
        self.wait(X_NEAR, "x", origin, 0, 1, self.first)
        self.put(C_X_NEAR, "c", origin, 0, 1, self.first)
        self.wait(Y_NEAR, "y", origin, 1, 0, self.last)
        self.put(C_Y_NEAR, "c", origin, 1, 0, self.last)

    def far_to_core(self, at):
        origin = self.order[at]
        self.wait(X_FAR, "x", origin, 1, 1, self.first)
        self.put(C_X_FAR, "c", origin, 1, 1, self.first)
        self.wait(Y_FAR, "y", origin, 1, 1, self.last)
        self.put(C_Y_FAR, "c", origin, 1, 1, self.last)

    def steps(self, base):
        start = max(0.0, base - Z_AHEAD)
        out = [(start, self.begin)]
        out += [(start + 1.0 + 7.5 * far, functools.partial(self.along_z, far)) for far in (1, 2, 3)]
        for at in range(4):
            known = start + 24.0 if at else 0.0
            out.append((max(known, base + 9.0 + 9.0 * at), functools.partial(self.across, at)))
            out.append((max(known + 1.0, base + 15.0 + 9.0 * at), functools.partial(self.near_to_core, at)))
            out.append((max(known + 2.0, base + 25.0 + 9.0 * at), functools.partial(self.far_to_core, at)))
        out.append((base + 56.0, self.finish))
        return out

    def finish(self):
        firsts = (Y_FIRST, X_NEAR, X_FAR, C_Y, C_X_NEAR, C_X_FAR)
        lasts = (X_LAST, Y_NEAR, Y_FAR, C_X, C_Y_NEAR, C_Y_FAR)
        for origin in range(4):
            for base in (C_Y, C_X_NEAR, C_X_FAR):
                self.wait(base, "c", origin, 0, 0, self.first)
            for base in (C_X, C_Y_NEAR, C_Y_FAR):
                self.wait(base, "c", origin, 0, 0, self.last)
            self.wait(C_OWN, "c", origin, 0, 0, self.every)
        for origin in range(4):
            for base in firsts:
                self.copy(base, "c", origin, 0, 0, self.first).wait_send()
            for base in lasts:
                self.copy(base, "c", origin, 0, 0, self.last).wait_send()
            self.copy(C_OWN, "c", origin, 0, 0, self.every).wait_send()
        self.line.finish()
        self.local.wait()


def column_ids(width):
    return lax.broadcasted_iota(jnp.int32, (1, width), 1)


def unit_rows(values):
    average = jnp.mean(values, axis=-1, keepdims=True)
    centred = values - average
    variance = jnp.mean(centred * centred, axis=-1, keepdims=True)
    scale = lax.rsqrt(variance + eps_norm)
    return centred * scale, scale


def dot_plain(left, right):
    return lax.dot_general(left, right, (((1,), (0,)), ((), ())), preferred_element_type=f32)


def dot_turned(left, right):
    return lax.dot_general(left, right, (((1,), (1,)), ((), ())), preferred_element_type=f32)


def remote(src, dst, send, recv, peer):
    copy = pltpu.make_async_remote_copy(
        src_ref=src, dst_ref=dst, send_sem=send, recv_sem=recv, device_id=peer, device_id_type=MESH
    )
    copy.start()
    return copy


def z_line(place, every, send, recv):
    return Line(place, lambda origin: every.at[origin], send, recv)


class Stream:
    def __init__(self, slots, sems, sources):
        self.slots, self.sems, self.sources = slots, sems, sources
        self.started = 0

    def ensure(self, upto):
        while self.started <= upto and self.started < len(self.sources):
            at = self.started
            pltpu.make_async_copy(self.sources[at], self.slots.at[at % 2], self.sems.at[at % 2]).start()
            self.started += 1

    def take(self, at):
        self.ensure(at)
        pltpu.make_async_copy(self.sources[at], self.slots.at[at % 2], self.sems.at[at % 2]).wait()
        return self.slots.at[at % 2]


FORWARD_IN = 17
LAYER_SAVED = 6


def edges(head_cols):
    return 3 * head_cols // 128 * 128, -(-3 * head_cols // 128) * 128


def gelu(values):
    inner = math.sqrt(2.0 / math.pi) * (values + 0.044715 * values * values * values)
    return 0.5 * values * (1.0 + jnp.tanh(inner))


def window_bias(windows, put):
    for grid_row in range(GRID):
        shift = (GRID - 1 - grid_row) * GRID
        moved = windows if shift == 0 else pltpu.roll(windows, 512 - shift, 1)
        put(grid_row, moved[:, :PATCHES])


def forward_kernel(layers, *refs):
    units = 3 * layers
    refs = list(refs)

    def take(count):
        out = refs[:count]
        del refs[:count]
        return out

    (tokens, cot, pick, time_own, time_weight, windows_own, small_own, gains, shifts, out_bias) = take(10)
    packed = take(layers)
    (mlp_weight,) = take(1)
    pieces = []
    for layer in range(layers):
        pieces += [packed[layer], mlp_weight.at[layer, 0], mlp_weight.at[layer, 1]]
    wholes = take(units)
    saved = [take(LAYER_SAVED) for _ in range(layers)]
    block_out, grad_out, time_out, time_sel_out = take(4)
    (
        send, recv, z_send, z_recv, t_send, t_recv, save_sem, w_sem,
        w_slots, tok_all, cot_all, windows_all, small_all, time_all, share, share_y, share_x, share_c, share_z,
        x_buf, mid_buf, low_buf, acc_buf, s_buf, att_buf, act_buf, hid_buf, bias_buf, mixed_buf,
    ) = refs
    place = Place()
    place.greet()
    gather = [
        GatherUnit(place, pieces[u], wholes[u], send.at[u], recv.at[u], unit_cut(u, pieces[u].shape[0]))
        for u in range(units)
    ]
    state = set()
    tokens_n, d_model = tokens.shape
    head_cols = d_model // 4
    yp, xp, cp = ((place.wide(1, 0, 0), place.z), (place.wide(0, 1, 0), place.z), (place.wide(0, 0, 1), place.z))
    py, px, pc = place.y, place.x, place.c

    tok, win, small, cots, rz = (
        z_line(place, every, z_send.at[at], z_recv.at[at])
        for at, every in enumerate((tok_all, windows_all, small_all, cot_all, share_z))
    )
    kept = [
        pltpu.make_async_copy(src, every.at[place.z], save_sem.at[at])
        for at, (src, every) in enumerate(
            ((tokens, tok_all), (windows_own, windows_all), (small_own, small_all), (cot, cot_all))
        )
    ]
    given = {}

    def give(slot, src, dst, peer):
        given[slot] = remote(src, dst, t_send.at[slot], t_recv.at[slot], peer)

    def time_core():
        for copy in kept:
            copy.start()
        time_all[py, px, pc] = time_own[...]
        give(0, time_all.at[py, px, pc], time_all.at[py, px, pc], cp)

    def time_x():
        given[0].wait_recv()
        give(1, time_all.at[py, px], time_all.at[py, px], xp)

    def time_y():
        given[1].wait_recv()
        give(2, time_all.at[py], time_all.at[py], yp)

    def time_share():
        given[2].wait_recv()
        rows = time_all[...].reshape(128, d_model)
        cut = time_weight.shape[1]
        at_row = lax.broadcasted_iota(jnp.int32, (d_model, cut), 0)
        at_col = lax.broadcasted_iota(jnp.int32, (d_model, cut), 1)
        select = (at_row == at_col + place.wide() * cut).astype(bf16)
        picked = dot_plain(rows, select).astype(bf16)
        time_sel_out[...] = picked
        time_out[...] = rows
        for layer in range(layers):
            part = dot_plain(picked, time_weight[layer]).reshape(2, 2, 2, 16, d_model)
            share[:, :, :, layer] = part[:, :, :, :8]
        give(3, share.at[1 - py], share_y, yp)

    def share_step_x():
        given[3].wait_recv()
        share[py] = share[py] + share_y[...]
        give(4, share.at[py, 1 - px], share_x, xp)

    def share_step_c():
        given[4].wait_recv()
        share[py, px] = share[py, px] + share_x[...]
        give(5, share.at[py, px, 1 - pc], share_c, cp)

    def share_step_z():
        given[5].wait_recv()
        share[py, px, pc] = share[py, px, pc] + share_c[...]
        share_z[place.z] = share[py, px, pc]
        rz.begin(share_z.at[place.z])
        for slot in range(6):
            given[slot].wait_send()

    def line_steps(line, own, start, pace):
        steps = [(start, functools.partial(line.begin, own))]
        steps += [(start + pace * far, functools.partial(line.arrive, far)) for far in (1, 2, 3)]
        return steps + [(start + 3 * pace + 4.0, line.finish)]

    def mark(key):
        if key == "rows":
            for copy in kept:
                copy.wait()
        state.add(key)

    events = [
        (0.1, time_core),
        (3.0, time_x),
        (7.0, time_y),
        (11.0, time_share),
        (18.0, share_step_x),
        (24.0, share_step_c),
        (28.0, share_step_z),
    ]
    events += line_steps(small, small_own, 0.2, 5.0)
    events += [(28.0 + 8.0 * far, functools.partial(rz.arrive, far)) for far in (1, 2, 3)] + [(56.0, rz.finish)]
    events += line_steps(win, windows_own, 34.0, 10.0)
    events += line_steps(tok, tokens, 36.0, 14.0)
    events += [(84.0, functools.partial(mark, "rows"))]
    events += line_steps(cots, cot, 130.0, 16.0)
    for at, unit in enumerate(gather):
        events += unit.steps(UNIT_TIME * at)
        events.append((UNIT_TIME * at + 56.5, functools.partial(mark, at)))

    stream = Stream(w_slots, w_sem, [wholes[u].at[z] for u in range(units) for z in range(4)])
    pending = {}

    def save(slot, src, dst):
        copy = pltpu.make_async_copy(src, dst, save_sem.at[slot])
        copy.start()
        pending[slot] = copy

    def settle(slot):
        if slot in pending:
            pending.pop(slot).wait()

    def weights(unit, z):
        at = unit * 4 + z
        stream.ensure(at)
        if (at + 1) // 4 in state:
            stream.ensure(at + 1)
        return stream.take(at)

    def compute_steps():
        columns = column_ids(d_model)
        out_start, qkv_end = edges(head_cols)
        for layer in range(layers):
            x_save, mid_save, s_save, att_save, hid_save, act_save = saved[layer]
            row = 2 * layer
            yield (3 * layer if layer else "rows"), 2.0
            if layer == 0:
                total = dot_plain(pick[:, 0:tokens_n], tok_all[0])
                for z in range(1, 4):
                    total = total + dot_plain(pick[:, z * tokens_n : (z + 1) * tokens_n], tok_all[z])
                x_buf[...] = total
            settle(4)
            settle(5)
            save(4, x_buf, x_save)
            unit, _ = unit_rows(x_buf[...])
            low_buf[...] = (unit * gains[row : row + 1, :] + shifts[row : row + 1, :]).astype(bf16)
            settle(6)
            for z in range(4):
                yield 3 * layer, 2.0
                w = weights(3 * layer, z)
                share_rows = share_z[z, layer]
                at_image = lax.broadcasted_iota(jnp.int32, share_rows.shape, 0) == place.z
                offset = jnp.sum(jnp.where(at_image, share_rows, 0.0), axis=0, keepdims=True)
                offset = offset + small_all[z, 2 + layer : 3 + layer, :]
                spatial = dot_plain(low_buf[...], w[:, :qkv_end]) + offset[:, :qkv_end]
                s_buf[z, :, :qkv_end] = spatial.astype(bf16)
                yield 3 * layer, 2.0
                q = s_buf[z, :, 0:head_cols]
                k = s_buf[z, :, head_cols : 2 * head_cols]
                v = s_buf[z, :, 2 * head_cols : 3 * head_cols]
                head_of = column_ids(head_cols) // HEAD_DIM
                slot = z % 2
                settle(8 + slot)

                def one_head(head, carry):
                    here = head_of == head

                    def put(grid_row, block):
                        bias_buf[grid_row * GRID : (grid_row + 1) * GRID, :] = block

                    first_row = pl.multiple_of(head * GRID, GRID)
                    window_bias(windows_all[z, layer, pl.ds(first_row, GRID), :], put)
                    scores = dot_turned(jnp.where(here, q, 0), k)
                    scores = scores * HEAD_DIM ** (-0.5) + bias_buf[...]
                    top = jnp.max(scores, axis=-1, keepdims=True)
                    exponent = jnp.exp(scores - top)
                    attention = exponent / jnp.sum(exponent, axis=-1, keepdims=True)
                    att_buf[slot, head] = attention
                    mixed_buf[...] += dot_plain(attention.astype(bf16), jnp.where(here, v, 0))
                    return carry

                mixed_buf[...] = jnp.zeros_like(mixed_buf)
                for pair in range(2):
                    lax.fori_loop(2 * pair, 2 * pair + 2, one_head, 0)
                    yield 3 * layer, 2.0
                save(8 + slot, att_buf.at[slot], att_save.at[z])
                s_buf[z, :, 3 * head_cols :] = mixed_buf[...].astype(bf16)
                heads = jnp.where(columns[:, out_start:] >= 3 * head_cols, s_buf[z, :, out_start:], 0)
                branch = dot_turned(heads, w[:, out_start:])
                acc_buf[...] = branch if z == 0 else acc_buf[...] + branch
            save(6, s_buf, s_save)
            settle(4)
            mid_buf[...] = x_buf[...] + (acc_buf[...] + out_bias[row : row + 1, :])
            save(5, mid_buf, mid_save)
            unit, _ = unit_rows(mid_buf[...])
            low_buf[...] = (unit * gains[row + 1 : row + 2, :] + shifts[row + 1 : row + 2, :]).astype(bf16)
            settle(7)
            for z in range(4):
                yield 3 * layer + 1, 2.5
                w = weights(3 * layer + 1, z)
                slot = z % 2
                settle(10 + slot)
                hid_buf[slot] = dot_plain(low_buf[...], w[...]) + small_all[z, layer : layer + 1, :]
                save(10 + slot, hid_buf.at[slot], hid_save.at[z])
                act_buf[z] = gelu(hid_buf[slot]).astype(bf16)
            save(7, act_buf, act_save)
            if layer == layers - 1:
                yield 3 * layer + 1, 1.5
                total = dot_plain(pick[:, 0:tokens_n], cot_all[0])
                for z in range(1, 4):
                    total = total + dot_plain(pick[:, z * tokens_n : (z + 1) * tokens_n], cot_all[z])
                grad_out[...] = total
            for z in range(4):
                yield 3 * layer + 2, 1.8
                w = weights(3 * layer + 2, z)
                branch = dot_turned(act_buf[z], w[...])
                acc_buf[...] = branch if z == 0 else acc_buf[...] + branch
            x_buf[...] = mid_buf[...] + (acc_buf[...] + out_bias[row + 1 : row + 2, :])
        block_out[...] = x_buf[...].astype(bf16)
        for slot in list(pending):
            settle(slot)

    interleave(events, compute_steps(), state)


def interleave(events, compute, state):
    events = sorted(events, key=lambda item: item[0])
    clock = 0.0
    wanted = next(compute)
    while wanted is not None or events:
        if events and (events[0][0] <= clock or wanted is None or wanted[0] not in state):
            at, step = events.pop(0)
            clock = max(clock, at)
            step()
            continue
        clock += wanted[1]
        wanted = next(compute, None)


def forward_all(
    tokens, cot, pick, time_own, time_weight, windows_own, small_own, gains, shifts, out_bias, packed, mlp_weight
):
    layers = len(packed)
    units = 3 * layers
    rows, d_model = tokens.shape
    piece_rows = packed[0].shape[0]
    any_space = pl.BlockSpec(memory_space=pl.ANY)
    vmem = pl.BlockSpec(memory_space=pltpu.VMEM)
    layer_shapes = [
        ((rows, d_model), f32),
        ((rows, d_model), f32),
        ((4, rows, d_model), bf16),
        ((4, 4, rows, rows), f32),
        ((4, rows, d_model), f32),
        ((4, rows, d_model), bf16),
    ]
    out_shape = (
        [jax.ShapeDtypeStruct((4, 8 * piece_rows, d_model), bf16)] * units
        + [jax.ShapeDtypeStruct(*item) for item in layer_shapes] * layers
        + [
            jax.ShapeDtypeStruct((rows, d_model), bf16),
            jax.ShapeDtypeStruct((rows, d_model), f32),
            jax.ShapeDtypeStruct((128, d_model), bf16),
            jax.ShapeDtypeStruct((128, piece_rows), bf16),
        ]
    )
    share_tail = (layers, 8, d_model)
    scratch = [
        pltpu.SemaphoreType.DMA((units, GATHER_SEMS)),
        pltpu.SemaphoreType.DMA((units, GATHER_SEMS)),
        pltpu.SemaphoreType.DMA((5, LINE_SEMS)),
        pltpu.SemaphoreType.DMA((5, LINE_SEMS)),
        pltpu.SemaphoreType.DMA((6,)),
        pltpu.SemaphoreType.DMA((6,)),
        pltpu.SemaphoreType.DMA((12,)),
        pltpu.SemaphoreType.DMA((2,)),
        pltpu.VMEM((2, d_model, d_model), bf16),
        pltpu.VMEM((4, rows, d_model), bf16),
        pltpu.VMEM((4, rows, d_model), bf16),
        pltpu.VMEM((4,) + windows_own.shape, f32),
        pltpu.VMEM((4,) + small_own.shape, f32),
        pltpu.VMEM((2, 2, 2, 16, d_model), bf16),
        pltpu.VMEM((2, 2, 2) + share_tail, f32),
        pltpu.VMEM((2, 2) + share_tail, f32),
        pltpu.VMEM((2,) + share_tail, f32),
        pltpu.VMEM(share_tail, f32),
        pltpu.VMEM((4,) + share_tail, f32),
        pltpu.VMEM((rows, d_model), f32),
        pltpu.VMEM((rows, d_model), f32),
        pltpu.VMEM((rows, d_model), bf16),
        pltpu.VMEM((rows, d_model), f32),
        pltpu.VMEM((4, rows, d_model), bf16),
        pltpu.VMEM((2, 4, rows, rows), f32),
        pltpu.VMEM((4, rows, d_model), bf16),
        pltpu.VMEM((2, rows, d_model), f32),
        pltpu.VMEM((rows, rows), f32),
        pltpu.VMEM((rows, d_model // 4), f32),
    ]
    out = pl.pallas_call(
        functools.partial(forward_kernel, layers),
        out_shape=out_shape,
        in_specs=[any_space] * 2 + [vmem] * 8 + [any_space] * (layers + 1),
        out_specs=[any_space] * (units + LAYER_SAVED * layers) + [vmem] * 4,
        scratch_shapes=scratch,
        compiler_params=pltpu.CompilerParams(
            collective_id=0, has_side_effects=True, vmem_limit_bytes=60 * 2**20
        ),
        name="forward_all",
    )(tokens, cot, pick, time_own, time_weight, windows_own, small_own, gains, shifts, out_bias, *packed, mlp_weight)
    wholes = out[:units]
    saved = [out[units + LAYER_SAVED * at : units + LAYER_SAVED * (at + 1)] for at in range(layers)]
    return wholes, saved, out[units + LAYER_SAVED * layers :]


def gelu_slope(values):
    factor = math.sqrt(2.0 / math.pi)
    square = values * values
    bend = jnp.tanh(factor * (values + 0.044715 * square * values))
    return 0.5 * (1.0 + bend) + 0.5 * values * (1.0 - bend * bend) * factor * (1.0 + 3 * 0.044715 * square)


def dot_rows(left, right):
    return lax.dot_general(left, right, (((0,), (0,)), ((), ())), preferred_element_type=f32)


def norm_back(grad, unit, scale, norm_gain):
    weighted = grad * norm_gain
    first = jnp.mean(weighted, axis=-1, keepdims=True)
    second = jnp.mean(weighted * unit, axis=-1, keepdims=True)
    return scale * (weighted - first - unit * second)


def column_sums(values):
    return jnp.sum(values, axis=0, keepdims=True)


def fold_window(grads):
    total = None
    empty = jnp.zeros((GRID, 512 - PATCHES), f32)
    for grid_row in range(GRID):
        wide = jnp.concatenate([grads[grid_row * GRID : (grid_row + 1) * GRID, :], empty], axis=1)
        shift = (GRID - 1 - grid_row) * GRID
        moved = wide if shift == 0 else pltpu.roll(wide, shift, 1)
        total = moved if total is None else total + moved
    return total


SCATTER_SEMS = 23


def add_into(total, part):
    total[...] = total[...] + part[...]


class ScatterUnit:
    def __init__(self, place, out, total, far, near, from_z, send, recv, cut):
        self.place, self.out = place, out
        self.total, self.far, self.near, self.from_z = total, far, near, from_z
        self.send, self.recv = send, recv
        self.rows, self.cut = total.shape[3], cut
        self.first, self.last = pl.ds(0, cut), pl.ds(cut, self.rows - cut)
        self.copies, self.unsent, self.closed = {}, set(), set()

    def put(self, slot, peer, src, dst):
        self.copies[slot] = remote(src, dst, self.send.at[slot], self.recv.at[slot], peer)
        self.unsent.add(slot)

    def settle(self, slots):
        for slot in sorted(self.unsent.intersection(slots)):
            self.copies[slot].wait_send()
            self.unsent.remove(slot)

    def first_stage(self, k):
        p = self.place
        self.put(4 + k, (p.wide(0, 1), p.z), self.total.at[k, :, 1 - p.x, self.first], self.far.at[k, :, self.first])
        self.put(8 + k, (p.wide(1, 0), p.z), self.total.at[k, 1 - p.y, :, self.last], self.far.at[k, :, self.last])

    def second_stage(self, k):
        p = self.place
        self.copies[4 + k].wait_recv()
        for block in range(2):
            add_into(self.total.at[k, block, p.x, self.first], self.far.at[k, block, self.first])
        self.put(12 + k, (p.wide(1, 0), p.z), self.total.at[k, 1 - p.y, p.x, self.first], self.near.at[k, self.first])
        self.copies[8 + k].wait_recv()
        for block in range(2):
            add_into(self.total.at[k, p.y, block, self.last], self.far.at[k, block, self.last])
        self.put(16 + k, (p.wide(0, 1), p.z), self.total.at[k, p.y, 1 - p.x, self.last], self.near.at[k, self.last])

    def third_stage(self, k):
        p = self.place
        self.copies[12 + k].wait_recv()
        self.copies[16 + k].wait_recv()
        add_into(self.total.at[k, p.y, p.x], self.near.at[k])
        if k:
            self.put(19 + k, (p.wide(), p.along_z(k)), self.total.at[k, p.y, p.x], self.from_z.at[k - 1])
            self.closed.add(k)

    def finish(self):
        p = self.place
        for k in (1, 2, 3):
            self.copies[19 + k].wait_recv()
        both = self.total[0, p.y, p.x].astype(f32)
        for k in range(3):
            both = both + self.from_z[k].astype(f32)
        self.out[...] = both
        self.settle(list(self.copies))
        self.closed.add(0)


FAR_FIRST = (2, 1, 3, 0)


def scatter_step(unit, k, late):
    unit.second_stage(k)

    def third():
        unit.third_stage(k)
        if k == 0:
            return ((late, unit.finish),)

    return ((late, third),)


def backward_kernel(last_layer, *refs):
    refs = list(refs)

    def take(count):
        out = refs[:count]
        del refs[:count]
        return out

    (
        grad, mid_in, gains, shifts, trow_in, x_in, pick_in, time_weight, rows_in, s_all, att_all, hid_all, act_all,
        proj, up, down,
    ) = take(16)
    proj_out, up_out, down_out, grad_out, rows_out, row_sums, table_sums, time_sums, trow_out, rows_all = take(10)
    (
        total_a, total_b, far, near, from_z, right_a, right_b, left, turned,
        w_slots, s_slots, att_slots, hid_slots, acc_buf, low_buf, head_grads,
        row_parts, rows_z, rows_w, table_parts, table_low, table_z, table_w, trow_z, trow_kept, small_send, small_recv,
        send, recv, left_send, left_recv, line_send, line_recv, w_sem, s_sem, att_sem, hid_sem, load_sem, credit,
    ) = refs
    place = Place()
    place.greet()
    rows, d_model = grad.shape
    cut = down_out.shape[0]
    head_cols = d_model // 4
    core = (place.wide(0, 0, 1), place.z)
    zs = {k: place.along_z(k) for k in range(4)}
    columns = column_ids(d_model)
    out_start, qkv_end = edges(head_cols)
    units = {
        name: ScatterUnit(
            place, out, total, far.at[at], near.at[at], from_z.at[at], send.at[at], recv.at[at], unit_cut(at, cut)
        )
        for at, (name, out, total) in enumerate(
            (("down", down_out, total_a), ("up", up_out, total_b), ("proj", proj_out, total_a))
        )
    }
    line = z_line(place, rows_all, line_send, line_recv)

    right_copies = {}

    def give_right(name, at, k, src, buffer):
        right_copies[name, k] = remote(
            src, buffer.at[zs[k], pl.ds(rows, rows)], send.at[at, k], recv.at[at, k], core
        )

    left_copies = {}

    def make_left(at, values):
        if at > 1:
            for copy in left_copies[at - 2]:
                copy.wait_send()
        flipped = turned.at[at % 2]
        flipped[...] = values.T
        copies = []
        for block in range(4):
            mine = pl.multiple_of((2 * block + place.c) * cut, 16)
            other = pl.multiple_of((2 * block + 1 - place.c) * cut, 16)
            here = pl.ds(block * cut, cut)
            copies.append(
                remote(
                    flipped.at[pl.ds(other, cut)], left.at[at, here, pl.ds(rows, rows)],
                    left_send.at[at, block], left_recv.at[at, block], core,
                )
            )
            left[at, here, 0:rows] = flipped[pl.ds(mine, cut), :]
        left_copies[at] = copies

    def left_ready(at):
        for copy in left_copies[at]:
            copy.wait_recv()

    loads, keep = [], []
    if last_layer:
        line.begin(rows_in)
        keep.append(pltpu.make_async_copy(rows_in, rows_all.at[place.z], load_sem.at[4]))
        keep[0].start()
    for k in FAR_FIRST:
        give_right("down", 0, k, act_all.at[zs[k]], right_a)
        load = pltpu.make_async_copy(act_all.at[zs[k]], right_a.at[zs[k], pl.ds(0, rows)], load_sem.at[k])
        load.start()
        loads.append((k, load))
    w_sources = []
    for k in FAR_FIRST:
        w_sources += [down.at[zs[k]], up.at[zs[k]]]
    w_sources += [proj.at[zs[k]] for k in FAR_FIRST]
    weights = Stream(w_slots, w_sem, w_sources)
    hidden = Stream(hid_slots, hid_sem, [hid_all.at[zs[k]] for k in FAR_FIRST])
    saved = Stream(s_slots, s_sem, [s_all.at[zs[k]] for k in FAR_FIRST])
    attentions = Stream(att_slots, att_sem, [att_all.at[zs[k]] for k in FAR_FIRST])
    for stream in (weights, hidden, saved, attentions):
        stream.ensure(1)

    def weight_grad(name, k, buffer, *lefts):
        unit = units[name]
        if len(lefts) == 1:
            ranges = [(0, d_model, dot_plain(left[lefts[0]], buffer[zs[k]]))]
        else:
            first = dot_plain(left[lefts[0]], buffer[zs[k], :, 0:qkv_end])
            last = dot_plain(left[lefts[1]], buffer[zs[k], :, out_start:])
            edge = jnp.where(
                columns[:, out_start:qkv_end] < 3 * head_cols, first[:, out_start:], last[:, : qkv_end - out_start]
            )
            ranges = [
                (0, out_start, first[:, :out_start]), (out_start, qkv_end, edge),
                (qkv_end, d_model, last[:, qkv_end - out_start :]),
            ]
        for start, stop, part in ranges:
            low = part.astype(bf16)
            for block in range(4):
                unit.total[k, block // 2, block % 2, :, start:stop] = low[block * cut : (block + 1) * cut]

    late = {}

    def late_load(src, dst, slot):
        late[slot] = pltpu.make_async_copy(src, dst, load_sem.at[slot])
        late[slot].start()

    def late_wait(slot):
        late[slot].wait()

    def put_row(row, values):
        for z in range(4):
            row_parts[z, row : row + 1, :] = values

    small = {}
    axes = ((core, 6), ((place.wide(0, 1, 0), place.z), 9), ((place.wide(1, 0, 0), place.z), 12))
    own_time = (
        time_sums.at[place.y, place.x, place.c], time_sums.at[place.y, place.x], time_sums.at[place.y]
    )
    own_trow = (trow_out.at[place.y, place.x, place.c], trow_out.at[place.y, place.x], trow_out.at[place.y])

    def give(slot, src, dst, peer):
        small[slot] = remote(src, dst, small_send.at[slot], small_recv.at[slot], peer)

    def small_begin():
        table_low[...] = table_parts[...].astype(bf16)
        for k in (1, 2, 3):
            peer = (place.wide(), zs[k])
            give(k - 1, row_parts.at[zs[k]], rows_z.at[k - 1], peer)
            give(k + 2, table_low.at[zs[k]], table_z.at[k - 1], peer)
        return ((9.0, small_along_z),)

    def small_along_z():
        for slot in range(6):
            small[slot].wait_recv()
        totals = row_parts[place.z]
        at_row = lax.broadcasted_iota(jnp.int32, (16, d_model), 0)
        times = jnp.where(at_row == place.z, totals[7:8, :], 0.0)
        tables = table_parts[place.z]
        for k in (1, 2, 3):
            part = rows_z[k - 1]
            times = jnp.where(at_row == place.along_z(4 - k), part[7:8, :], times)
            totals = totals + part
            tables = tables + table_z[k - 1].astype(f32)
        row_sums[...] = totals
        table_sums[...] = tables
        time_sums[place.y, place.x, place.c] = times.astype(bf16)
        small_across(0)
        return ((4.0, functools.partial(small_step, 0)),)

    def small_across(axis):
        peer, slot = axes[axis]
        give(slot, row_sums, rows_w.at[axis], peer)
        table_low[place.z] = table_sums[...].astype(bf16)
        give(slot + 1, table_low.at[place.z], table_w.at[axis], peer)
        give(slot + 2, own_time[axis], own_time[axis], peer)

    def small_step(axis):
        slot = axes[axis][1]
        for at in range(slot, slot + 3):
            small[at].wait_recv()
            small[at].wait_send()
        row_sums[...] = row_sums[...] + rows_w[axis]
        table_sums[...] = table_low[place.z].astype(f32) + table_w[axis].astype(f32)
        if axis < 2:
            small_across(axis + 1)
            return ((5.0, functools.partial(small_step, axis + 1)),)
        late_wait(6)
        times = jnp.where(columns < 3 * head_cols, time_sums[...].reshape(128, d_model), 0)
        part = dot_turned(times, s_slots[0, 0:cut]).reshape(8, 16, cut)[:, :8]
        late_wait(8)
        part = part + trow_kept[...]
        trow_out[place.y, place.x, place.c] = part
        if last_layer:
            return None
        for k in (1, 2, 3):
            give(14 + k, own_trow[0], trow_z.at[k - 1], (place.wide(), zs[k]))
        return ((6.0, trow_along_z),)

    def trow_along_z():
        for slot in (15, 16, 17):
            small[slot].wait_recv()
            small[slot].wait_send()
        here = trow_out[place.y, place.x, place.c] + trow_z[0] + trow_z[1] + trow_z[2]
        trow_out[place.y, place.x, place.c] = here
        give(18, own_trow[0], own_trow[0], axes[0][0])
        return ((4.0, functools.partial(trow_step, 0)),)

    def trow_step(axis):
        small[18 + axis].wait_recv()
        small[18 + axis].wait_send()
        if axis < 2:
            give(19 + axis, own_trow[axis + 1], own_trow[axis + 1], axes[axis + 1][0])
            return ((5.0, functools.partial(trow_step, axis + 1)),)

    def close_rows():
        unit, scale = unit_rows(hid_slots[0])
        from_norm = norm_back(acc_buf[...], unit, scale, gains[0:1, :])
        put_row(0, column_sums(acc_buf[...] * unit))
        put_row(2, column_sums(acc_buf[...]))
        grad_out[...] = grad_out[...] + from_norm
        late_load(time_weight, s_slots.at[0, pl.ds(0, cut)], 6)
        late_load(trow_in.at[place.y, place.x, place.c], trow_kept, 8)
        late_load(pick_in, s_slots.at[1, :, pl.ds(0, 4 * rows)], 7)
        following = [(0.0, small_begin)]
        if not last_layer:
            low_buf[0] = grad_out[...].astype(bf16)
            line.begin(low_buf.at[0])
            keep.append(pltpu.make_async_copy(low_buf.at[0], rows_all.at[place.z], load_sem.at[4]))
            keep[0].start()
            following += [(14.0 * far_off, functools.partial(line.arrive, far_off)) for far_off in (1, 2, 3)]
        return following

    def compute():
        low_buf[0] = grad[...].astype(bf16)
        put_row(5, column_sums(low_buf[0].astype(f32)))
        make_left(0, low_buf[0])
        left_ready(0)
        for at, k in enumerate(FAR_FIRST):
            loads[at][1].wait()
            right_copies["down", k].wait_recv()
            weight_grad("down", k, right_a, 0)
            yield 1.8, [(units["down"], k)]
            w = weights.take(2 * at)
            hid = hidden.take(at)
            act_grad = dot_plain(low_buf[0], w[...])
            hid_grad = (act_grad * gelu_slope(hid[...])).astype(bf16)
            right_b[zs[k], 0:rows] = hid_grad
            weights.ensure(2 * at + 2)
            hidden.ensure(at + 2)
            give_right("up", 1, k, right_b.at[zs[k], pl.ds(0, rows)], right_b)
            row_parts[zs[k], 6:7, :] = column_sums(hid_grad.astype(f32))
            yield 2.5, []
            w = weights.take(2 * at + 1)
            part = dot_turned(right_b[zs[k], 0:rows], w[...])
            acc_buf[...] = part if at == 0 else acc_buf[...] + part
            weights.ensure(2 * at + 3)
            yield 1.5, []
        for k in FAR_FIRST:
            right_copies["down", k].wait_send()
        pl.semaphore_signal(credit, inc=1, device_id=core, device_id_type=MESH)
        unit, scale = unit_rows(mid_in[...])
        make_left(1, (unit * gains[1:2, :] + shifts[1:2, :]).astype(bf16))
        from_norm = norm_back(acc_buf[...], unit, scale, gains[1:2, :])
        put_row(1, column_sums(acc_buf[...] * unit))
        put_row(3, column_sums(acc_buf[...]))
        grad_out[...] = grad[...] + from_norm
        low_buf[0] = grad_out[...].astype(bf16)
        put_row(4, column_sums(low_buf[0].astype(f32)))
        late_load(x_in, hid_slots.at[0], 5)
        yield 4.0, []
        left_ready(1)
        right_copies["up", FAR_FIRST[0]].wait_recv()
        weight_grad("up", FAR_FIRST[0], right_b, 1)
        yield 1.5, [(units["up"], FAR_FIRST[0])]
        make_left(2, low_buf[0])
        late_wait(5)
        unit, scale = unit_rows(hid_slots[0])
        make_left(3, (unit * gains[0:1, :] + shifts[0:1, :]).astype(bf16))
        left_ready(2)
        left_ready(3)
        pl.semaphore_wait(credit, 1)
        yield 4.0, []
        head_of = column_ids(head_cols) // HEAD_DIM
        score_scale = HEAD_DIM ** (-0.5)
        for at, k in enumerate(FAR_FIRST):
            if at:
                right_copies["up", k].wait_recv()
                weight_grad("up", k, right_b, 1)
                yield 1.5, [(units["up"], k)]
            w = weights.take(8 + at)
            s = saved.take(at)
            attention_slot = attentions.take(at)
            low_buf[1, :, out_start:] = dot_plain(low_buf[0], w[:, out_start:]).astype(bf16)
            mixed_grad = low_buf[1, :, 3 * head_cols :]
            q = s[:, 0:head_cols]
            key = s[:, head_cols : 2 * head_cols]
            v = s[:, 2 * head_cols : 3 * head_cols]
            head_grads[...] = jnp.zeros_like(head_grads)

            def one_head(head, carry):
                here = head_of == head
                attention = attention_slot[head]
                own_grad = jnp.where(here, mixed_grad, 0)
                dot_back = dot_turned(own_grad, v)
                both = attention * dot_back
                score_low = (both - attention * jnp.sum(both, axis=-1, keepdims=True)).astype(bf16)
                first_row = pl.multiple_of(head * GRID, GRID)
                table_parts[zs[k], pl.ds(first_row, GRID), :] = fold_window(score_low.astype(f32))
                head_grads[0] += dot_plain(score_low, jnp.where(here, key, 0))
                head_grads[1] += dot_rows(score_low, jnp.where(here, q, 0))
                head_grads[2] += dot_rows(attention.astype(bf16), own_grad)
                return carry

            lax.fori_loop(0, 2, one_head, 0)
            yield 2.5, []
            lax.fori_loop(2, 4, one_head, 0)
            here = right_a.at[zs[k]]
            here[0:rows, 0:head_cols] = (head_grads[0] * score_scale).astype(bf16)
            here[0:rows, head_cols : 2 * head_cols] = (head_grads[1] * score_scale).astype(bf16)
            here[0:rows, 2 * head_cols : 3 * head_cols] = head_grads[2].astype(bf16)
            here[0:rows, 3 * head_cols :] = s[:, 3 * head_cols :]
            give_right("proj", 2, k, right_a.at[zs[k], pl.ds(0, rows)], right_a)
            saved.ensure(at + 2)
            attentions.ensure(at + 2)
            yield 2.5, []
            own = right_a[zs[k], 0:rows]
            row_parts[zs[k], 7:8, :] = column_sums(own.astype(f32))
            own = jnp.where(columns < 3 * head_cols, own, 0)
            part = dot_turned(own[:, :qkv_end], w[:, :qkv_end])
            acc_buf[...] = part if at == 0 else acc_buf[...] + part
            weights.ensure(8 + at + 2)
            yield 1.5, []
        yield 2.0, [], None, close_rows()
        for k in FAR_FIRST:
            right_copies["proj", k].wait_recv()
            yield 0.2, [], (units["down"], k)
            units["down"].settle((4 + k, 8 + k, 12 + k, 16 + k, 19 + k))
            weight_grad("proj", k, right_a, 3, 2)
            yield 2.0, [(units["proj"], k)]

    first_events = []
    if last_layer:
        first_events = [(20.0 * far_off, functools.partial(line.arrive, far_off)) for far_off in (1, 2, 3)]
    merge_steps(compute(), first_events, 10.7, 12.0 if last_layer else 12.0, 12.0)
    for slot in range(6):
        small[slot].wait_send()
    for (name, k), copy in right_copies.items():
        if name != "down":
            copy.wait_send()
    for at in (2, 3):
        for copy in left_copies[at]:
            copy.wait_send()
    line.finish()
    keep[0].wait()
    gathered = pltpu.make_async_copy(rows_all, right_b.at[:, pl.ds(0, rows)], load_sem.at[4])
    gathered.start()
    gathered.wait()
    late_wait(7)
    total = dot_plain(s_slots[1, :, 0:rows], right_b[0, 0:rows])
    for z in range(1, 4):
        total = total + dot_plain(s_slots[1, :, z * rows : (z + 1) * rows], right_b[z, 0:rows])
    rows_out[...] = total.astype(bf16)


def merge_steps(compute, events, links, late, follow):
    clock, link_free = 0.0, 0.0
    events = list(events)

    def run_first():
        events.sort(key=lambda item: item[0])
        at, step = events.pop(0)
        for delay, following in step() or ():
            events.append((max(clock, at) + delay, following))
        return max(clock, at)

    while True:
        while events and min(item[0] for item in events) <= clock:
            clock = run_first()
        made = next(compute, None)
        if made is None:
            break
        clock += made[0]
        for unit, k in made[1]:
            unit.first_stage(k)
            start = max(clock, link_free)
            link_free = start + links
            events.append((start + late, functools.partial(scatter_step, unit, k, follow)))
        if len(made) > 2 and made[2]:
            unit, k = made[2]
            while k not in unit.closed:
                clock = run_first()
        if len(made) > 3:
            events += [(clock + delay, step) for delay, step in made[3]]
    while events:
        clock = run_first()


def backward_layer(last_layer, grad, saved, gains, shifts, trow, pick, time_weight, rows_in, weights):
    x_in, mid_in, s_all, att_all, hid_all, act_all = saved
    proj, up, down = weights
    rows, d_model = grad.shape
    cut = d_model // 8
    any_space = pl.BlockSpec(memory_space=pl.ANY)
    vmem = pl.BlockSpec(memory_space=pltpu.VMEM)
    block = jax.ShapeDtypeStruct((cut, d_model), f32)
    out_shape = [
        block,
        block,
        block,
        jax.ShapeDtypeStruct((rows, d_model), f32),
        jax.ShapeDtypeStruct((rows, d_model), bf16),
        jax.ShapeDtypeStruct((8, d_model), f32),
        jax.ShapeDtypeStruct((4 * GRID, 512), f32),
        jax.ShapeDtypeStruct((2, 2, 2, 16, d_model), bf16),
        jax.ShapeDtypeStruct((2, 2, 2, 8, 8, cut), f32),
        jax.ShapeDtypeStruct((4, rows, d_model), bf16),
    ]
    dma = pltpu.SemaphoreType.DMA
    scratch = [
        pltpu.VMEM((4, 2, 2, cut, d_model), bf16),
        pltpu.VMEM((4, 2, 2, cut, d_model), bf16),
        pltpu.VMEM((3, 4, 2, cut, d_model), bf16),
        pltpu.VMEM((3, 4, cut, d_model), bf16),
        pltpu.VMEM((3, 3, cut, d_model), bf16),
        pltpu.VMEM((4, 2 * rows, d_model), bf16),
        pltpu.VMEM((4, 2 * rows, d_model), bf16),
        pltpu.VMEM((4, 4 * cut, 2 * rows), bf16),
        pltpu.VMEM((2, d_model, rows), bf16),
        pltpu.VMEM((2, d_model, d_model), bf16),
        pltpu.VMEM((2, rows, d_model), bf16),
        pltpu.VMEM((2, 4, rows, rows), f32),
        pltpu.VMEM((2, rows, d_model), f32),
        pltpu.VMEM((rows, d_model), f32),
        pltpu.VMEM((2, rows, d_model), bf16),
        pltpu.VMEM((3, rows, d_model // 4), f32),
        pltpu.VMEM((4, 8, d_model), f32),
        pltpu.VMEM((3, 8, d_model), f32),
        pltpu.VMEM((3, 8, d_model), f32),
        pltpu.VMEM((4, 4 * GRID, 512), f32),
        pltpu.VMEM((4, 4 * GRID, 512), bf16),
        pltpu.VMEM((3, 4 * GRID, 512), bf16),
        pltpu.VMEM((3, 4 * GRID, 512), bf16),
        pltpu.VMEM((3, 8, 8, cut), f32),
        pltpu.VMEM((8, 8, cut), f32),
        dma((21,)),
        dma((21,)),
        dma((3, SCATTER_SEMS)),
        dma((3, SCATTER_SEMS)),
        dma((4, 4)),
        dma((4, 4)),
        dma((LINE_SEMS,)),
        dma((LINE_SEMS,)),
        dma((2,)),
        dma((2,)),
        dma((2,)),
        dma((2,)),
        dma((9,)),
        pltpu.SemaphoreType.REGULAR,
    ]
    return pl.pallas_call(
        functools.partial(backward_kernel, last_layer),
        out_shape=out_shape,
        in_specs=[vmem] * 4 + [any_space] * 12,
        out_specs=[vmem] * 9 + [any_space],
        scratch_shapes=scratch,
        compiler_params=pltpu.CompilerParams(
            collective_id=1 if last_layer else 2, has_side_effects=True, vmem_limit_bytes=63 * 2**20
        ),
        name="backward_last" if last_layer else "backward_first",
    )(
        grad, mid_in, gains, shifts, trow, x_in, pick, time_weight, rows_in, s_all, att_all, hid_all, act_all,
        proj, up, down,
    )


def shards_plain(
    tokens,
    cotangent,
    segment_ids,
    patch_pos,
    time_index,
    time_table,
    norm_gain,
    norm_shift,
    attn_weight,
    out_weight,
    qkv_bias,
    out_bias,
    mlp_weight,
    up_bias,
    rel_table,
):
    image_count = time_index.shape[0]
    layer_count = attn_weight.shape[0]
    narrow_at = lax.axis_index("narrow")
    wide_at = lax.axis_index("wide")
    wide_size = lax.axis_size("wide")
    own_rows = tokens.shape[0]
    in_rows, cols = attn_weight.shape[2:]
    image_local = segment_ids % image_count
    grid_slot = image_local * PATCHES + patch_pos
    own_slots = narrow_at * own_rows + jnp.arange(own_rows, dtype=jnp.int32)
    pick_in = (own_slots[:, None] == grid_slot[None, :]).astype(bf16)
    own_grid = lax.dynamic_slice_in_dim(grid_slot, narrow_at * own_rows, own_rows)
    pick_out = (own_grid[:, None] == jnp.arange(grid_slot.shape[0], dtype=jnp.int32)[None, :]).astype(bf16)

    def to_images(rows):
        every = lax.all_gather(rows, "narrow", axis=0, tiled=True)
        return jnp.dot(pick_in, every, preferred_element_type=f32)

    def to_rows(rows):
        every = lax.all_gather(rows, "narrow", axis=0, tiled=True)
        return jnp.dot(pick_out, every, preferred_element_type=f32).astype(bf16)

    steps_all = lax.all_gather(time_index, "wide", axis=0, tiled=True)
    step_hot = (steps_all[:, None] == jnp.arange(time_table.shape[0], dtype=jnp.int32)[None, :]).astype(bf16)
    time_rows = jnp.dot(step_hot, time_table, preferred_element_type=f32).astype(bf16)
    time_slice = lax.dynamic_slice_in_dim(time_rows, wide_at * in_rows, in_rows, axis=1)
    time_weight = attn_weight[:, 3:6]
    time_share = jnp.einsum("id,ljdc->ljic", time_slice, time_weight, preferred_element_type=f32)
    time_share = lax.psum_scatter(time_share, "wide", scatter_dimension=2, tiled=True)
    time_share = lax.all_gather(time_share, "narrow", axis=3, tiled=True)
    time_part = lax.dynamic_index_in_dim(time_share, narrow_at, axis=2, keepdims=False)

    tables = lax.all_gather(rel_table, "narrow", axis=1, tiled=True)
    qkv_bias_all = lax.all_gather(qkv_bias, "narrow", axis=2, tiled=True)
    up_bias_all = lax.all_gather(up_bias, "narrow", axis=1, tiled=True)

    def layer_params(at):
        return (norm_gain[at], norm_shift[at], qkv_bias_all[at], out_bias[at])

    weights = []
    for at in range(layer_count):
        packed = jnp.concatenate([attn_weight[at, 0], attn_weight[at, 1], attn_weight[at, 2], out_weight[at]], axis=1)
        weights.append((gather_unit(packed), gather_unit(mlp_weight[at, 0]), gather_unit(mlp_weight[at, 1])))

    residual = to_images(tokens)
    kept = []
    for at in range(layer_count):
        pairs = pair_bias(tables[at])
        middle, attn_saved = attention_forward(residual, weights[at][0], time_part[at], layer_params(at), pairs)
        residual, mlp_saved = mlp_forward(middle, weights[at][1], weights[at][2], layer_params(at), up_bias_all[at])
        kept.append((attn_saved, mlp_saved))
    block_output = to_rows(residual.astype(bf16))
    gradient = to_images(cotangent)
    attn_grads, out_grads, mlp_grads = [], [], []
    time_sums, small = [], []
    for at in reversed(range(layer_count)):
        attn_saved, mlp_saved = kept[at]
        grad_mid, up_grad, down_grad, mlp_small = mlp_backward(
            gradient, weights[at][1], weights[at][2], layer_params(at), mlp_saved
        )
        mlp_grads.insert(0, jnp.stack([scatter_unit(up_grad), scatter_unit(down_grad)]))
        gradient, proj_grad, sums, table_grad, attn_small = attention_backward(
            grad_mid, weights[at][0], layer_params(at), attn_saved
        )
        packed = scatter_unit(proj_grad)
        attn_grads.insert(0, jnp.stack([packed[:, j * cols : (j + 1) * cols] for j in range(3)]))
        out_grads.insert(0, packed[:, 3 * cols :])
        time_sums.insert(0, sums)
        small.insert(
            0,
            (
                jnp.stack([attn_small[0], mlp_small[0]]),
                jnp.stack([attn_small[1], mlp_small[1]]),
                jnp.stack([attn_small[2], mlp_small[2]]),
                jnp.stack([sums[0], sums[2]]),
                mlp_small[3],
                table_grad,
            ),
        )
    input_grad = to_rows(gradient.astype(bf16))

    def stacked(index_at):
        return jnp.stack([entry[index_at] for entry in small])

    totals = lax.psum(tuple(stacked(index_at) for index_at in range(6)), ("wide", "narrow"))

    def own_part(array, axis):
        size = array.shape[axis] // lax.axis_size("narrow")
        return lax.dynamic_slice_in_dim(array, narrow_at * size, size, axis=axis)

    time_low = jnp.stack(time_sums).astype(bf16)
    time_all = lax.all_gather(time_low, ("wide", "narrow"), axis=0, tiled=False)
    time_own = own_part(time_all, 3)
    time_weight_grad = jnp.einsum("id,iljc->ljdc", time_slice, time_own, preferred_element_type=f32)
    trow_share = jnp.einsum("iljc,ljdc->id", time_own, time_weight, preferred_element_type=f32)
    trow_share = lax.psum(trow_share, "narrow")
    trow = lax.all_gather(trow_share, "wide", axis=1, tiled=True)
    time_grad = jnp.einsum("is,id->sd", step_hot.astype(f32), trow, precision=highest)
    attn_grad = jnp.concatenate([jnp.stack(attn_grads).astype(f32), time_weight_grad], axis=1)
    return (
        block_output,
        input_grad,
        time_grad,
        totals[0],
        totals[1],
        attn_grad,
        jnp.stack(out_grads).astype(f32),
        own_part(totals[3], 2),
        totals[2],
        jnp.stack(mlp_grads).astype(f32),
        own_part(totals[4], 1),
        own_part(totals[5], 1),
    )


def bias_windows(tables):
    layers, heads = tables.shape[:2]
    near = jnp.arange(GRID, dtype=jnp.int32)
    span = jnp.arange(SPAN, dtype=jnp.int32)
    steps = (span[None, :, None] == near[:, None, None] - near[None, None, :] + (GRID - 1)).astype(f32)
    grid = tables.reshape(layers, heads, SPAN, SPAN)[:, :, ::-1]
    windows = jnp.einsum("lhab,xby->lhxay", grid, steps, precision=highest)
    windows = windows.reshape(layers, heads * GRID, SPAN * GRID)
    return jnp.pad(windows, ((0, 0), (0, 0), (0, 512 - SPAN * GRID)))


def fold_windows(windows):
    layers, heads = windows.shape[0], windows.shape[1] // GRID
    near = jnp.arange(GRID, dtype=jnp.int32)
    span = jnp.arange(SPAN, dtype=jnp.int32)
    steps = (span[None, :, None] == near[:, None, None] - near[None, None, :] + (GRID - 1)).astype(f32)
    grid = windows[:, :, : SPAN * GRID].reshape(layers, heads, GRID, SPAN, GRID)
    tables = jnp.einsum("lhxay,xby->lhab", grid, steps, precision=highest)
    return tables[:, :, ::-1].reshape(layers, heads, SPAN * SPAN)


def shards(
    tokens,
    cotangent,
    segment_ids,
    patch_pos,
    time_index,
    time_table,
    norm_gain,
    norm_shift,
    attn_weight,
    out_weight,
    qkv_bias,
    out_bias,
    mlp_weight,
    up_bias,
    rel_table,
):
    image_count = time_index.shape[0]
    layer_count = attn_weight.shape[0]
    in_rows, cols = attn_weight.shape[2:]
    by_links = lax.axis_size("wide") == 8 and lax.axis_size("narrow") == 4 and in_rows % 16 == 0
    if not by_links:
        return shards_plain(
            tokens, cotangent, segment_ids, patch_pos, time_index, time_table, norm_gain, norm_shift,
            attn_weight, out_weight, qkv_bias, out_bias, mlp_weight, up_bias, rel_table,
        )
    narrow_at = lax.axis_index("narrow")
    wide_at = lax.axis_index("wide")
    own_rows, d_model = tokens.shape
    image_local = segment_ids % image_count
    grid_slot = image_local * PATCHES + patch_pos
    own_slots = narrow_at * own_rows + jnp.arange(own_rows, dtype=jnp.int32)
    pick_in = (own_slots[:, None] == grid_slot[None, :]).astype(bf16)
    own_grid = lax.dynamic_slice_in_dim(grid_slot, narrow_at * own_rows, own_rows)
    pick_out = (own_grid[:, None] == jnp.arange(grid_slot.shape[0], dtype=jnp.int32)[None, :]).astype(bf16)

    step_own = (time_index[:, None] == jnp.arange(time_table.shape[0], dtype=jnp.int32)[None, :]).astype(bf16)
    time_own = jnp.dot(step_own, time_table, preferred_element_type=f32).astype(bf16)
    digits = jnp.stack([time_index // 32, time_index % 32]).astype(bf16)
    digits = jnp.pad(digits, ((0, 16 - image_count - 2), (0, d_model - image_count)))
    time_own = jnp.concatenate([time_own, digits], axis=0)
    time_weight = attn_weight[:, 3:6]
    time_packed = jnp.concatenate(
        [time_weight[:, 0], time_weight[:, 1], time_weight[:, 2], jnp.zeros_like(time_weight[:, 0])], axis=2
    )
    qkv_packed = jnp.concatenate(
        [qkv_bias[:, 0], jnp.zeros_like(qkv_bias[:, 0]), qkv_bias[:, 1], jnp.zeros_like(qkv_bias[:, 0])], axis=1
    )
    small_own = jnp.pad(jnp.concatenate([up_bias, qkv_packed], axis=0), ((0, 8 - 2 * layer_count), (0, 0)))
    packed_own = [
        jnp.concatenate([attn_weight[at, 0], attn_weight[at, 1], attn_weight[at, 2], out_weight[at]], axis=1)
        for at in range(layer_count)
    ]
    wholes, saved, (block_low, gradient, time_all, time_sel) = forward_all(
        tokens,
        cotangent,
        pick_in,
        time_own,
        time_packed,
        bias_windows(rel_table),
        small_own,
        norm_gain.reshape(-1, d_model),
        norm_shift.reshape(-1, d_model),
        out_bias.reshape(-1, d_model),
        packed_own,
        mlp_weight,
    )
    time_all = time_all.reshape(8, 16, d_model)
    steps_all = time_all[:, image_count : image_count + 2, :image_count].astype(f32)
    steps_all = (steps_all[:, 0] * 32 + steps_all[:, 1]).astype(jnp.int32).reshape(-1)
    step_hot = (steps_all[:, None] == jnp.arange(time_table.shape[0], dtype=jnp.int32)[None, :]).astype(f32)
    time_slice = time_sel.reshape(8, 16, in_rows)[:, :image_count].reshape(-1, in_rows)

    attn_grads, out_grads, mlp_grads = [], [], []
    row_sums, table_sums, time_sums = [], [], []
    block_output = None
    trow = jnp.zeros((2, 2, 2, 8, 8, in_rows), f32)
    for at in reversed(range(layer_count)):
        last_layer = at == layer_count - 1
        packed, up_part, down_part, gradient, moved, rows_part, tables_part, times_part, trow, _ = backward_layer(
            last_layer, gradient, saved[at], norm_gain[at], norm_shift[at], trow, pick_out, time_packed[at], block_low,
            wholes[3 * at : 3 * at + 3],
        )
        if last_layer:
            block_output = moved
        mlp_grads.insert(0, jnp.stack([up_part, down_part]))
        attn_grads.insert(0, jnp.stack([packed[:, j * cols : (j + 1) * cols] for j in range(3)]))
        out_grads.insert(0, packed[:, 3 * cols :])
        row_sums.insert(0, rows_part)
        table_sums.insert(0, tables_part)
        time_sums.insert(0, times_part.reshape(8, 16, d_model)[:, :image_count].reshape(-1, d_model))
    input_grad = moved
    row_sums = jnp.stack(row_sums)
    table_grad = fold_windows(jnp.stack(table_sums))
    time_weight_grad = jnp.einsum("id,lic->ldc", time_slice, jnp.stack(time_sums), preferred_element_type=f32)
    time_weight_grad = jnp.stack([time_weight_grad[:, :, j * cols : (j + 1) * cols] for j in range(3)], axis=1)
    trow = trow.reshape(8, 8, 8, in_rows)[:, :, :image_count].transpose(1, 2, 0, 3).reshape(-1, d_model)
    time_grad = jnp.einsum("is,id->sd", step_hot, trow, precision=highest)
    attn_grad = jnp.concatenate([jnp.stack(attn_grads), time_weight_grad], axis=1)
    qkv_bias_grad = jnp.stack([row_sums[:, 7, :cols], row_sums[:, 7, 2 * cols : 3 * cols]], axis=1)
    return (
        block_output,
        input_grad,
        time_grad,
        row_sums[:, 0:2],
        row_sums[:, 2:4],
        attn_grad,
        jnp.stack(out_grads),
        qkv_bias_grad,
        row_sums[:, 4:6],
        jnp.stack(mlp_grads),
        row_sums[:, 6],
        table_grad,
    )


def solution(mesh):
    return jax.shard_map(
        shards,
        mesh=mesh,
        in_specs=(
            P(("wide", "narrow"), None),
            P(("wide", "narrow"), None),
            P("wide"),
            P("wide"),
            P("wide"),
            P(),
            P(),
            P(),
            P(None, None, "wide", "narrow"),
            P(None, "wide", "narrow"),
            P(None, None, "narrow"),
            P(),
            P(None, None, "wide", "narrow"),
            P(None, "narrow"),
            P(None, "narrow", None),
        ),
        out_specs=(
            P(("wide", "narrow"), None),
            P(("wide", "narrow"), None),
            P(),
            P(),
            P(),
            P(None, None, "wide", "narrow"),
            P(None, "wide", "narrow"),
            P(None, None, "narrow"),
            P(),
            P(None, None, "wide", "narrow"),
            P(None, "narrow"),
            P(None, "narrow", None),
        ),
        check_vma=False,
    )
```
